512 devices in a mesh: wa: 64 (over x, z), slab: 8 (over y, core).
Axes of the slice: x: 4, y: 4, z: 16, core: 2. Of those that a mesh axis runs over, the one named last changes fastest.
Arguments:
- visibilities: float32 [32768, 2, 128], P(('wa', 'slab')), may hold values from -6 to 6
- row_offset: float32 [32768, 128], P(('wa', 'slab')), may hold values from 0 to 16
- col_offset: float32 [32768, 128], P(('wa', 'slab')), may hold values from 0 to 128
- w_layer: int32 [32768], P(('wa', 'slab')), may hold values from 0 to 63, as said below
- grid_block: int32 [32768], P(('wa', 'slab')), may hold values from 0 to 63
Outputs:
- dirty_image: float32 [512, 1024], P('wa', 'slab')
The draws below stay inside these ranges and needn't reach their ends.
Inputs may be any that keep to these rules, and one draw needn't show every extreme that they name: `w_layer`: in each device's aligned block of 64 tiles no w-layer is named more than 2 times, and in every draw one w-layer is named exactly 2 times in every block.
All inputs are finite; a program needn't handle non-finite values.
Results may differ from the reference program's by a relative error of at most 0.0003.
Values sent between devices are 32-bit elements; how exact they have to be, the bound alone decides.
No kernel may reach another device: no remote copies, remote signals or barrier semaphores. Data moves between devices by JAX's collectives and lax.ppermute only.
A program may use at most 64 MiB of HBM per device.

```python
import math
import jax
import jax.numpy as jnp
from jax import lax

NG = 4096
VIS = 128
RB = 16
CB = 128
TILES_DEV = 64
CAP = 2
ROWS_DEV = 32
IMG_L = 512
IMG_M = 1024
W_PLANES = 64
TILES = 32768
BLOCKS = 64
N_SLAB = 8


def draw_w_layer(key, part):
    key = jax.random.fold_in(key, 7)
    key_busiest, key_extra_credit, key_jitter, key_permutation = jax.random.split(key, 4)
    device_total = TILES // TILES_DEV
    slot_total = W_PLANES * CAP
    position_layer = jnp.arange(slot_total, dtype=jnp.int32) // CAP
    busiest_layer = jax.random.randint(key_busiest, (), 0, W_PLANES)
    layer_extra_credit = jax.random.randint(key_extra_credit, (W_PLANES,), 0, 4096)
    position_jitter = jax.random.randint(key_jitter, (device_total, slot_total), 0, 4096)
    position_rating = position_jitter + layer_extra_credit[position_layer][None, :] + jnp.where(position_layer == busiest_layer, 1 << 20, 0)[None, :]
    position_rating = position_rating * slot_total + jnp.arange(slot_total, dtype=jnp.int32)[None, :]
    top_values, top_index = lax.top_k(position_rating, TILES_DEV)
    chosen = position_layer[top_index]
    shuffle = jax.random.randint(key_permutation, (device_total, TILES_DEV), 0, 65536) * TILES_DEV + jnp.arange(TILES_DEV, dtype=jnp.int32)[None, :]
    shuffle_order = jnp.argsort(shuffle, axis=1)
    return jnp.take_along_axis(chosen, shuffle_order, axis=1).reshape(-1).astype(jnp.int32)


def place_ends(result, stream_key, smallest, largest):
    longest = result.shape.index(max(result.shape))
    spots = []
    for shift in (0, 1):
        where = [jax.random.randint(jax.random.fold_in(stream_key, axis), (), 0, length) for axis, length in enumerate(result.shape)]
        where[longest] = (where[longest] + shift) % result.shape[longest]
        spots.append(tuple(where))
    return result.at[spots[0]].set(smallest).at[spots[1]].set(largest)


def block_scale(key, shape, cuts, low, high):
    loudness, own = 1.0, jax.random.fold_in(key, 6)
    for dim, parts in cuts:
        draws = jnp.exp(jax.random.uniform(jax.random.fold_in(own, dim), (parts,), jnp.float32, low / len(cuts), high / len(cuts)))
        loudness = loudness * jnp.repeat(draws, shape[dim] // parts).reshape([-1 if axis == dim else 1 for axis in range(len(shape))])
    return loudness


def noise(stream_key, shape, deviation, most, pieces=(), kind=jnp.bfloat16):
    result = deviation * jax.random.normal(stream_key, shape, jnp.float32)
    if pieces:
        result = result * block_scale(stream_key, shape, pieces, -0.22, 0.18)
    return jnp.clip(result, -most, most).astype(kind)


def setup_inputs(seed: int = 0) -> dict:
    key_list = jax.random.split(jax.random.key(seed), 6)
    return {
        "visibilities": noise(key_list[0], (TILES, 2, VIS), 1.0, 6.0, ((0, 512),), jnp.float32),
        "row_offset": jnp.clip(16.0 * jax.random.uniform(key_list[1], (TILES, VIS), jnp.float32) ** block_scale(key_list[1], (TILES, VIS), ((0, 512),), -0.2, 0.2), 0.0, 16.0),
        "col_offset": jnp.clip(128.0 * jax.random.uniform(key_list[2], (TILES, VIS), jnp.float32) ** block_scale(key_list[2], (TILES, VIS), ((0, 512),), -0.2, 0.2), 0.0, 128.0),
        "w_layer": draw_w_layer(jax.random.fold_in(key_list[5], 71), 0),
        "grid_block": place_ends(jax.random.randint(key_list[4], (TILES,), 0, BLOCKS), jax.random.fold_in(key_list[4], 1), 0, BLOCKS - 1).astype(jnp.int32),
    }


kernel_width = 1.0
cell_size = 2.4e-05
w_reach = 20000.0
group_size = 16

def kernel_rows(offsets, extent):
    centers = jnp.arange(extent, dtype=jnp.float32) + 0.5
    return jnp.exp(-0.5 * ((centers - offsets[..., None]) / kernel_width) ** 2)

def grid_patches(visibilities, row_offset, col_offset):
    row_kernel = kernel_rows(row_offset, RB)
    col_kernel = kernel_rows(col_offset, CB)
    weighted = visibilities[..., :, :, None] * row_kernel[..., None, :, :]
    return jnp.einsum('...xkr,...kc->...xrc', weighted, col_kernel, precision=lax.Precision.HIGHEST)

def screen_phase(w_value, l_index, m_index):
    l_direction = l_index.astype(jnp.float32)[:, None] * cell_size
    m_direction = m_index.astype(jnp.float32)[None, :] * cell_size
    radius = l_direction * l_direction + m_direction * m_direction
    n_lift = -radius / (1.0 + jnp.sqrt(1.0 - radius))
    phase_angle = -2.0 * math.pi * w_value * n_lift
    return (jnp.cos(phase_angle), jnp.sin(phase_angle))

def reference(visibilities, row_offset, col_offset, w_layer, grid_block):
    window_rows = ROWS_DEV * N_SLAB
    block_cols = NG // CB
    tile_ids = jnp.arange(TILES, dtype=jnp.int32)
    slab_of = tile_ids // TILES_DEV % N_SLAB
    first_row = (slab_of * ROWS_DEV + grid_block // block_cols * RB).astype(jnp.int32)
    first_col = (grid_block % block_cols * CB).astype(jnp.int32)
    layer_hits = (w_layer[:, None] == jnp.arange(W_PLANES, dtype=jnp.int32)[None, :]).astype(jnp.int32)
    counts = lax.optimization_barrier(jnp.sum(layer_hits, axis=0)).astype(jnp.int32)
    starts = (jnp.cumsum(counts) - counts).astype(jnp.int32)
    tile_order = jnp.argsort(w_layer, stable=True).astype(jnp.int32)
    l_index = jnp.arange(IMG_L, dtype=jnp.int32) - IMG_L // 2
    m_index = jnp.arange(IMG_M, dtype=jnp.int32) - IMG_M // 2
    m_pick = jnp.mod(m_index, NG)
    l_pick = jnp.mod(l_index, NG)
    m_sign = jnp.where(jnp.mod(m_index, 2) == 0, 1.0, -1.0).astype(jnp.float32)
    l_angle = 2.0 * math.pi * jnp.mod(window_rows // 2 * l_index, NG).astype(jnp.float32) / NG
    l_shift = jnp.exp(-1j * l_angle)
    spread = 1.0 / (2.0 * math.pi * kernel_width ** 2 * math.sqrt(TILES * VIS))

    def layer_step(layer_index, image_sum):
        first_tile = starts[layer_index]
        tile_count = counts[layer_index]

        def add_group(group_index, layer_grid):
            position = first_tile + group_index * group_size + jnp.arange(group_size, dtype=jnp.int32)
            live_mask = (position < first_tile + tile_count).astype(jnp.float32)
            chosen = tile_order[jnp.minimum(position, TILES - 1)]
            patches = grid_patches(visibilities[chosen] * live_mask[:, None, None], row_offset[chosen], col_offset[chosen])
            rows_at = first_row[chosen][:, None, None] + jnp.arange(RB, dtype=jnp.int32)[None, :, None]
            cols_at = first_col[chosen][:, None, None] + jnp.arange(CB, dtype=jnp.int32)[None, None, :]
            return layer_grid.at[:, rows_at, cols_at].add(jnp.moveaxis(patches, 1, 0))
        group_count = (tile_count + group_size - 1) // group_size
        layer_grid = lax.fori_loop(0, group_count, add_group, jnp.zeros((2, window_rows, NG), jnp.float32))
        grid_wave = layer_grid[0] + 1j * layer_grid[1]
        along_v = jnp.fft.ifft(grid_wave, axis=1) * NG
        picked = along_v[:, m_pick] * m_sign[None, :]
        padded = jnp.zeros((NG, IMG_M), picked.dtype).at[:window_rows].set(picked)
        along_u = jnp.fft.ifft(padded, axis=0) * NG
        layer_image = along_u[l_pick] * l_shift[:, None]
        w_value = w_reach * (2.0 * layer_index.astype(jnp.float32) + 1.0 - W_PLANES) / W_PLANES
        cos_screen, sin_screen = screen_phase(w_value, l_index, m_index)
        return image_sum + (jnp.real(layer_image) * cos_screen - jnp.imag(layer_image) * sin_screen)
    image_sum = lax.fori_loop(0, W_PLANES, layer_step, jnp.zeros((IMG_L, IMG_M), jnp.float32))
    return image_sum * spread
```

```python
import math

import numpy as np

import jax
import jax.numpy as jnp
from jax import lax
from jax.sharding import PartitionSpec as P

NG = 4096
VIS = 128
RB = 16
CB = 128
ROWS_DEV = 32
IMG_L = 512
IMG_M = 1024
CAP = 2
X_CHIPS = 4
SUB = 32


kernel_width = 1.0
cell_size = 2.4e-05
w_reach = 20000.0


def kernel_rows(offsets, extent):
    centers = jnp.arange(extent, dtype=jnp.float32) + 0.5
    return jnp.exp(-0.5 * ((centers - offsets[..., None]) / kernel_width) ** 2)


def screen_phase(w_value, l_index, m_index):
    l_direction = l_index.astype(jnp.float32)[:, None] * cell_size
    m_direction = m_index.astype(jnp.float32)[None, :] * cell_size
    radius = l_direction * l_direction + m_direction * m_direction
    n_lift = -radius / (1.0 + jnp.sqrt(1.0 - radius))
    phase_angle = -2.0 * math.pi * w_value * n_lift
    return (jnp.cos(phase_angle), jnp.sin(phase_angle))


def wave(turns, period):
    angle = 2.0 * np.pi * (np.asarray(turns) % period) / period
    return np.cos(angle), np.sin(angle)


def real_form(cos_part, sin_part):
    return np.stack([np.stack([cos_part, sin_part]), np.stack([-sin_part, cos_part])]).astype(
        np.float32
    )


def body(visibilities, row_offset, col_offset, w_layer, grid_block):
    highest = lax.Precision.HIGHEST
    high = lax.Precision.HIGH
    wa_count = lax.axis_size("wa")
    slab_count = lax.axis_size("slab")
    tile_count = w_layer.shape[0]
    slot_count = wa_count * CAP
    layer_hits = (w_layer[:, None] == w_layer[None, :]) & (
        jnp.arange(tile_count)[:, None] > jnp.arange(tile_count)[None, :]
    )
    target = w_layer * CAP + jnp.sum(layer_hits.astype(jnp.int32), axis=1)
    placing = (jnp.arange(slot_count, dtype=jnp.int32)[:, None] == target[None, :]).astype(
        jnp.float32
    )
    z_count = wa_count // X_CHIPS
    own_x = lax.axis_index("wa") // z_count
    z_groups = [[x * z_count + z for z in range(z_count)] for x in range(X_CHIPS)]

    def to_x(step):
        return [
            (x * z_count + z, (x + step) % X_CHIPS * z_count + z)
            for x in range(X_CHIPS)
            for z in range(z_count)
        ]

    tile_row = jnp.concatenate(
        [
            visibilities.reshape(tile_count, 2 * VIS),
            row_offset,
            col_offset,
            jnp.broadcast_to(grid_block.astype(jnp.float32)[:, None], (tile_count, 64)),
        ],
        1,
    )
    width = tile_row.shape[1]
    sent = jnp.dot(placing, tile_row, precision=highest).reshape(X_CHIPS, z_count, CAP * width)
    sent = jnp.swapaxes(sent, 0, 1).reshape(z_count, 1, X_CHIPS * CAP * width)
    got = lax.all_to_all(
        sent, "wa", split_axis=0, concat_axis=0, tiled=True, axis_index_groups=z_groups
    )
    got = got.reshape(z_count, X_CHIPS, CAP * width).swapaxes(0, 1)
    chunks = [
        lax.dynamic_index_in_dim(got, (own_x + step) % X_CHIPS, 0, False) for step in range(X_CHIPS)
    ]
    got = jnp.stack(
        chunks[:1] + [lax.ppermute(chunks[step], "wa", to_x(step)) for step in range(1, X_CHIPS)]
    )
    got = got.reshape(slot_count, width)
    vis_piece = got[:, : 2 * VIS].reshape(slot_count, 2, VIS)
    row_piece = got[:, 2 * VIS : 3 * VIS]
    col_piece = got[:, 3 * VIS : 4 * VIS]
    block_piece = got[:, 4 * VIS].astype(jnp.int32)

    weighted = vis_piece[:, :, None, :] * jnp.swapaxes(kernel_rows(row_piece, RB), 1, 2)[:, None]
    patches = jnp.einsum("txrk,tkc->txrc", weighted, kernel_rows(col_piece, CB), precision=high)

    q = np.arange(SUB)
    turn = jnp.asarray(
        (real_form(*wave(q[:, None] * q[None, :], SUB)) * (1 - 2 * (q % 2))).astype(np.float32)
    )
    half = ROWS_DEV // RB
    block_hot = (block_piece[:, None] == jnp.arange(half * SUB)[None, :]).astype(jnp.float32)
    turns = jnp.einsum(
        "thb,xybq->txhyq", block_hot.reshape(slot_count, half, SUB), turn, precision=highest
    )
    along_b = jnp.einsum("txhyq,txrc->hryqc", turns, patches, precision=high)
    c = np.arange(CB)
    cos_twist, sin_twist = (
        jnp.asarray(part.astype(np.float32)) for part in wave(q[:, None] * c[None, :], NG)
    )
    real_b, imag_b = along_b[:, :, 0], along_b[:, :, 1]
    twisted = jnp.stack(
        [real_b * cos_twist - imag_b * sin_twist, real_b * sin_twist + imag_b * cos_twist], 2
    )
    last = jnp.asarray(real_form(*wave(c[:, None] * (q[None, :] - SUB // 2), CB)))
    spectrum = jnp.einsum("hryqc,yzcn->hrznq", twisted, last, precision=high)
    columns = IMG_M // slab_count
    pieces = spectrum.reshape(ROWS_DEV, 2, slab_count, columns).transpose(2, 0, 1, 3)
    pieces = pieces.reshape(slab_count, 2 * ROWS_DEV, columns)
    turned = lax.all_to_all(pieces, "slab", split_axis=0, concat_axis=0, tiled=True)

    window_rows = ROWS_DEV * slab_count
    rows = np.arange(window_rows) - window_rows // 2
    lines = np.arange(IMG_L) - IMG_L // 2
    spread = 1.0 / (
        2.0 * math.pi * kernel_width**2 * math.sqrt(tile_count * wa_count * slab_count * VIS)
    )
    u_table = jnp.asarray(
        real_form(*wave(lines[:, None] * rows[None, :], NG)).transpose(1, 2, 3, 0).reshape(
            2 * IMG_L, 2 * window_rows
        )
        * np.float32(spread)
    )
    image = jnp.dot(u_table, turned.reshape(2 * window_rows, columns), precision=high)
    l_index = jnp.arange(IMG_L, dtype=jnp.int32) - IMG_L // 2
    m_index = lax.axis_index("slab") * columns + jnp.arange(columns, dtype=jnp.int32) - IMG_M // 2
    layer_number = lax.axis_index("wa").astype(jnp.float32)
    w_value = w_reach * (2.0 * layer_number + 1.0 - wa_count) / wa_count
    cos_screen, sin_screen = screen_phase(w_value, l_index, m_index)
    layer_image = image[:IMG_L] * cos_screen - image[IMG_L:] * sin_screen
    layer_image = layer_image.reshape(X_CHIPS, IMG_L // X_CHIPS, columns)
    parts = [
        lax.dynamic_index_in_dim(layer_image, (own_x + step) % X_CHIPS, 0, False)
        for step in range(X_CHIPS)
    ]
    part_sum = parts[0]
    for step in range(1, X_CHIPS):
        part_sum = part_sum + lax.ppermute(parts[step], "wa", to_x(step))
    shares = lax.all_to_all(
        part_sum.reshape(z_count, IMG_L // wa_count, columns),
        "wa",
        split_axis=0,
        concat_axis=0,
        tiled=True,
        axis_index_groups=z_groups,
    )
    return jnp.sum(shares, 0)


def solution(mesh):
    placed = (
        P(("wa", "slab"), None, None),
        P(("wa", "slab"), None),
        P(("wa", "slab"), None),
        P(("wa", "slab")),
        P(("wa", "slab")),
    )
    return jax.shard_map(
        body, mesh=mesh, in_specs=placed, out_specs=P("wa", "slab"), check_vma=False
    )
```

```python
import math

import ml_dtypes
import numpy as np

import jax
import jax.numpy as jnp
from jax import lax
from jax.experimental import pallas as pl
from jax.experimental.pallas import tpu as pltpu
from jax.sharding import Mesh
from jax.sharding import PartitionSpec as P

NG = 4096
VIS = 128
RB = 16
CB = 128
ROWS_DEV = 32
IMG_L = 512
IMG_M = 1024
CAP = 2
LAYERS = 64
N_SLAB = 8
X_CHIPS = 4
Z_CHIPS = 16
SUB = 32
SLOTS = LAYERS * CAP
LANES = 128
SENT = 4 * CAP + 1
PEERS = X_CHIPS * N_SLAB
PAIRS = RB // 2


kernel_width = 1.0
cell_size = 2.4e-05
w_reach = 20000.0

f32 = jnp.float32
bf16 = jnp.bfloat16
VMEM = pl.BlockSpec(memory_space=pltpu.VMEM)
SMEM = pl.BlockSpec(memory_space=pltpu.SMEM)
NT = (((1,), (1,)), ((), ()))
NN = (((1,), (0,)), ((), ()))


def wave(turns, period):
    angle = 2.0 * np.pi * (np.asarray(turns) % period) / period
    return np.cos(angle), np.sin(angle)


def np_split(table):
    table = np.asarray(table, np.float32)
    upper = table.astype(ml_dtypes.bfloat16)
    return upper, (table - upper.astype(np.float32)).astype(ml_dtypes.bfloat16)


def split(value):
    upper = value.astype(bf16)
    return upper, (value - upper.astype(f32)).astype(bf16)


def dot(left, right, dims):
    return lax.dot_general(left, right, dims, preferred_element_type=f32)


def route_kernel(layer_ref, block_ref, vis_ref, row_ref, col_ref, out_ref, count_ref, blocks_ref):
    out_ref[...] = jnp.zeros_like(out_ref)

    def clear(layer, carry):
        count_ref[layer] = 0
        blocks_ref[layer * CAP] = 0
        blocks_ref[layer * CAP + 1] = 0
        return carry

    lax.fori_loop(0, LAYERS, clear, 0, unroll=8)

    def place(tile, carry):
        layer = layer_ref[tile]
        slot = count_ref[layer]
        count_ref[layer] = slot + 1
        blocks_ref[layer * CAP + slot] = block_ref[tile]
        start = layer * SENT + slot * 4
        out_ref[pl.ds(start, 2), :] = vis_ref[pl.ds(2 * tile, 2), :]
        out_ref[pl.ds(start + 2, 1), :] = row_ref[pl.ds(tile, 1), :]
        out_ref[pl.ds(start + 3, 1), :] = col_ref[pl.ds(tile, 1), :]
        return carry

    tiles = layer_ref.shape[0]
    lax.fori_loop(0, tiles, place, 0, unroll=8)
    lower = lax.broadcasted_iota(jnp.int32, (1, LANES), 1) < LANES // CAP

    def name(layer, carry):
        both = jnp.where(lower, blocks_ref[layer * CAP], blocks_ref[layer * CAP + 1])
        out_ref[pl.ds(layer * SENT + 4 * CAP, 1), :] = both.astype(f32)
        return carry

    lax.fori_loop(0, LAYERS, name, 0, unroll=8)


def grid_kernel(got_ref, twist_ref, last_ref, out_ref, patch_ref):
    rows = lax.broadcasted_iota(jnp.int32, (RB, VIS), 0).astype(f32) + 0.5
    cols = lax.broadcasted_iota(jnp.int32, (CB, VIS), 0).astype(f32) + 0.5
    empty = jnp.zeros((2 * RB, VIS), bf16)

    def one(source, slot):
        start = source * SENT + 4 * slot
        real = got_ref[pl.ds(start, 1), :]
        imag = got_ref[pl.ds(start + 1, 1), :]
        away = rows - got_ref[pl.ds(start + 2, 1), :]
        near = jnp.exp(-0.5 * (away * away))
        upper, lower = split(jnp.concatenate([near * real, near * imag], 0))
        away = cols - got_ref[pl.ds(start + 3, 1), :]
        col_upper, col_lower = split(jnp.exp(-0.5 * (away * away)))
        left = jnp.concatenate(
            [jnp.concatenate([upper, upper], 1), jnp.concatenate([lower, empty], 1)], 0
        )
        both = dot(left, jnp.concatenate([col_upper, col_lower], 1), NT)
        patch = both[: 2 * RB] + both[2 * RB :]
        row = slot * LAYERS + source
        patch_ref[pl.ds(row, RB, stride=2 * SLOTS), :] = patch[:RB]
        patch_ref[pl.ds(row + SLOTS, RB, stride=2 * SLOTS), :] = patch[RB:]

    together = 4

    def some(step, carry):
        for part in range(together):
            for slot in range(CAP):
                one(step * together + part, slot)
        return carry

    lax.fori_loop(0, LAYERS // together, some, 0)

    named = got_ref[pl.ds(4 * CAP, LAYERS, stride=SENT), :]
    source = lax.broadcasted_iota(jnp.int32, (LAYERS, SLOTS), 0)
    lane = lax.broadcasted_iota(jnp.int32, (LAYERS, SLOTS), 1)
    block = jnp.sum(
        jnp.where(source == jnp.bitwise_and(lane, LAYERS - 1), named, 0.0), 0, keepdims=True
    )
    second = block >= float(SUB)
    turn = jnp.where(second, block - float(SUB), block) * lax.broadcasted_iota(
        jnp.int32, (SUB, SLOTS), 0
    ).astype(f32)
    angle = (turn - SUB * jnp.floor(turn * (1.0 / SUB))) * (2.0 * math.pi / SUB)
    cos_all, sin_all = jnp.cos(angle), jnp.sin(angle)
    second = jnp.broadcast_to(second, (SUB, SLOTS))
    cos_part = jnp.concatenate(
        [jnp.where(second, 0.0, cos_all), jnp.where(second, cos_all, 0.0)], 0
    )
    sin_part = jnp.concatenate(
        [jnp.where(second, 0.0, sin_all), jnp.where(second, sin_all, 0.0)], 0
    )
    turns = jnp.concatenate(
        [
            jnp.concatenate([cos_part, -sin_part], 1),
            jnp.concatenate([sin_part, cos_part], 1),
        ],
        0,
    )
    turn_upper, turn_lower = split(turns)
    turn_both = jnp.concatenate([turn_upper, turn_lower], 0)
    twist_cos = twist_ref[: 2 * SUB, :]
    twist_sin = twist_ref[2 * SUB :, :]
    last_both = last_ref[...]
    last_upper = last_both[: 2 * SUB]

    for pair in range(PAIRS):
        patch = jnp.concatenate(
            [
                patch_ref[pl.ds((2 * pair + r) * 2 * SLOTS, 2 * SLOTS), :]
                for r in range(2)
            ],
            1,
        )
        patch_upper, patch_lower = split(patch)
        both = dot(turn_both, patch_upper, NN)
        along = both[: 4 * SUB] + both[4 * SUB :] + dot(turn_upper, patch_lower, NN)
        parts = []
        for r in range(2):
            real = along[: 2 * SUB, r * CB : (r + 1) * CB]
            imag = along[2 * SUB :, r * CB : (r + 1) * CB]
            parts.append(
                jnp.concatenate(
                    [real * twist_cos - imag * twist_sin, real * twist_sin + imag * twist_cos], 1
                )
            )
        upper, lower = split(jnp.concatenate(parts, 0))
        both = dot(last_both, upper, NT)
        wide = both[: 2 * SUB] + both[2 * SUB :] + dot(last_upper, lower, NT)
        for part in range(2):
            out_ref[pl.ds(2 * pair + part, PEERS, stride=2 * PAIRS), :] = wide[
                part * PEERS : (part + 1) * PEERS
            ]


def image_kernel(got_ref, upper_ref, lower_ref, cos_ref, sin_ref, out_ref, right_ref):
    group = lax.broadcasted_iota(jnp.int32, (N_SLAB, LANES), 1) // SUB
    for step in range(2 * PAIRS):
        turned = []
        for layer in range(X_CHIPS):
            value = got_ref[pl.ds(layer * N_SLAB * 2 * PAIRS + step, N_SLAB, stride=2 * PAIRS), :]
            turned.append(
                [value] + [pltpu.roll(value, SUB * shift, 1) for shift in range(1, X_CHIPS)]
            )
        parts = []
        for part in range(X_CHIPS):
            value = turned[0][(0 - part) % X_CHIPS]
            for layer in range(1, X_CHIPS):
                value = jnp.where(group == layer, turned[layer][(layer - part) % X_CHIPS], value)
            parts.append(value)
        upper, lower = split(jnp.concatenate(parts, 0))
        rows = X_CHIPS * N_SLAB
        right_ref[step * rows : (step + 1) * rows, :] = jnp.concatenate([upper, lower], 1)
    count = IMG_L // X_CHIPS
    group = lax.broadcasted_iota(jnp.int32, (count, LANES), 1) // SUB
    right = right_ref[...]
    total = None
    for part in range(X_CHIPS):
        rows = pl.ds(part * 2 * count, 2 * count)
        both = dot(upper_ref[rows, :], right, NN)
        wave_sum = both[:, :LANES] + both[:, LANES:] + dot(lower_ref[rows, :], right[:, :LANES], NN)
        lines = pl.ds(part * count, count)
        screened = wave_sum[:count] * cos_ref[lines, :] - wave_sum[count:] * sin_ref[lines, :]
        screened = screened + pltpu.roll(screened, 2 * SUB, 1)
        screened = screened + pltpu.roll(screened, SUB, 1)
        total = screened if total is None else jnp.where(group == part, screened, total)
    out_ref[...] = total


def sum_kernel(got_ref, out_ref):
    line = lax.broadcasted_iota(jnp.int32, (8, LANES), 0)
    group = lax.broadcasted_iota(jnp.int32, (8, LANES), 1) // SUB
    straight = (line // 4) == jnp.bitwise_and(line, 1)
    result = jnp.zeros((8, LANES), f32)
    for chip in range(X_CHIPS):
        total = got_ref[pl.ds(chip * 2 * Z_CHIPS, 8), :]
        for step in range(1, 2 * Z_CHIPS // 8):
            total = total + got_ref[pl.ds(chip * 2 * Z_CHIPS + 8 * step, 8), :]
        total = total + pltpu.roll(total, 4, 0)
        total = total + pltpu.roll(total, 2, 0)
        total = jnp.where(straight, total, pltpu.roll(total, 1, 0))
        for part in range(X_CHIPS):
            shift = (chip - part) % X_CHIPS
            moved = pltpu.roll(total, SUB * shift, 1) if shift else total
            chosen = (group == chip) & (jnp.bitwise_and(line, 3) == part)
            result = jnp.where(chosen, moved, result)
    out_ref[...] = result


def call(kernel, shape, specs, scratch, flops, moved):
    return pl.pallas_call(
        kernel,
        out_shape=jax.ShapeDtypeStruct(shape, f32),
        in_specs=specs,
        out_specs=VMEM,
        scratch_shapes=scratch,
        compiler_params=pltpu.CompilerParams(vmem_limit_bytes=24 * 1024 * 1024),
        cost_estimate=pl.CostEstimate(flops=flops, bytes_accessed=moved, transcendentals=0),
    )


def grid_tables():
    q = np.arange(SUB)
    c = np.arange(CB)
    sign = (1 - 2 * (q % 2))[:, None]
    twist = np.concatenate(
        [np.tile(part * sign, (2, 1)) for part in wave(q[:, None] * c[None, :], NG)], 0
    ).astype(np.float32)
    n = (4 * np.arange(N_SLAB)[None, :] + np.arange(X_CHIPS)[:, None]).reshape(-1)
    cos_part, sin_part = wave((n[:, None] - SUB // 2) * c[None, :], CB)
    last = np.concatenate(
        [
            np.concatenate([cos_part, -sin_part], 1),
            np.concatenate([sin_part, cos_part], 1),
        ],
        0,
    )
    return twist, np.concatenate(np_split(last), 0)


def image_lines():
    part, chip, half = np.meshgrid(np.arange(4), np.arange(LAYERS), np.arange(2), indexing="ij")
    return (8 * chip + 4 * half + part).reshape(-1) - IMG_L // 2


def image_tables(spread):
    pair, y, r, h, slab = np.meshgrid(
        np.arange(PAIRS), np.arange(2), np.arange(2), np.arange(2), np.arange(N_SLAB), indexing="ij"
    )
    row = (slab * ROWS_DEV + h * RB + 2 * pair + r).reshape(-1) - ROWS_DEV * N_SLAB // 2
    y = y.reshape(-1)[None, :]
    cos_part, sin_part = wave(image_lines()[:, None] * row[None, :], NG)
    real = np.where(y == 0, cos_part, -sin_part).reshape(4, -1, row.size)
    imag = np.where(y == 0, sin_part, cos_part).reshape(4, -1, row.size)
    return np_split(np.concatenate([real, imag], 1).reshape(2 * IMG_L, row.size) * spread)


def screen_tables():
    columns = IMG_M // N_SLAB
    lines = jnp.asarray(image_lines().astype(np.float32))
    lane = jnp.arange(LANES, dtype=jnp.int32)
    m_index = (
        lax.axis_index("slab") * columns
        + lax.axis_index("x") * SUB
        + jnp.bitwise_and(lane, SUB - 1)
        - IMG_M // 2
    )
    layer = ((lane // SUB) * Z_CHIPS + lax.axis_index("z")).astype(f32)
    w_value = w_reach * (2.0 * layer + 1.0 - LAYERS) / LAYERS
    l_direction = lines[:, None] * cell_size
    m_direction = m_index.astype(f32)[None, :] * cell_size
    radius = l_direction * l_direction + m_direction * m_direction
    n_lift = -radius / (1.0 + jnp.sqrt(1.0 - radius))
    phase_angle = -2.0 * math.pi * w_value[None, :] * n_lift
    return jnp.cos(phase_angle), jnp.sin(phase_angle)


def body(visibilities, row_offset, col_offset, w_layer, grid_block):
    tiles = w_layer.shape[0]
    spread = 1.0 / (
        2.0 * math.pi * kernel_width**2 * math.sqrt(tiles * LAYERS * N_SLAB * VIS)
    )
    sent = call(
        route_kernel,
        (LAYERS * SENT, VIS),
        [SMEM, SMEM, VMEM, VMEM, VMEM],
        [pltpu.SMEM((LAYERS,), jnp.int32), pltpu.SMEM((SLOTS,), jnp.int32)],
        10**6,
        5 * 10**5,
    )(w_layer, grid_block, visibilities.reshape(2 * tiles, VIS), row_offset, col_offset)
    got = lax.all_to_all(
        sent.reshape(LAYERS, 1, SENT * VIS), ("x", "z"), split_axis=0, concat_axis=0, tiled=True
    ).reshape(LAYERS * SENT, VIS)
    cos_screen, sin_screen = screen_tables()
    twist, last = grid_tables()
    pieces = call(
        grid_kernel,
        (PEERS * 2 * PAIRS, LANES),
        [VMEM] * 3,
        [pltpu.VMEM((RB * 2 * SLOTS, CB), f32)],
        10**9,
        10**6,
    )(got, jnp.asarray(twist), jnp.asarray(last))
    turned = lax.all_to_all(
        pieces.reshape(PEERS, 2 * PAIRS, LANES),
        ("x", "slab"),
        split_axis=0,
        concat_axis=0,
        tiled=True,
    ).reshape(PEERS * 2 * PAIRS, LANES)
    upper, lower = image_tables(spread)
    shares = call(
        image_kernel,
        (2 * LAYERS, LANES),
        [VMEM] * 5,
        [pltpu.VMEM((PEERS * 2 * PAIRS, 2 * LANES), bf16)],
        10**9,
        3 * 10**6,
    )(turned, jnp.asarray(upper), jnp.asarray(lower), cos_screen, sin_screen)
    got = lax.all_to_all(
        shares.reshape(LAYERS, 2, LANES), ("x", "z"), split_axis=0, concat_axis=0, tiled=True
    ).reshape(2 * LAYERS, LANES)
    return call(sum_kernel, (8, LANES), [VMEM], [], 10**5, 7 * 10**4)(got)


def solution(mesh):
    whole = ("x", "z", "slab")
    chips = Mesh(mesh.devices.reshape(X_CHIPS, Z_CHIPS, N_SLAB), whole)
    placed = (P(whole, None, None), P(whole, None), P(whole, None), P(whole), P(whole))
    return jax.shard_map(
        body, mesh=chips, in_specs=placed, out_specs=P(("x", "z"), "slab"), check_vma=False
    )
```

```python
import math

import ml_dtypes
import numpy as np

import jax
import jax.numpy as jnp
from jax import lax
from jax.experimental import pallas as pl
from jax.experimental.pallas import tpu as pltpu
from jax.sharding import Mesh
from jax.sharding import PartitionSpec as P

NG = 4096
VIS = 128
RB = 16
CB = 128
ROWS_DEV = 32
IMG_L = 512
IMG_M = 1024
CAP = 2
LAYERS = 64
N_SLAB = 8
X_CHIPS = 4
Z_CHIPS = 16
SUB = 32
SLOTS = LAYERS * CAP
LANES = 128
SENT = 4 * CAP + 1
PEERS = X_CHIPS * N_SLAB
PAIRS = RB // 2


kernel_width = 1.0
cell_size = 2.4e-05
w_reach = 20000.0

f32 = jnp.float32
bf16 = jnp.bfloat16
VMEM = pl.BlockSpec(memory_space=pltpu.VMEM)
HBM = pl.BlockSpec(memory_space=pltpu.HBM)
NT = (((1,), (1,)), ((), ()))
NN = (((1,), (0,)), ((), ()))


def wave(turns, period):
    angle = 2.0 * np.pi * (np.asarray(turns) % period) / period
    return np.cos(angle), np.sin(angle)


def np_split(table):
    table = np.asarray(table, np.float32)
    upper = table.astype(ml_dtypes.bfloat16)
    return upper, (table - upper.astype(np.float32)).astype(ml_dtypes.bfloat16)


def split(value):
    upper = value.astype(bf16)
    return upper, (value - upper.astype(f32)).astype(bf16)


def dot(left, right, dims):
    return lax.dot_general(left, right, dims, preferred_element_type=f32)


def route_kernel(*refs):
    given, out_ref, held, (count_ref, blocks_ref, sems) = refs[:5], refs[5], refs[6:11], refs[11:]
    layer_ref, block_ref, vis_ref, row_ref, col_ref = held
    copies = [
        pltpu.make_async_copy(source, target, sems.at[index])
        for index, (source, target) in enumerate(zip(given, held))
    ]
    for copy in copies:
        copy.start()
    out_ref[...] = jnp.zeros_like(out_ref)

    def clear(layer, carry):
        count_ref[layer] = 0
        blocks_ref[layer * CAP] = 0
        blocks_ref[layer * CAP + 1] = 0
        return carry

    lax.fori_loop(0, LAYERS, clear, 0, unroll=8)
    for copy in copies:
        copy.wait()

    def place(tile, carry):
        layer = layer_ref[tile]
        slot = count_ref[layer]
        count_ref[layer] = slot + 1
        blocks_ref[layer * CAP + slot] = block_ref[tile]
        start = layer * SENT + slot * 4
        out_ref[pl.ds(start, 2), :] = vis_ref[pl.ds(2 * tile, 2), :]
        out_ref[pl.ds(start + 2, 1), :] = row_ref[pl.ds(tile, 1), :]
        out_ref[pl.ds(start + 3, 1), :] = col_ref[pl.ds(tile, 1), :]
        return carry

    tiles = layer_ref.shape[0]
    lax.fori_loop(0, tiles, place, 0, unroll=8)
    lower = lax.broadcasted_iota(jnp.int32, (1, LANES), 1) < LANES // CAP

    def name(layer, carry):
        both = jnp.where(lower, blocks_ref[layer * CAP], blocks_ref[layer * CAP + 1])
        out_ref[pl.ds(layer * SENT + 4 * CAP, 1), :] = both.astype(f32)
        return carry

    lax.fori_loop(0, LAYERS, name, 0, unroll=8)


def turn_by(value, step, period):
    real, imag = value
    step = step % period
    if 4 * step % period == 0:
        quarter = 4 * step // period
        return [(real, imag), (-imag, real), (-real, -imag), (imag, -real)][quarter]
    angle = 2.0 * math.pi * step / period
    cos_part, sin_part = math.cos(angle), math.sin(angle)
    return real * cos_part - imag * sin_part, real * sin_part + imag * cos_part


def dft(values):
    count = len(values)
    if count == 1:
        return values
    even, odd = dft(values[::2]), dft(values[1::2])
    odd = [turn_by(value, index, count) for index, value in enumerate(odd)]
    return [(a[0] + b[0], a[1] + b[1]) for a, b in zip(even, odd)] + [
        (a[0] - b[0], a[1] - b[1]) for a, b in zip(even, odd)
    ]


def grid_kernel(
    got_ref, twist_ref, last_ref, out_ref, grid_ref, upper_ref, lower_ref, name_ref, block_ref, sem
):
    named = got_ref[pl.ds(4 * CAP, LAYERS, stride=SENT), :]
    source = lax.broadcasted_iota(jnp.int32, (LAYERS, SLOTS), 0)
    lane = lax.broadcasted_iota(jnp.int32, (LAYERS, SLOTS), 1)
    name_ref[...] = jnp.sum(
        jnp.where(source == jnp.bitwise_and(lane, LAYERS - 1), named, 0.0), 0, keepdims=True
    ).astype(jnp.int32)
    copy = pltpu.make_async_copy(name_ref, block_ref, sem)
    copy.start()
    grid_ref[...] = jnp.zeros_like(grid_ref)
    offsets = jnp.concatenate(
        [got_ref[pl.ds(4 * slot + 3, LAYERS, stride=SENT), :] for slot in range(CAP)], 0
    ).T
    rows = lax.broadcasted_iota(jnp.int32, (RB, VIS), 0).astype(f32) + 0.5
    cols = lax.broadcasted_iota(jnp.int32, (VIS, CB), 1).astype(f32) + 0.5
    empty = jnp.zeros((2 * RB, VIS), bf16)
    copy.wait()

    def one(source, slot, center):
        start = source * SENT + 4 * slot
        real = got_ref[pl.ds(start, 1), :]
        imag = got_ref[pl.ds(start + 1, 1), :]
        away = rows - got_ref[pl.ds(start + 2, 1), :]
        near = jnp.exp(-0.5 * (away * away))
        upper, lower = split(jnp.concatenate([near * real, near * imag], 0))
        away = cols - center
        col_upper, col_lower = split(jnp.exp(-0.5 * (away * away)))
        left = jnp.concatenate(
            [jnp.concatenate([upper, upper], 1), jnp.concatenate([lower, empty], 1)], 0
        )
        both = dot(left, jnp.concatenate([col_upper, col_lower], 0), NN)
        grid_ref[block_ref[0, slot * LAYERS + source]] += both[: 2 * RB] + both[2 * RB :]

    together = 16

    def some(step, held):
        for part in range(together):
            for slot in range(CAP):
                lane = slot * LAYERS + part
                one(step * together + part, slot, held[:, lane : lane + 1])
        return pltpu.roll(held, SLOTS - together, 1)

    lax.fori_loop(0, LAYERS // together, some, offsets)

    wide, narrow = 8, SUB // 8
    for second in range(2):
        for low in range(wide):
            at = [second * SUB + low + wide * high for high in range(narrow)]
            turned = dft([(grid_ref[k, :RB, :], grid_ref[k, RB:, :]) for k in at])
            for index, k in enumerate(at):
                real, imag = turn_by(turned[index], index * low, SUB)
                grid_ref[k, :RB, :] = real
                grid_ref[k, RB:, :] = imag
        for low in range(narrow):
            at = [second * SUB + wide * low + high for high in range(wide)]
            turned = dft([(grid_ref[k, :RB, :], grid_ref[k, RB:, :]) for k in at])
            for index, (real, imag) in enumerate(turned):
                q = low + narrow * index
                cos_part = twist_ref[q : q + 1, :]
                sin_part = twist_ref[SUB + q : SUB + q + 1, :]
                upper, lower = split(
                    jnp.concatenate(
                        [real * cos_part - imag * sin_part, real * sin_part + imag * cos_part], 1
                    )
                )
                place = (second * SUB + q) * RB
                upper_ref[place : place + RB, :] = upper
                lower_ref[place : place + RB, :] = lower

    last_both = last_ref[...]
    last_upper = last_both[: 2 * SUB]
    for pair in range(PAIRS // 2):
        piece = slice(pair * 2 * LANES, (pair + 1) * 2 * LANES)
        both = dot(last_both, upper_ref[piece, :], NT)
        wave_sum = both[: 2 * SUB] + both[2 * SUB :] + dot(last_upper, lower_ref[piece, :], NT)
        for half in range(2):
            for part in range(2):
                row = 2 * (2 * pair + half) + part
                out_ref[pl.ds(row, PEERS, stride=2 * PAIRS), :] = wave_sum[
                    part * PEERS : (part + 1) * PEERS, half * LANES : (half + 1) * LANES
                ]


def swap_blocks(value):
    line = lax.broadcasted_iota(jnp.int32, value.shape, 0)
    block = lax.broadcasted_iota(jnp.int32, value.shape, 1) // RB
    for step in (4, 2, 1):
        line_bit = jnp.bitwise_and(line, step) != 0
        block_bit = jnp.bitwise_and(block, step) != 0
        up = pltpu.roll(pltpu.roll(value, 8 - step, 0), RB * step, 1)
        down = pltpu.roll(pltpu.roll(value, step, 0), LANES - RB * step, 1)
        moved = jnp.where(line_bit, down, up)
        value = jnp.where(line_bit == block_bit, value, moved)
    return value


def image_kernel(got_ref, upper_ref, lower_ref, cos_ref, sin_ref, out_ref, right_ref):
    blocks = SUB // N_SLAB
    for layer in range(X_CHIPS):
        for pair in range(blocks // 2):
            lines = []
            for high in (2 * pair, 2 * pair + 1):
                parts = []
                for y in range(2):
                    for h in range(2):
                        step = 2 * (h * blocks + high) + y
                        row = layer * N_SLAB * 2 * PAIRS + step
                        parts.append(
                            swap_blocks(got_ref[pl.ds(row, N_SLAB, stride=2 * PAIRS), :])
                        )
                lines.append(jnp.concatenate(parts, 1))
            upper, lower = split(jnp.concatenate(lines, 0))
            row = layer * SUB + pair * 2 * N_SLAB
            right_ref[row : row + 2 * N_SLAB, :] = upper
            right_ref[LANES + row : LANES + row + 2 * N_SLAB, :] = lower
    count = IMG_L // X_CHIPS
    group = lax.broadcasted_iota(jnp.int32, (count, LANES), 1) // SUB
    right = right_ref[...]
    total = None
    for part in range(X_CHIPS):
        rows = pl.ds(part * 2 * count, 2 * count)
        both = dot(upper_ref[rows, :], right, NT)
        wave_sum = both[:, :LANES] + both[:, LANES:] + dot(lower_ref[rows, :], right[:LANES], NT)
        lines = pl.ds(part * count, count)
        screened = wave_sum[:count] * cos_ref[lines, :] - wave_sum[count:] * sin_ref[lines, :]
        screened = screened + pltpu.roll(screened, 2 * SUB, 1)
        screened = screened + pltpu.roll(screened, SUB, 1)
        total = screened if total is None else jnp.where(group == part, screened, total)
    out_ref[...] = total


def sum_kernel(got_ref, out_ref):
    line = lax.broadcasted_iota(jnp.int32, (8, LANES), 0)
    group = lax.broadcasted_iota(jnp.int32, (8, LANES), 1) // SUB
    straight = (line // 4) == jnp.bitwise_and(line, 1)
    result = jnp.zeros((8, LANES), f32)
    for chip in range(X_CHIPS):
        total = got_ref[pl.ds(chip * 2 * Z_CHIPS, 8), :]
        for step in range(1, 2 * Z_CHIPS // 8):
            total = total + got_ref[pl.ds(chip * 2 * Z_CHIPS + 8 * step, 8), :]
        total = total + pltpu.roll(total, 4, 0)
        total = total + pltpu.roll(total, 2, 0)
        total = jnp.where(straight, total, pltpu.roll(total, 1, 0))
        for part in range(X_CHIPS):
            shift = (chip - part) % X_CHIPS
            moved = pltpu.roll(total, SUB * shift, 1) if shift else total
            chosen = (group == chip) & (jnp.bitwise_and(line, 3) == part)
            result = jnp.where(chosen, moved, result)
    out_ref[...] = result


def call(kernel, shape, specs, scratch, flops, moved, limit=24):
    return pl.pallas_call(
        kernel,
        out_shape=jax.ShapeDtypeStruct(shape, f32),
        in_specs=specs,
        out_specs=VMEM,
        scratch_shapes=scratch,
        compiler_params=pltpu.CompilerParams(vmem_limit_bytes=limit * 1024 * 1024),
        cost_estimate=pl.CostEstimate(flops=flops, bytes_accessed=moved, transcendentals=0),
    )


def grid_tables():
    q = np.arange(SUB)
    c = np.arange(CB)
    sign = (1 - 2 * (q % 2))[:, None]
    twist = np.concatenate([part * sign for part in wave(q[:, None] * c[None, :], NG)], 0)
    n = (4 * np.arange(N_SLAB)[None, :] + np.arange(X_CHIPS)[:, None]).reshape(-1)
    cos_part, sin_part = wave((n[:, None] - SUB // 2) * c[None, :], CB)
    last = np.concatenate(
        [
            np.concatenate([cos_part, -sin_part], 1),
            np.concatenate([sin_part, cos_part], 1),
        ],
        0,
    )
    return twist.astype(np.float32), np.concatenate(np_split(last), 0)


def image_lines():
    part, chip, half = np.meshgrid(np.arange(4), np.arange(LAYERS), np.arange(2), indexing="ij")
    return (8 * chip + 4 * half + part).reshape(-1) - IMG_L // 2


def image_tables(spread):
    y, h, slab, r = np.meshgrid(
        np.arange(2), np.arange(2), np.arange(N_SLAB), np.arange(RB), indexing="ij"
    )
    row = (slab * ROWS_DEV + h * RB + r).reshape(-1) - ROWS_DEV * N_SLAB // 2
    y = y.reshape(-1)[None, :]
    cos_part, sin_part = wave(image_lines()[:, None] * row[None, :], NG)
    real = np.where(y == 0, cos_part, -sin_part).reshape(4, -1, row.size)
    imag = np.where(y == 0, sin_part, cos_part).reshape(4, -1, row.size)
    return np_split(np.concatenate([real, imag], 1).reshape(2 * IMG_L, row.size) * spread)


def screen_tables():
    columns = IMG_M // N_SLAB
    lines = jnp.asarray(image_lines().astype(np.float32))
    lane = jnp.arange(LANES, dtype=jnp.int32)
    m_index = (
        lax.axis_index("slab") * columns
        + lax.axis_index("x") * SUB
        + jnp.bitwise_and(lane, SUB - 1)
        - IMG_M // 2
    )
    layer = ((lane // SUB) * Z_CHIPS + lax.axis_index("z")).astype(f32)
    w_value = w_reach * (2.0 * layer + 1.0 - LAYERS) / LAYERS
    l_direction = lines[:, None] * cell_size
    m_direction = m_index.astype(f32)[None, :] * cell_size
    radius = l_direction * l_direction + m_direction * m_direction
    n_lift = -radius / (1.0 + jnp.sqrt(1.0 - radius))
    phase_angle = -2.0 * math.pi * w_value[None, :] * n_lift
    return jnp.cos(phase_angle), jnp.sin(phase_angle)


def body(visibilities, row_offset, col_offset, w_layer, grid_block):
    tiles = w_layer.shape[0]
    spread = 1.0 / (
        2.0 * math.pi * kernel_width**2 * math.sqrt(tiles * LAYERS * N_SLAB * VIS)
    )
    sent = call(
        route_kernel,
        (LAYERS * SENT, VIS),
        [HBM] * 5,
        [
            pltpu.SMEM((tiles,), jnp.int32),
            pltpu.SMEM((tiles,), jnp.int32),
            pltpu.VMEM((2 * tiles, VIS), f32),
            pltpu.VMEM((tiles, VIS), f32),
            pltpu.VMEM((tiles, VIS), f32),
            pltpu.SMEM((LAYERS,), jnp.int32),
            pltpu.SMEM((SLOTS,), jnp.int32),
            pltpu.SemaphoreType.DMA((5,)),
        ],
        10**6,
        5 * 10**5,
        limit=60,
    )(w_layer, grid_block, visibilities.reshape(2 * tiles, VIS), row_offset, col_offset)
    got = lax.all_to_all(
        sent.reshape(LAYERS, 1, SENT * VIS), ("x", "z"), split_axis=0, concat_axis=0, tiled=True
    ).reshape(LAYERS * SENT, VIS)
    cos_screen, sin_screen = screen_tables()
    twist, last = grid_tables()
    pieces = call(
        grid_kernel,
        (PEERS * 2 * PAIRS, LANES),
        [VMEM] * 3,
        [
            pltpu.VMEM((2 * SUB, 2 * RB, CB), f32),
            pltpu.VMEM((2 * SUB * RB, 2 * CB), bf16),
            pltpu.VMEM((2 * SUB * RB, 2 * CB), bf16),
            pltpu.VMEM((1, SLOTS), jnp.int32),
            pltpu.SMEM((1, SLOTS), jnp.int32),
            pltpu.SemaphoreType.DMA,
        ],
        10**9,
        10**6,
    )(got, jnp.asarray(twist), jnp.asarray(last))
    turned = lax.all_to_all(
        pieces.reshape(PEERS, 2 * PAIRS, LANES),
        ("x", "slab"),
        split_axis=0,
        concat_axis=0,
        tiled=True,
    ).reshape(PEERS * 2 * PAIRS, LANES)
    upper, lower = image_tables(spread)
    shares = call(
        image_kernel,
        (2 * LAYERS, LANES),
        [VMEM] * 5,
        [pltpu.VMEM((2 * LANES, 2 * ROWS_DEV * N_SLAB), bf16)],
        10**9,
        3 * 10**6,
    )(turned, jnp.asarray(upper), jnp.asarray(lower), cos_screen, sin_screen)
    got = lax.all_to_all(
        shares.reshape(LAYERS, 2, LANES), ("x", "z"), split_axis=0, concat_axis=0, tiled=True
    ).reshape(2 * LAYERS, LANES)
    return call(sum_kernel, (8, LANES), [VMEM], [], 10**5, 7 * 10**4)(got)


def solution(mesh):
    whole = ("x", "z", "slab")
    chips = Mesh(mesh.devices.reshape(X_CHIPS, Z_CHIPS, N_SLAB), whole)
    placed = (P(whole, None, None), P(whole, None), P(whole, None), P(whole), P(whole))
    return jax.shard_map(
        body, mesh=chips, in_specs=placed, out_specs=P(("x", "z"), "slab"), check_vma=False
    )
```

```python
import math

import ml_dtypes
import numpy as np

import jax
import jax.numpy as jnp
from jax import lax
from jax.experimental import pallas as pl
from jax.experimental.pallas import tpu as pltpu
from jax.sharding import Mesh
from jax.sharding import PartitionSpec as P

NG = 4096
VIS = 128
RB = 16
CB = 128
ROWS_DEV = 32
IMG_L = 512
IMG_M = 1024
CAP = 2
LAYERS = 64
N_SLAB = 8
X_CHIPS = 4
Z_CHIPS = 16
FIRST_X = 2
FIRST_SLAB = 4
TILE_Z = 9
IMAGE_Z = 8
SUB = 32
SLOTS = LAYERS * CAP
LANES = 128
SENT = 4 * CAP + 1
PEERS = X_CHIPS * N_SLAB
PAIRS = RB // 2
NARROW = math.sqrt(0.5 / math.log(2.0))


kernel_width = 1.0
cell_size = 2.4e-05
w_reach = 20000.0

f32 = jnp.float32
bf16 = jnp.bfloat16
VMEM = pl.BlockSpec(memory_space=pltpu.VMEM)
HBM = pl.BlockSpec(memory_space=pltpu.HBM)
NT = (((1,), (1,)), ((), ()))
NN = (((1,), (0,)), ((), ()))


def wave(turns, period):
    angle = 2.0 * np.pi * (np.asarray(turns) % period) / period
    return np.cos(angle), np.sin(angle)


def np_split(table):
    table = np.asarray(table, np.float32)
    upper = table.astype(ml_dtypes.bfloat16)
    return upper, (table - upper.astype(np.float32)).astype(ml_dtypes.bfloat16)


def split(value):
    upper = value.astype(bf16)
    return upper, (value - upper.astype(f32)).astype(bf16)


def dot(left, right, dims):
    return lax.dot_general(left, right, dims, preferred_element_type=f32)


def route_kernel(*refs):
    given, out_ref, held, (count_ref, blocks_ref, sems) = refs[:5], refs[5], refs[6:11], refs[11:]
    layer_ref, block_ref, vis_ref, row_ref, col_ref = held
    copies = [
        pltpu.make_async_copy(source, target, sems.at[index])
        for index, (source, target) in enumerate(zip(given, held))
    ]
    for copy in copies:
        copy.start()
    out_ref[...] = jnp.zeros_like(out_ref)

    def clear(layer, carry):
        count_ref[layer] = 0
        blocks_ref[layer * CAP] = 0
        blocks_ref[layer * CAP + 1] = 0
        return carry

    lax.fori_loop(0, LAYERS, clear, 0, unroll=8)
    for copy in copies:
        copy.wait()

    def place(tile, carry):
        layer = layer_ref[tile]
        slot = count_ref[layer]
        count_ref[layer] = slot + 1
        blocks_ref[layer * CAP + slot] = block_ref[tile]
        start = layer * SENT + slot * 4
        out_ref[pl.ds(start, 2), :] = vis_ref[pl.ds(2 * tile, 2), :]
        out_ref[pl.ds(start + 2, 1), :] = row_ref[pl.ds(tile, 1), :]
        out_ref[pl.ds(start + 3, 1), :] = col_ref[pl.ds(tile, 1), :]
        return carry

    tiles = layer_ref.shape[0]
    lax.fori_loop(0, tiles, place, 0, unroll=8)
    lower = lax.broadcasted_iota(jnp.int32, (1, LANES), 1) < LANES // CAP

    def name(layer, carry):
        both = jnp.where(lower, blocks_ref[layer * CAP], blocks_ref[layer * CAP + 1])
        out_ref[pl.ds(layer * SENT + 4 * CAP, 1), :] = both.astype(f32)
        return carry

    lax.fori_loop(0, LAYERS, name, 0, unroll=8)


def turn_by(value, step, period):
    real, imag = value
    step = step % period
    if 4 * step % period == 0:
        quarter = 4 * step // period
        return [(real, imag), (-imag, real), (-real, -imag), (imag, -real)][quarter]
    angle = 2.0 * math.pi * step / period
    cos_part, sin_part = math.cos(angle), math.sin(angle)
    return real * cos_part - imag * sin_part, real * sin_part + imag * cos_part


def dft(values):
    count = len(values)
    if count == 1:
        return values
    even, odd = dft(values[::2]), dft(values[1::2])
    odd = [turn_by(value, index, count) for index, value in enumerate(odd)]
    return [(a[0] + b[0], a[1] + b[1]) for a, b in zip(even, odd)] + [
        (a[0] - b[0], a[1] - b[1]) for a, b in zip(even, odd)
    ]


def grid_kernel(
    got_ref, twist_ref, last_ref, out_ref, grid_ref, upper_ref, lower_ref, name_ref, block_ref, sem
):
    named = got_ref[pl.ds(4 * CAP, LAYERS, stride=SENT), :]
    source = lax.broadcasted_iota(jnp.int32, (LAYERS, SLOTS), 0)
    lane = lax.broadcasted_iota(jnp.int32, (LAYERS, SLOTS), 1)
    name_ref[...] = jnp.sum(
        jnp.where(source == jnp.bitwise_and(lane, LAYERS - 1), named, 0.0), 0, keepdims=True
    ).astype(jnp.int32)
    copy = pltpu.make_async_copy(name_ref, block_ref, sem)
    copy.start()
    grid_ref[...] = jnp.zeros_like(grid_ref)
    offsets = jnp.concatenate(
        [got_ref[pl.ds(4 * slot + 3, LAYERS, stride=SENT), :] for slot in range(CAP)], 0
    ).T * NARROW
    rows = (lax.broadcasted_iota(jnp.int32, (RB, VIS), 0).astype(f32) + 0.5) * NARROW
    cols = (lax.broadcasted_iota(jnp.int32, (VIS, CB), 1).astype(f32) + 0.5) * NARROW
    empty = jnp.zeros((2 * RB, VIS), bf16)
    copy.wait()

    def one(source, slot, center):
        start = source * SENT + 4 * slot
        real = got_ref[pl.ds(start, 1), :]
        imag = got_ref[pl.ds(start + 1, 1), :]
        away = rows - got_ref[pl.ds(start + 2, 1), :] * NARROW
        near = jnp.exp2(-(away * away))
        upper, lower = split(jnp.concatenate([near * real, near * imag], 0))
        away = cols - center
        col_upper, col_lower = split(jnp.exp2(-(away * away)))
        left = jnp.concatenate(
            [jnp.concatenate([upper, upper], 1), jnp.concatenate([lower, empty], 1)], 0
        )
        both = dot(left, jnp.concatenate([col_upper, col_lower], 0), NN)
        grid_ref[block_ref[0, slot * LAYERS + source]] += both[: 2 * RB] + both[2 * RB :]

    together = 16

    def some(step, held):
        for part in range(together):
            for slot in range(CAP):
                lane = slot * LAYERS + part
                one(step * together + part, slot, held[:, lane : lane + 1])
        return pltpu.roll(held, SLOTS - together, 1)

    lax.fori_loop(0, LAYERS // together, some, offsets)

    wide, narrow = 8, SUB // 8
    for second in range(2):
        for low in range(wide):
            at = [second * SUB + low + wide * high for high in range(narrow)]
            turned = dft([(grid_ref[k, :RB, :], grid_ref[k, RB:, :]) for k in at])
            for index, k in enumerate(at):
                real, imag = turn_by(turned[index], index * low, SUB)
                grid_ref[k, :RB, :] = real
                grid_ref[k, RB:, :] = imag
        for low in range(narrow):
            at = [second * SUB + wide * low + high for high in range(wide)]
            turned = dft([(grid_ref[k, :RB, :], grid_ref[k, RB:, :]) for k in at])
            for index, (real, imag) in enumerate(turned):
                q = low + narrow * index
                cos_part = twist_ref[q : q + 1, :]
                sin_part = twist_ref[SUB + q : SUB + q + 1, :]
                upper, lower = split(
                    jnp.concatenate(
                        [real * cos_part - imag * sin_part, real * sin_part + imag * cos_part], 1
                    )
                )
                place = (second * SUB + q) * RB
                upper_ref[place : place + RB, :] = upper
                lower_ref[place : place + RB, :] = lower

    last_both = last_ref[...]
    last_upper = last_both[: 2 * SUB]
    for pair in range(PAIRS // 2):
        piece = slice(pair * 2 * LANES, (pair + 1) * 2 * LANES)
        both = dot(last_both, upper_ref[piece, :], NT)
        wave_sum = both[: 2 * SUB] + both[2 * SUB :] + dot(last_upper, lower_ref[piece, :], NT)
        for half in range(2):
            for part in range(2):
                row = 2 * (2 * pair + half) + part
                out_ref[pl.ds(row, PEERS, stride=2 * PAIRS), :] = wave_sum[
                    part * PEERS : (part + 1) * PEERS, half * LANES : (half + 1) * LANES
                ]


def swap_blocks(value):
    line = lax.broadcasted_iota(jnp.int32, value.shape, 0)
    block = lax.broadcasted_iota(jnp.int32, value.shape, 1) // RB
    for step in (4, 2, 1):
        line_bit = jnp.bitwise_and(line, step) != 0
        block_bit = jnp.bitwise_and(block, step) != 0
        up = pltpu.roll(pltpu.roll(value, 8 - step, 0), RB * step, 1)
        down = pltpu.roll(pltpu.roll(value, step, 0), LANES - RB * step, 1)
        moved = jnp.where(line_bit, down, up)
        value = jnp.where(line_bit == block_bit, value, moved)
    return value


def image_kernel(got_ref, upper_ref, lower_ref, cos_ref, sin_ref, out_ref, right_ref):
    blocks = SUB // N_SLAB
    for layer in range(X_CHIPS):
        for pair in range(blocks // 2):
            lines = []
            for high in (2 * pair, 2 * pair + 1):
                parts = []
                for y in range(2):
                    for h in range(2):
                        step = 2 * (h * blocks + high) + y
                        row = layer * N_SLAB * 2 * PAIRS + step
                        parts.append(
                            swap_blocks(got_ref[pl.ds(row, N_SLAB, stride=2 * PAIRS), :])
                        )
                lines.append(jnp.concatenate(parts, 1))
            upper, lower = split(jnp.concatenate(lines, 0))
            row = layer * SUB + pair * 2 * N_SLAB
            right_ref[row : row + 2 * N_SLAB, :] = upper
            right_ref[LANES + row : LANES + row + 2 * N_SLAB, :] = lower
    count = IMG_L // X_CHIPS
    group = lax.broadcasted_iota(jnp.int32, (count, LANES), 1) // SUB
    right = right_ref[...]
    total = None
    for part in range(X_CHIPS):
        rows = pl.ds(part * 2 * count, 2 * count)
        both = dot(upper_ref[rows, :], right, NT)
        wave_sum = both[:, :LANES] + both[:, LANES:] + dot(lower_ref[rows, :], right[:LANES], NT)
        lines = pl.ds(part * count, count)
        screened = wave_sum[:count] * cos_ref[lines, :] - wave_sum[count:] * sin_ref[lines, :]
        screened = screened + pltpu.roll(screened, 2 * SUB, 1)
        screened = screened + pltpu.roll(screened, SUB, 1)
        total = screened if total is None else jnp.where(group == part, screened, total)
    out_ref[...] = total


def sum_kernel(got_ref, out_ref):
    line = lax.broadcasted_iota(jnp.int32, (8, LANES), 0)
    group = lax.broadcasted_iota(jnp.int32, (8, LANES), 1) // SUB
    straight = (line // 4) == jnp.bitwise_and(line, 1)
    result = jnp.zeros((8, LANES), f32)
    for place in range(X_CHIPS):
        chip = (place + FIRST_X) % X_CHIPS
        total = got_ref[pl.ds(place * 2 * Z_CHIPS, 8), :]
        for step in range(1, 2 * Z_CHIPS // 8):
            total = total + got_ref[pl.ds(place * 2 * Z_CHIPS + 8 * step, 8), :]
        total = total + pltpu.roll(total, 4, 0)
        total = total + pltpu.roll(total, 2, 0)
        total = jnp.where(straight, total, pltpu.roll(total, 1, 0))
        for part in range(X_CHIPS):
            shift = (chip - part) % X_CHIPS
            moved = pltpu.roll(total, SUB * shift, 1) if shift else total
            chosen = (group == chip) & (jnp.bitwise_and(line, 3) == part)
            result = jnp.where(chosen, moved, result)
    out_ref[...] = result


def call(kernel, shape, specs, scratch, flops, moved, limit=24):
    return pl.pallas_call(
        kernel,
        out_shape=jax.ShapeDtypeStruct(shape, f32),
        in_specs=specs,
        out_specs=VMEM,
        scratch_shapes=scratch,
        compiler_params=pltpu.CompilerParams(vmem_limit_bytes=limit * 1024 * 1024),
        cost_estimate=pl.CostEstimate(flops=flops, bytes_accessed=moved, transcendentals=0),
    )


def grid_tables():
    q = np.arange(SUB)
    c = np.arange(CB)
    sign = (1 - 2 * (q % 2))[:, None]
    twist = np.concatenate([part * sign for part in wave(q[:, None] * c[None, :], NG)], 0)
    x, slab = np.divmod(column_members(), N_SLAB)
    n = 4 * slab + x
    cos_part, sin_part = wave((n[:, None] - SUB // 2) * c[None, :], CB)
    last = np.concatenate(
        [
            np.concatenate([cos_part, -sin_part], 1),
            np.concatenate([sin_part, cos_part], 1),
        ],
        0,
    )
    return twist.astype(np.float32), np.concatenate(np_split(last), 0)


def rotated(slow, fast, first_slow, first_fast):
    i, j = np.meshgrid(np.arange(slow), np.arange(fast), indexing="ij")
    return ((i + first_slow) % slow * fast + (j + first_fast) % fast).reshape(-1)


def layer_members():
    return rotated(X_CHIPS, Z_CHIPS, FIRST_X, TILE_Z)


def column_members():
    return rotated(X_CHIPS, N_SLAB, FIRST_X, FIRST_SLAB)


def image_members():
    return rotated(X_CHIPS, Z_CHIPS, FIRST_X, IMAGE_Z)


def exchange(value, axes, members):
    groups = [[int(member) for member in members]]
    return lax.all_to_all(
        value, axes, split_axis=0, concat_axis=0, tiled=True, axis_index_groups=groups
    )


def image_lines():
    part, chip, half = np.meshgrid(
        np.arange(4), image_members(), np.arange(2), indexing="ij"
    )
    return (8 * chip + 4 * half + part).reshape(-1) - IMG_L // 2


def image_tables(spread):
    y, h, slab, r = np.meshgrid(
        np.arange(2), np.arange(2), np.arange(N_SLAB), np.arange(RB), indexing="ij"
    )
    slab = (slab + FIRST_SLAB) % N_SLAB
    row = (slab * ROWS_DEV + h * RB + r).reshape(-1) - ROWS_DEV * N_SLAB // 2
    y = y.reshape(-1)[None, :]
    cos_part, sin_part = wave(image_lines()[:, None] * row[None, :], NG)
    real = np.where(y == 0, cos_part, -sin_part).reshape(4, -1, row.size)
    imag = np.where(y == 0, sin_part, cos_part).reshape(4, -1, row.size)
    return np_split(np.concatenate([real, imag], 1).reshape(2 * IMG_L, row.size) * spread)


def screen_tables():
    columns = IMG_M // N_SLAB
    lines = jnp.asarray(image_lines().astype(np.float32))
    lane = jnp.arange(LANES, dtype=jnp.int32)
    m_index = (
        lax.axis_index("slab") * columns
        + lax.axis_index("x") * SUB
        + jnp.bitwise_and(lane, SUB - 1)
        - IMG_M // 2
    )
    place = (lax.axis_index("z") + Z_CHIPS - TILE_Z) % Z_CHIPS
    layer = ((lane // SUB) * Z_CHIPS + place).astype(f32)
    w_value = w_reach * (2.0 * layer + 1.0 - LAYERS) / LAYERS
    l_direction = lines[:, None] * cell_size
    m_direction = m_index.astype(f32)[None, :] * cell_size
    radius = l_direction * l_direction + m_direction * m_direction
    n_lift = -radius / (1.0 + jnp.sqrt(1.0 - radius))
    phase_angle = -2.0 * math.pi * w_value[None, :] * n_lift
    return jnp.cos(phase_angle), jnp.sin(phase_angle)


def body(visibilities, row_offset, col_offset, w_layer, grid_block):
    tiles = w_layer.shape[0]
    spread = 1.0 / (
        2.0 * math.pi * kernel_width**2 * math.sqrt(tiles * LAYERS * N_SLAB * VIS)
    )
    sent = call(
        route_kernel,
        (LAYERS * SENT, VIS),
        [HBM] * 5,
        [
            pltpu.SMEM((tiles,), jnp.int32),
            pltpu.SMEM((tiles,), jnp.int32),
            pltpu.VMEM((2 * tiles, VIS), f32),
            pltpu.VMEM((tiles, VIS), f32),
            pltpu.VMEM((tiles, VIS), f32),
            pltpu.SMEM((LAYERS,), jnp.int32),
            pltpu.SMEM((SLOTS,), jnp.int32),
            pltpu.SemaphoreType.DMA((5,)),
        ],
        10**6,
        5 * 10**5,
        limit=60,
    )(w_layer, grid_block, visibilities.reshape(2 * tiles, VIS), row_offset, col_offset)
    got = exchange(sent.reshape(LAYERS, 1, SENT * VIS), ("x", "z"), layer_members())
    got = got.reshape(LAYERS * SENT, VIS)
    cos_screen, sin_screen = screen_tables()
    twist, last = grid_tables()
    pieces = call(
        grid_kernel,
        (PEERS * 2 * PAIRS, LANES),
        [VMEM] * 3,
        [
            pltpu.VMEM((2 * SUB, 2 * RB, CB), f32),
            pltpu.VMEM((2 * SUB * RB, 2 * CB), bf16),
            pltpu.VMEM((2 * SUB * RB, 2 * CB), bf16),
            pltpu.VMEM((1, SLOTS), jnp.int32),
            pltpu.SMEM((1, SLOTS), jnp.int32),
            pltpu.SemaphoreType.DMA,
        ],
        10**9,
        10**6,
    )(got, jnp.asarray(twist), jnp.asarray(last))
    turned = exchange(
        pieces.reshape(PEERS, 2 * PAIRS, LANES), ("x", "slab"), column_members()
    ).reshape(PEERS * 2 * PAIRS, LANES)
    upper, lower = image_tables(spread)
    shares = call(
        image_kernel,
        (2 * LAYERS, LANES),
        [VMEM] * 5,
        [pltpu.VMEM((2 * LANES, 2 * ROWS_DEV * N_SLAB), bf16)],
        10**9,
        3 * 10**6,
    )(turned, jnp.asarray(upper), jnp.asarray(lower), cos_screen, sin_screen)
    got = exchange(shares.reshape(LAYERS, 2, LANES), ("x", "z"), image_members())
    got = got.reshape(2 * LAYERS, LANES)
    return call(sum_kernel, (8, LANES), [VMEM], [], 10**5, 7 * 10**4)(got)


def solution(mesh):
    whole = ("x", "z", "slab")
    chips = Mesh(mesh.devices.reshape(X_CHIPS, Z_CHIPS, N_SLAB), whole)
    placed = (P(whole, None, None), P(whole, None), P(whole, None), P(whole), P(whole))
    return jax.shard_map(
        body, mesh=chips, in_specs=placed, out_specs=P(("x", "z"), "slab"), check_vma=False
    )
```

```python
import math

import ml_dtypes
import numpy as np

import jax
import jax.numpy as jnp
from jax import lax
from jax.experimental import pallas as pl
from jax.experimental.pallas import tpu as pltpu
from jax.sharding import Mesh
from jax.sharding import PartitionSpec as P

NG = 4096
VIS = 128
RB = 16
CB = 128
ROWS_DEV = 32
IMG_L = 512
IMG_M = 1024
CAP = 2
LAYERS = 64
N_SLAB = 8
X_CHIPS = 4
Z_CHIPS = 16
FIRST_X = 2
FIRST_SLAB = 4
TILE_Z = 9
IMAGE_Z = 8
SUB = 32
SLOTS = LAYERS * CAP
LANES = 128
SENT = 4 * CAP + 1
PEERS = X_CHIPS * N_SLAB
PAIRS = RB // 2
NARROW = math.sqrt(0.5 / math.log(2.0))


kernel_width = 1.0
cell_size = 2.4e-05
w_reach = 20000.0

f32 = jnp.float32
bf16 = jnp.bfloat16
VMEM = pl.BlockSpec(memory_space=pltpu.VMEM)
HBM = pl.BlockSpec(memory_space=pltpu.HBM)
NT = (((1,), (1,)), ((), ()))
NN = (((1,), (0,)), ((), ()))


def wave(turns, period):
    angle = 2.0 * np.pi * (np.asarray(turns) % period) / period
    return np.cos(angle), np.sin(angle)


def np_split(table):
    table = np.asarray(table, np.float32)
    upper = table.astype(ml_dtypes.bfloat16)
    return upper, (table - upper.astype(np.float32)).astype(ml_dtypes.bfloat16)


def split(value):
    upper = value.astype(bf16)
    return upper, (value - upper.astype(f32)).astype(bf16)


def dot(left, right, dims):
    return lax.dot_general(left, right, dims, preferred_element_type=f32)


def route_kernel(*refs):
    given, out_ref, held, (count_ref, sems) = refs[:5], refs[5], refs[6:11], refs[11:]
    layer_ref, block_ref, vis_ref, row_ref, col_ref = held
    copies = [
        pltpu.make_async_copy(source, target, sems.at[index])
        for index, (source, target) in enumerate(zip(given, held))
    ]
    for copy in copies:
        copy.start()
    out_ref[...] = jnp.zeros_like(out_ref)

    def clear(layer, carry):
        count_ref[layer] = 0
        return carry

    lax.fori_loop(0, LAYERS, clear, 0, unroll=16)
    for copy in copies:
        copy.wait()
    part = lax.broadcasted_iota(jnp.int32, (1, LANES), 1) // (LANES // CAP)

    def place(tile, carry):
        layer = layer_ref[tile]
        slot = count_ref[layer]
        count_ref[layer] = slot + 1
        start = layer * SENT + slot * 4
        out_ref[pl.ds(start, 2), :] = vis_ref[pl.ds(2 * tile, 2), :]
        out_ref[pl.ds(start + 2, 1), :] = row_ref[pl.ds(tile, 1), :]
        out_ref[pl.ds(start + 3, 1), :] = col_ref[pl.ds(tile, 1), :]
        named = out_ref.at[pl.ds(layer * SENT + 4 * CAP, 1), :]
        block = jnp.full((1, LANES), block_ref[tile], jnp.int32).astype(f32)
        pltpu.store(named, block, mask=part == slot)
        return carry

    lax.fori_loop(0, layer_ref.shape[0], place, 0, unroll=16)


def turn_by(value, step, period):
    real, imag = value
    step = step % period
    if 4 * step % period == 0:
        quarter = 4 * step // period
        return [(real, imag), (-imag, real), (-real, -imag), (imag, -real)][quarter]
    angle = 2.0 * math.pi * step / period
    cos_part, sin_part = math.cos(angle), math.sin(angle)
    return real * cos_part - imag * sin_part, real * sin_part + imag * cos_part


def dft(values):
    count = len(values)
    if count == 1:
        return values
    even, odd = dft(values[::2]), dft(values[1::2])
    odd = [turn_by(value, index, count) for index, value in enumerate(odd)]
    return [(a[0] + b[0], a[1] + b[1]) for a, b in zip(even, odd)] + [
        (a[0] - b[0], a[1] - b[1]) for a, b in zip(even, odd)
    ]


def grid_kernel(
    got_ref, twist_ref, last_ref, out_ref, grid_ref, upper_ref, lower_ref, name_ref, block_ref, sem
):
    named = got_ref[pl.ds(4 * CAP, LAYERS, stride=SENT), :]
    source = lax.broadcasted_iota(jnp.int32, (LAYERS, SLOTS), 0)
    lane = lax.broadcasted_iota(jnp.int32, (LAYERS, SLOTS), 1)
    name_ref[...] = jnp.sum(
        jnp.where(source == jnp.bitwise_and(lane, LAYERS - 1), named, 0.0), 0, keepdims=True
    ).astype(jnp.int32)
    copy = pltpu.make_async_copy(name_ref, block_ref, sem)
    copy.start()
    grid_ref[...] = jnp.zeros_like(grid_ref)
    offsets = jnp.concatenate(
        [got_ref[pl.ds(4 * slot + 3, LAYERS, stride=SENT), :] for slot in range(CAP)], 0
    ).T * NARROW
    rows = (lax.broadcasted_iota(jnp.int32, (RB, VIS), 0).astype(f32) + 0.5) * NARROW
    cols = (lax.broadcasted_iota(jnp.int32, (VIS, CB), 1).astype(f32) + 0.5) * NARROW
    copy.wait()

    def one(source, slot, center):
        start = source * SENT + 4 * slot
        real = got_ref[pl.ds(start, 1), :]
        imag = got_ref[pl.ds(start + 1, 1), :]
        away = rows - got_ref[pl.ds(start + 2, 1), :] * NARROW
        near = jnp.exp2(-(away * away))
        upper, lower = split(jnp.concatenate([near * real, near * imag], 0))
        away = cols - center
        col_upper, col_lower = split(jnp.exp2(-(away * away)))
        left = jnp.concatenate([upper, lower], 0)
        both = dot(left, jnp.concatenate([col_upper, col_lower], 1), NN)
        patch = both[:, :CB] + both[:, CB:]
        grid_ref[block_ref[0, slot * LAYERS + source]] += patch[: 2 * RB] + patch[2 * RB :]

    together = 16

    def some(step, held):
        for part in range(together):
            for slot in range(CAP):
                lane = slot * LAYERS + part
                one(step * together + part, slot, held[:, lane : lane + 1])
        return pltpu.roll(held, SLOTS - together, 1)

    lax.fori_loop(0, LAYERS // together, some, offsets)

    wide, narrow = 8, SUB // 8
    for second in range(2):
        for low in range(wide):
            at = [second * SUB + low + wide * high for high in range(narrow)]
            turned = dft([(grid_ref[k, :RB, :], grid_ref[k, RB:, :]) for k in at])
            for index, k in enumerate(at):
                real, imag = turn_by(turned[index], index * low, SUB)
                grid_ref[k, :RB, :] = real
                grid_ref[k, RB:, :] = imag
        for low in range(narrow):
            at = [second * SUB + wide * low + high for high in range(wide)]
            turned = dft([(grid_ref[k, :RB, :], grid_ref[k, RB:, :]) for k in at])
            for index, (real, imag) in enumerate(turned):
                q = low + narrow * index
                cos_part = twist_ref[q : q + 1, :]
                sin_part = twist_ref[SUB + q : SUB + q + 1, :]
                upper, lower = split(
                    jnp.concatenate(
                        [real * cos_part - imag * sin_part, real * sin_part + imag * cos_part], 1
                    )
                )
                place = (second * SUB + q) * RB
                upper_ref[place : place + RB, :] = upper
                lower_ref[place : place + RB, :] = lower

    last_both = last_ref[...]
    last_upper = last_both[: 2 * SUB]
    for pair in range(PAIRS // 2):
        piece = slice(pair * 2 * LANES, (pair + 1) * 2 * LANES)
        both = dot(last_both, upper_ref[piece, :], NT)
        wave_sum = both[: 2 * SUB] + both[2 * SUB :] + dot(last_upper, lower_ref[piece, :], NT)
        for half in range(2):
            for part in range(2):
                row = 2 * (2 * pair + half) + part
                out_ref[pl.ds(row, PEERS, stride=2 * PAIRS), :] = wave_sum[
                    part * PEERS : (part + 1) * PEERS, half * LANES : (half + 1) * LANES
                ]


def swap_blocks(value):
    line = lax.broadcasted_iota(jnp.int32, value.shape, 0)
    block = lax.broadcasted_iota(jnp.int32, value.shape, 1) // RB
    for step in (4, 2, 1):
        line_bit = jnp.bitwise_and(line, step) != 0
        block_bit = jnp.bitwise_and(block, step) != 0
        up = pltpu.roll(pltpu.roll(value, 8 - step, 0), RB * step, 1)
        down = pltpu.roll(pltpu.roll(value, step, 0), LANES - RB * step, 1)
        moved = jnp.where(line_bit, down, up)
        value = jnp.where(line_bit == block_bit, value, moved)
    return value


def image_kernel(got_ref, upper_ref, lower_ref, cos_ref, sin_ref, out_ref, right_ref):
    blocks = SUB // N_SLAB
    for layer in range(X_CHIPS):
        for pair in range(blocks // 2):
            lines = []
            for high in (2 * pair, 2 * pair + 1):
                parts = []
                for y in range(2):
                    for h in range(2):
                        step = 2 * (h * blocks + high) + y
                        row = layer * N_SLAB * 2 * PAIRS + step
                        parts.append(
                            swap_blocks(got_ref[pl.ds(row, N_SLAB, stride=2 * PAIRS), :])
                        )
                lines.append(jnp.concatenate(parts, 1))
            upper, lower = split(jnp.concatenate(lines, 0))
            row = layer * SUB + pair * 2 * N_SLAB
            right_ref[row : row + 2 * N_SLAB, :] = upper
            right_ref[LANES + row : LANES + row + 2 * N_SLAB, :] = lower
    count = IMG_L // X_CHIPS
    group = lax.broadcasted_iota(jnp.int32, (count, LANES), 1) // SUB
    right = right_ref[...]
    total = None
    for part in range(X_CHIPS):
        rows = pl.ds(part * 2 * count, 2 * count)
        both = dot(upper_ref[rows, :], right, NT)
        wave_sum = both[:, :LANES] + both[:, LANES:] + dot(lower_ref[rows, :], right[:LANES], NT)
        lines = pl.ds(part * count, count)
        screened = wave_sum[:count] * cos_ref[lines, :] - wave_sum[count:] * sin_ref[lines, :]
        screened = screened + pltpu.roll(screened, 2 * SUB, 1)
        screened = screened + pltpu.roll(screened, SUB, 1)
        total = screened if total is None else jnp.where(group == part, screened, total)
    out_ref[...] = total


def sum_kernel(got_ref, out_ref):
    line = lax.broadcasted_iota(jnp.int32, (8, LANES), 0)
    group = lax.broadcasted_iota(jnp.int32, (8, LANES), 1) // SUB
    straight = (line // 4) == jnp.bitwise_and(line, 1)
    result = jnp.zeros((8, LANES), f32)
    for place in range(X_CHIPS):
        chip = (place + FIRST_X) % X_CHIPS
        total = got_ref[pl.ds(place * 2 * Z_CHIPS, 8), :]
        for step in range(1, 2 * Z_CHIPS // 8):
            total = total + got_ref[pl.ds(place * 2 * Z_CHIPS + 8 * step, 8), :]
        total = total + pltpu.roll(total, 4, 0)
        total = total + pltpu.roll(total, 2, 0)
        total = jnp.where(straight, total, pltpu.roll(total, 1, 0))
        for part in range(X_CHIPS):
            shift = (chip - part) % X_CHIPS
            moved = pltpu.roll(total, SUB * shift, 1) if shift else total
            chosen = (group == chip) & (jnp.bitwise_and(line, 3) == part)
            result = jnp.where(chosen, moved, result)
    out_ref[...] = result


def call(kernel, shape, specs, scratch, flops, moved, limit=24):
    return pl.pallas_call(
        kernel,
        out_shape=jax.ShapeDtypeStruct(shape, f32),
        in_specs=specs,
        out_specs=VMEM,
        scratch_shapes=scratch,
        compiler_params=pltpu.CompilerParams(vmem_limit_bytes=limit * 1024 * 1024),
        cost_estimate=pl.CostEstimate(flops=flops, bytes_accessed=moved, transcendentals=0),
    )


def grid_tables():
    q = np.arange(SUB)
    c = np.arange(CB)
    sign = (1 - 2 * (q % 2))[:, None]
    twist = np.concatenate([part * sign for part in wave(q[:, None] * c[None, :], NG)], 0)
    x, slab = np.divmod(column_members(), N_SLAB)
    n = 4 * slab + x
    cos_part, sin_part = wave((n[:, None] - SUB // 2) * c[None, :], CB)
    last = np.concatenate(
        [
            np.concatenate([cos_part, -sin_part], 1),
            np.concatenate([sin_part, cos_part], 1),
        ],
        0,
    )
    return twist.astype(np.float32), np.concatenate(np_split(last), 0)


def rotated(slow, fast, first_slow, first_fast):
    i, j = np.meshgrid(np.arange(slow), np.arange(fast), indexing="ij")
    return ((i + first_slow) % slow * fast + (j + first_fast) % fast).reshape(-1)


def layer_members():
    return rotated(X_CHIPS, Z_CHIPS, FIRST_X, TILE_Z)


def column_members():
    return rotated(X_CHIPS, N_SLAB, FIRST_X, FIRST_SLAB)


def image_members():
    return rotated(X_CHIPS, Z_CHIPS, FIRST_X, IMAGE_Z)


def exchange(value, axes, members):
    groups = [[int(member) for member in members]]
    return lax.all_to_all(
        value, axes, split_axis=0, concat_axis=0, tiled=True, axis_index_groups=groups
    )


def image_lines():
    part, chip, half = np.meshgrid(
        np.arange(4), image_members(), np.arange(2), indexing="ij"
    )
    return (8 * chip + 4 * half + part).reshape(-1) - IMG_L // 2


def image_tables(spread):
    y, h, slab, r = np.meshgrid(
        np.arange(2), np.arange(2), np.arange(N_SLAB), np.arange(RB), indexing="ij"
    )
    slab = (slab + FIRST_SLAB) % N_SLAB
    row = (slab * ROWS_DEV + h * RB + r).reshape(-1) - ROWS_DEV * N_SLAB // 2
    y = y.reshape(-1)[None, :]
    cos_part, sin_part = wave(image_lines()[:, None] * row[None, :], NG)
    real = np.where(y == 0, cos_part, -sin_part).reshape(4, -1, row.size)
    imag = np.where(y == 0, sin_part, cos_part).reshape(4, -1, row.size)
    return np_split(np.concatenate([real, imag], 1).reshape(2 * IMG_L, row.size) * spread)


def screen_tables():
    columns = IMG_M // N_SLAB
    lines = jnp.asarray(image_lines().astype(np.float32))
    lane = jnp.arange(LANES, dtype=jnp.int32)
    m_index = (
        lax.axis_index("slab") * columns
        + lax.axis_index("x") * SUB
        + jnp.bitwise_and(lane, SUB - 1)
        - IMG_M // 2
    )
    place = (lax.axis_index("z") + Z_CHIPS - TILE_Z) % Z_CHIPS
    layer = ((lane // SUB) * Z_CHIPS + place).astype(f32)
    w_value = w_reach * (2.0 * layer + 1.0 - LAYERS) / LAYERS
    l_direction = lines[:, None] * cell_size
    m_direction = m_index.astype(f32)[None, :] * cell_size
    radius = l_direction * l_direction + m_direction * m_direction
    n_lift = -radius / (1.0 + jnp.sqrt(1.0 - radius))
    phase_angle = -2.0 * math.pi * w_value[None, :] * n_lift
    return jnp.cos(phase_angle), jnp.sin(phase_angle)


def body(visibilities, row_offset, col_offset, w_layer, grid_block):
    tiles = w_layer.shape[0]
    spread = 1.0 / (
        2.0 * math.pi * kernel_width**2 * math.sqrt(tiles * LAYERS * N_SLAB * VIS)
    )
    sent = call(
        route_kernel,
        (LAYERS * SENT, VIS),
        [HBM] * 5,
        [
            pltpu.SMEM((tiles,), jnp.int32),
            pltpu.SMEM((tiles,), jnp.int32),
            pltpu.VMEM((2 * tiles, VIS), f32),
            pltpu.VMEM((tiles, VIS), f32),
            pltpu.VMEM((tiles, VIS), f32),
            pltpu.SMEM((LAYERS,), jnp.int32),
            pltpu.SemaphoreType.DMA((5,)),
        ],
        10**6,
        5 * 10**5,
        limit=60,
    )(w_layer, grid_block, visibilities.reshape(2 * tiles, VIS), row_offset, col_offset)
    got = exchange(sent.reshape(LAYERS, 1, SENT * VIS), ("x", "z"), layer_members())
    got = got.reshape(LAYERS * SENT, VIS)
    cos_screen, sin_screen = screen_tables()
    twist, last = grid_tables()
    pieces = call(
        grid_kernel,
        (PEERS * 2 * PAIRS, LANES),
        [VMEM] * 3,
        [
            pltpu.VMEM((2 * SUB, 2 * RB, CB), f32),
            pltpu.VMEM((2 * SUB * RB, 2 * CB), bf16),
            pltpu.VMEM((2 * SUB * RB, 2 * CB), bf16),
            pltpu.VMEM((1, SLOTS), jnp.int32),
            pltpu.SMEM((1, SLOTS), jnp.int32),
            pltpu.SemaphoreType.DMA,
        ],
        10**9,
        10**6,
    )(got, jnp.asarray(twist), jnp.asarray(last))
    turned = exchange(
        pieces.reshape(PEERS, 2 * PAIRS, LANES), ("x", "slab"), column_members()
    ).reshape(PEERS * 2 * PAIRS, LANES)
    upper, lower = image_tables(spread)
    shares = call(
        image_kernel,
        (2 * LAYERS, LANES),
        [VMEM] * 5,
        [pltpu.VMEM((2 * LANES, 2 * ROWS_DEV * N_SLAB), bf16)],
        10**9,
        3 * 10**6,
    )(turned, jnp.asarray(upper), jnp.asarray(lower), cos_screen, sin_screen)
    got = exchange(shares.reshape(LAYERS, 2, LANES), ("x", "z"), image_members())
    got = got.reshape(2 * LAYERS, LANES)
    return call(sum_kernel, (8, LANES), [VMEM], [], 10**5, 7 * 10**4)(got)


def solution(mesh):
    whole = ("x", "z", "slab")
    chips = Mesh(mesh.devices.reshape(X_CHIPS, Z_CHIPS, N_SLAB), whole)
    placed = (P(whole, None, None), P(whole, None), P(whole, None), P(whole), P(whole))
    return jax.shard_map(
        body, mesh=chips, in_specs=placed, out_specs=P(("x", "z"), "slab"), check_vma=False
    )
```

```python
import math

import ml_dtypes
import numpy as np

import jax
import jax.numpy as jnp
from jax import lax
from jax.experimental import pallas as pl
from jax.experimental.pallas import tpu as pltpu
from jax.sharding import Mesh
from jax.sharding import PartitionSpec as P

NG = 4096
VIS = 128
RB = 16
CB = 128
ROWS_DEV = 32
IMG_L = 512
IMG_M = 1024
CAP = 2
LAYERS = 64
N_SLAB = 8
X_CHIPS = 4
Z_CHIPS = 16
FIRST_X = 2
FIRST_SLAB = 4
TILE_Z = 9
IMAGE_Z = 8
SUB = 32
SLOTS = LAYERS * CAP
LANES = 128
SENT = 4 * CAP + 1
PEERS = X_CHIPS * N_SLAB
PAIRS = RB // 2
NARROW = math.sqrt(0.5 / math.log(2.0))


kernel_width = 1.0
cell_size = 2.4e-05
w_reach = 20000.0

f32 = jnp.float32
bf16 = jnp.bfloat16
VMEM = pl.BlockSpec(memory_space=pltpu.VMEM)
HBM = pl.BlockSpec(memory_space=pltpu.HBM)
NT = (((1,), (1,)), ((), ()))
NN = (((1,), (0,)), ((), ()))


def wave(turns, period):
    angle = 2.0 * np.pi * (np.asarray(turns) % period) / period
    return np.cos(angle), np.sin(angle)


def np_split(table):
    table = np.asarray(table, np.float32)
    upper = table.astype(ml_dtypes.bfloat16)
    return upper, (table - upper.astype(np.float32)).astype(ml_dtypes.bfloat16)


def split(value):
    upper = value.astype(bf16)
    return upper, (value - upper.astype(f32)).astype(bf16)


def dot(left, right, dims):
    return lax.dot_general(left, right, dims, preferred_element_type=f32)


def route_kernel(*refs):
    given, out_ref, held, (count_ref, sems) = refs[:5], refs[5], refs[6:11], refs[11:]
    layer_ref, block_ref, vis_ref, row_ref, col_ref = held
    copies = [
        pltpu.make_async_copy(source, target, sems.at[index])
        for index, (source, target) in enumerate(zip(given, held))
    ]
    for copy in copies:
        copy.start()
    out_ref[...] = jnp.zeros_like(out_ref)

    def clear(layer, carry):
        count_ref[layer] = 0
        return carry

    lax.fori_loop(0, LAYERS, clear, 0, unroll=16)
    for copy in copies:
        copy.wait()
    part = lax.broadcasted_iota(jnp.int32, (1, LANES), 1) // (LANES // CAP)

    def place(tile, carry):
        layer = layer_ref[tile]
        slot = count_ref[layer]
        count_ref[layer] = slot + 1
        start = layer * SENT + slot * 4
        out_ref[pl.ds(start, 2), :] = vis_ref[pl.ds(2 * tile, 2), :]
        out_ref[pl.ds(start + 2, 1), :] = row_ref[pl.ds(tile, 1), :] * NARROW
        out_ref[pl.ds(start + 3, 1), :] = col_ref[pl.ds(tile, 1), :] * NARROW
        named = out_ref.at[pl.ds(layer * SENT + 4 * CAP, 1), :]
        block = jnp.full((1, LANES), block_ref[tile], jnp.int32).astype(f32)
        pltpu.store(named, block, mask=part == slot)
        return carry

    lax.fori_loop(0, layer_ref.shape[0], place, 0, unroll=16)


def turn_by(value, step, period):
    real, imag = value
    step = step % period
    if 4 * step % period == 0:
        quarter = 4 * step // period
        return [(real, imag), (-imag, real), (-real, -imag), (imag, -real)][quarter]
    angle = 2.0 * math.pi * step / period
    cos_part, sin_part = math.cos(angle), math.sin(angle)
    return real * cos_part - imag * sin_part, real * sin_part + imag * cos_part


def dft(values):
    count = len(values)
    if count == 1:
        return values
    even, odd = dft(values[::2]), dft(values[1::2])
    odd = [turn_by(value, index, count) for index, value in enumerate(odd)]
    return [(a[0] + b[0], a[1] + b[1]) for a, b in zip(even, odd)] + [
        (a[0] - b[0], a[1] - b[1]) for a, b in zip(even, odd)
    ]


def grid_kernel(
    got_ref, twist_ref, last_ref, out_ref, grid_ref, upper_ref, lower_ref, name_ref, block_ref, sem
):
    named = got_ref[pl.ds(4 * CAP, LAYERS, stride=SENT), :]
    source = lax.broadcasted_iota(jnp.int32, (LAYERS, SLOTS), 0)
    lane = lax.broadcasted_iota(jnp.int32, (LAYERS, SLOTS), 1)
    name_ref[...] = jnp.sum(
        jnp.where(source == jnp.bitwise_and(lane, LAYERS - 1), named, 0.0), 0, keepdims=True
    ).astype(jnp.int32)
    copy = pltpu.make_async_copy(name_ref, block_ref, sem)
    copy.start()
    grid_ref[...] = jnp.zeros_like(grid_ref)
    rows = (lax.broadcasted_iota(jnp.int32, (RB, VIS), 0).astype(f32) + 0.5) * NARROW
    cols = (lax.broadcasted_iota(jnp.int32, (CB, VIS), 0).astype(f32) + 0.5) * NARROW
    copy.wait()

    def one(source, slot):
        start = source * SENT + 4 * slot
        real = got_ref[pl.ds(start, 1), :]
        imag = got_ref[pl.ds(start + 1, 1), :]
        away = rows - got_ref[pl.ds(start + 2, 1), :]
        near = jnp.exp2(-(away * away))
        upper, lower = split(jnp.concatenate([near * real, near * imag], 0))
        away = cols - got_ref[pl.ds(start + 3, 1), :]
        col_upper, col_lower = split(jnp.exp2(-(away * away)))
        left = jnp.concatenate([upper, lower, upper], 1)
        right = jnp.concatenate([col_upper, col_upper, col_lower], 1)
        grid_ref[block_ref[0, slot * LAYERS + source]] += dot(left, right, NT)

    together = 16

    def some(step, carry):
        for part in range(together):
            for slot in range(CAP):
                one(step * together + part, slot)
        return carry

    lax.fori_loop(0, LAYERS // together, some, 0)

    wide, narrow = 8, SUB // 8
    for second in range(2):
        for low in range(wide):
            at = [second * SUB + low + wide * high for high in range(narrow)]
            turned = dft([(grid_ref[k, :RB, :], grid_ref[k, RB:, :]) for k in at])
            for index, k in enumerate(at):
                real, imag = turn_by(turned[index], index * low, SUB)
                grid_ref[k, :RB, :] = real
                grid_ref[k, RB:, :] = imag
        for low in range(narrow):
            at = [second * SUB + wide * low + high for high in range(wide)]
            turned = dft([(grid_ref[k, :RB, :], grid_ref[k, RB:, :]) for k in at])
            for index, (real, imag) in enumerate(turned):
                q = low + narrow * index
                cos_part = twist_ref[q : q + 1, :]
                sin_part = twist_ref[SUB + q : SUB + q + 1, :]
                upper, lower = split(
                    jnp.concatenate(
                        [real * cos_part - imag * sin_part, real * sin_part + imag * cos_part], 1
                    )
                )
                place = (second * SUB + q) * RB
                upper_ref[place : place + RB, :] = upper
                lower_ref[place : place + RB, :] = lower

    last_both = last_ref[...]
    last_upper = last_both[: 2 * SUB]
    for pair in range(PAIRS // 2):
        piece = slice(pair * 2 * LANES, (pair + 1) * 2 * LANES)
        both = dot(last_both, upper_ref[piece, :], NT)
        wave_sum = both[: 2 * SUB] + both[2 * SUB :] + dot(last_upper, lower_ref[piece, :], NT)
        for half in range(2):
            for part in range(2):
                row = 2 * (2 * pair + half) + part
                out_ref[pl.ds(row, PEERS, stride=2 * PAIRS), :] = wave_sum[
                    part * PEERS : (part + 1) * PEERS, half * LANES : (half + 1) * LANES
                ]


def swap_blocks(value):
    line = lax.broadcasted_iota(jnp.int32, value.shape, 0)
    block = lax.broadcasted_iota(jnp.int32, value.shape, 1) // RB
    for step in (4, 2, 1):
        line_bit = jnp.bitwise_and(line, step) != 0
        block_bit = jnp.bitwise_and(block, step) != 0
        up = pltpu.roll(pltpu.roll(value, 8 - step, 0), RB * step, 1)
        down = pltpu.roll(pltpu.roll(value, step, 0), LANES - RB * step, 1)
        moved = jnp.where(line_bit, down, up)
        value = jnp.where(line_bit == block_bit, value, moved)
    return value


def image_kernel(got_ref, upper_ref, lower_ref, cos_ref, sin_ref, out_ref, right_ref):
    blocks = SUB // N_SLAB
    for layer in range(X_CHIPS):
        for pair in range(blocks // 2):
            lines = []
            for high in (2 * pair, 2 * pair + 1):
                parts = []
                for y in range(2):
                    for h in range(2):
                        step = 2 * (h * blocks + high) + y
                        row = layer * N_SLAB * 2 * PAIRS + step
                        parts.append(
                            swap_blocks(got_ref[pl.ds(row, N_SLAB, stride=2 * PAIRS), :])
                        )
                lines.append(jnp.concatenate(parts, 1))
            upper, lower = split(jnp.concatenate(lines, 0))
            row = layer * SUB + pair * 2 * N_SLAB
            right_ref[row : row + 2 * N_SLAB, :] = upper
            right_ref[LANES + row : LANES + row + 2 * N_SLAB, :] = lower
    count = IMG_L // X_CHIPS
    group = lax.broadcasted_iota(jnp.int32, (count, LANES), 1) // SUB
    right = right_ref[...]
    total = None
    for part in range(X_CHIPS):
        rows = pl.ds(part * 2 * count, 2 * count)
        both = dot(upper_ref[rows, :], right, NT)
        wave_sum = both[:, :LANES] + both[:, LANES:] + dot(lower_ref[rows, :], right[:LANES], NT)
        lines = pl.ds(part * count, count)
        screened = wave_sum[:count] * cos_ref[lines, :] - wave_sum[count:] * sin_ref[lines, :]
        screened = screened + pltpu.roll(screened, 2 * SUB, 1)
        screened = screened + pltpu.roll(screened, SUB, 1)
        total = screened if total is None else jnp.where(group == part, screened, total)
    out_ref[...] = total


def sum_kernel(got_ref, out_ref):
    line = lax.broadcasted_iota(jnp.int32, (8, LANES), 0)
    group = lax.broadcasted_iota(jnp.int32, (8, LANES), 1) // SUB
    straight = (line // 4) == jnp.bitwise_and(line, 1)
    result = jnp.zeros((8, LANES), f32)
    for place in range(X_CHIPS):
        chip = (place + FIRST_X) % X_CHIPS
        total = got_ref[pl.ds(place * 2 * Z_CHIPS, 8), :]
        for step in range(1, 2 * Z_CHIPS // 8):
            total = total + got_ref[pl.ds(place * 2 * Z_CHIPS + 8 * step, 8), :]
        total = total + pltpu.roll(total, 4, 0)
        total = total + pltpu.roll(total, 2, 0)
        total = jnp.where(straight, total, pltpu.roll(total, 1, 0))
        for part in range(X_CHIPS):
            shift = (chip - part) % X_CHIPS
            moved = pltpu.roll(total, SUB * shift, 1) if shift else total
            chosen = (group == chip) & (jnp.bitwise_and(line, 3) == part)
            result = jnp.where(chosen, moved, result)
    out_ref[...] = result


def call(kernel, shape, specs, scratch, flops, moved, limit=24, out=jax.ShapeDtypeStruct):
    return pl.pallas_call(
        kernel,
        out_shape=out(shape, f32),
        in_specs=specs,
        out_specs=VMEM,
        scratch_shapes=scratch,
        compiler_params=pltpu.CompilerParams(vmem_limit_bytes=limit * 1024 * 1024),
        cost_estimate=pl.CostEstimate(flops=flops, bytes_accessed=moved, transcendentals=0),
    )


def grid_tables():
    q = np.arange(SUB)
    c = np.arange(CB)
    sign = (1 - 2 * (q % 2))[:, None]
    twist = np.concatenate([part * sign for part in wave(q[:, None] * c[None, :], NG)], 0)
    x, slab = np.divmod(column_members(), N_SLAB)
    n = 4 * slab + x
    cos_part, sin_part = wave((n[:, None] - SUB // 2) * c[None, :], CB)
    last = np.concatenate(
        [
            np.concatenate([cos_part, -sin_part], 1),
            np.concatenate([sin_part, cos_part], 1),
        ],
        0,
    )
    return twist.astype(np.float32), np.concatenate(np_split(last), 0)


def rotated(slow, fast, first_slow, first_fast):
    i, j = np.meshgrid(np.arange(slow), np.arange(fast), indexing="ij")
    return ((i + first_slow) % slow * fast + (j + first_fast) % fast).reshape(-1)


def layer_members():
    return rotated(X_CHIPS, Z_CHIPS, FIRST_X, TILE_Z)


def column_members():
    return rotated(X_CHIPS, N_SLAB, FIRST_X, FIRST_SLAB)


def image_members():
    return rotated(X_CHIPS, Z_CHIPS, FIRST_X, IMAGE_Z)


def exchange(value, axes, members):
    groups = [[int(member) for member in members]]
    return lax.all_to_all(
        value, axes, split_axis=0, concat_axis=0, tiled=True, axis_index_groups=groups
    )


def image_lines():
    part, chip, half = np.meshgrid(
        np.arange(4), image_members(), np.arange(2), indexing="ij"
    )
    return (8 * chip + 4 * half + part).reshape(-1) - IMG_L // 2


def image_tables(spread):
    y, h, slab, r = np.meshgrid(
        np.arange(2), np.arange(2), np.arange(N_SLAB), np.arange(RB), indexing="ij"
    )
    slab = (slab + FIRST_SLAB) % N_SLAB
    row = (slab * ROWS_DEV + h * RB + r).reshape(-1) - ROWS_DEV * N_SLAB // 2
    y = y.reshape(-1)[None, :]
    cos_part, sin_part = wave(image_lines()[:, None] * row[None, :], NG)
    real = np.where(y == 0, cos_part, -sin_part).reshape(4, -1, row.size)
    imag = np.where(y == 0, sin_part, cos_part).reshape(4, -1, row.size)
    return np_split(np.concatenate([real, imag], 1).reshape(2 * IMG_L, row.size) * spread)


def screen_tables():
    columns = IMG_M // N_SLAB
    lines = jnp.asarray(image_lines().astype(np.float32))
    lane = jnp.arange(LANES, dtype=jnp.int32)
    m_index = (
        lax.axis_index("slab") * columns
        + lax.axis_index("x") * SUB
        + jnp.bitwise_and(lane, SUB - 1)
        - IMG_M // 2
    )
    place = (lax.axis_index("z") + Z_CHIPS - TILE_Z) % Z_CHIPS
    layer = ((lane // SUB) * Z_CHIPS + place).astype(f32)
    w_value = w_reach * (2.0 * layer + 1.0 - LAYERS) / LAYERS
    l_direction = lines[:, None] * cell_size
    m_direction = m_index.astype(f32)[None, :] * cell_size
    radius = l_direction * l_direction + m_direction * m_direction
    n_lift = -radius / (1.0 + jnp.sqrt(1.0 - radius))
    phase_angle = -2.0 * math.pi * w_value[None, :] * n_lift
    return jnp.cos(phase_angle), jnp.sin(phase_angle)


def body(visibilities, row_offset, col_offset, w_layer, grid_block):
    tiles = w_layer.shape[0]
    spread = 1.0 / (
        2.0 * math.pi * kernel_width**2 * math.sqrt(tiles * LAYERS * N_SLAB * VIS)
    )
    sent = call(
        route_kernel,
        (LAYERS * SENT, VIS),
        [HBM] * 5,
        [
            pltpu.SMEM((tiles,), jnp.int32),
            pltpu.SMEM((tiles,), jnp.int32),
            pltpu.VMEM((2 * tiles, VIS), f32),
            pltpu.VMEM((tiles, VIS), f32),
            pltpu.VMEM((tiles, VIS), f32),
            pltpu.SMEM((LAYERS,), jnp.int32),
            pltpu.SemaphoreType.DMA((5,)),
        ],
        10**6,
        5 * 10**5,
        limit=60,
        out=pltpu.VMEM,
    )(w_layer, grid_block, visibilities.reshape(2 * tiles, VIS), row_offset, col_offset)
    got = exchange(sent.reshape(LAYERS, 1, SENT * VIS), ("x", "z"), layer_members())
    got = got.reshape(LAYERS * SENT, VIS)
    cos_screen, sin_screen = screen_tables()
    twist, last = grid_tables()
    pieces = call(
        grid_kernel,
        (PEERS * 2 * PAIRS, LANES),
        [VMEM] * 3,
        [
            pltpu.VMEM((2 * SUB, 2 * RB, CB), f32),
            pltpu.VMEM((2 * SUB * RB, 2 * CB), bf16),
            pltpu.VMEM((2 * SUB * RB, 2 * CB), bf16),
            pltpu.VMEM((1, SLOTS), jnp.int32),
            pltpu.SMEM((1, SLOTS), jnp.int32),
            pltpu.SemaphoreType.DMA,
        ],
        10**9,
        10**6,
        out=pltpu.VMEM,
    )(got, jnp.asarray(twist), jnp.asarray(last))
    turned = exchange(
        pieces.reshape(PEERS, 2 * PAIRS, LANES), ("x", "slab"), column_members()
    ).reshape(PEERS * 2 * PAIRS, LANES)
    upper, lower = image_tables(spread)
    shares = call(
        image_kernel,
        (2 * LAYERS, LANES),
        [VMEM] * 5,
        [pltpu.VMEM((2 * LANES, 2 * ROWS_DEV * N_SLAB), bf16)],
        10**9,
        3 * 10**6,
    )(turned, jnp.asarray(upper), jnp.asarray(lower), cos_screen, sin_screen)
    got = exchange(shares.reshape(LAYERS, 2, LANES), ("x", "z"), image_members())
    got = got.reshape(2 * LAYERS, LANES)
    return call(sum_kernel, (8, LANES), [VMEM], [], 10**5, 7 * 10**4)(got)


def solution(mesh):
    whole = ("x", "z", "slab")
    chips = Mesh(mesh.devices.reshape(X_CHIPS, Z_CHIPS, N_SLAB), whole)
    placed = (P(whole, None, None), P(whole, None), P(whole, None), P(whole), P(whole))
    return jax.shard_map(
        body, mesh=chips, in_specs=placed, out_specs=P(("x", "z"), "slab"), check_vma=False
    )
```

```python
import math

import ml_dtypes
import numpy as np

import jax
import jax.numpy as jnp
from jax import lax
from jax.experimental import pallas as pl
from jax.experimental.pallas import tpu as pltpu
from jax.sharding import Mesh
from jax.sharding import PartitionSpec as P

NG = 4096
VIS = 128
RB = 16
CB = 128
ROWS_DEV = 32
IMG_L = 512
IMG_M = 1024
CAP = 2
LAYERS = 64
N_SLAB = 8
X_CHIPS = 4
Z_CHIPS = 16
FIRST_X = 2
FIRST_SLAB = 4
TILE_Z = 9
IMAGE_Z = 8
SUB = 32
SLOTS = LAYERS * CAP
LANES = 128
SENT = 4 * CAP + 1
PEERS = X_CHIPS * N_SLAB
PAIRS = RB // 2
NARROW = math.sqrt(0.5 / math.log(2.0))


kernel_width = 1.0
cell_size = 2.4e-05
w_reach = 20000.0

f32 = jnp.float32
bf16 = jnp.bfloat16
VMEM = pl.BlockSpec(memory_space=pltpu.VMEM)
HBM = pl.BlockSpec(memory_space=pltpu.HBM)
NT = (((1,), (1,)), ((), ()))
NN = (((1,), (0,)), ((), ()))


def wave(turns, period):
    angle = 2.0 * np.pi * (np.asarray(turns) % period) / period
    return np.cos(angle), np.sin(angle)


def np_split(table):
    table = np.asarray(table, np.float32)
    upper = table.astype(ml_dtypes.bfloat16)
    return upper, (table - upper.astype(np.float32)).astype(ml_dtypes.bfloat16)


def split(value):
    upper = value.astype(bf16)
    return upper, (value - upper.astype(f32)).astype(bf16)


def dot(left, right, dims):
    return lax.dot_general(left, right, dims, preferred_element_type=f32)


def route_kernel(*refs):
    given, out_ref, held, (count_ref, sems) = refs[:5], refs[5], refs[6:11], refs[11:]
    layer_ref, block_ref, vis_ref, row_ref, col_ref = held
    copies = [
        pltpu.make_async_copy(source, target, sems.at[index])
        for index, (source, target) in enumerate(zip(given, held))
    ]
    for copy in copies:
        copy.start()
    out_ref[...] = jnp.zeros_like(out_ref)

    def clear(layer, carry):
        count_ref[layer] = 0
        return carry

    lax.fori_loop(0, LAYERS, clear, 0, unroll=16)
    for copy in copies:
        copy.wait()
    part = lax.broadcasted_iota(jnp.int32, (1, LANES), 1) // (LANES // CAP)

    def place(tile, carry):
        layer = layer_ref[tile]
        slot = count_ref[layer]
        count_ref[layer] = slot + 1
        start = layer * SENT + slot * 4
        out_ref[pl.ds(start, 2), :] = vis_ref[pl.ds(2 * tile, 2), :]
        out_ref[pl.ds(start + 2, 1), :] = row_ref[pl.ds(tile, 1), :]
        out_ref[pl.ds(start + 3, 1), :] = col_ref[pl.ds(tile, 1), :]
        named = out_ref.at[pl.ds(layer * SENT + 4 * CAP, 1), :]
        block = jnp.full((1, LANES), block_ref[tile], jnp.int32).astype(f32)
        pltpu.store(named, block, mask=part == slot)
        return carry

    lax.fori_loop(0, layer_ref.shape[0], place, 0, unroll=16)


def turn_by(value, step, period):
    real, imag = value
    step = step % period
    if 4 * step % period == 0:
        quarter = 4 * step // period
        return [(real, imag), (-imag, real), (-real, -imag), (imag, -real)][quarter]
    angle = 2.0 * math.pi * step / period
    cos_part, sin_part = math.cos(angle), math.sin(angle)
    return real * cos_part - imag * sin_part, real * sin_part + imag * cos_part


def dft(values):
    count = len(values)
    if count == 1:
        return values
    even, odd = dft(values[::2]), dft(values[1::2])
    odd = [turn_by(value, index, count) for index, value in enumerate(odd)]
    return [(a[0] + b[0], a[1] + b[1]) for a, b in zip(even, odd)] + [
        (a[0] - b[0], a[1] - b[1]) for a, b in zip(even, odd)
    ]


def grid_kernel(
    got_ref, twist_ref, last_ref, out_ref, grid_ref, upper_ref, lower_ref, name_ref, block_ref, sem
):
    named = got_ref[pl.ds(4 * CAP, LAYERS, stride=SENT), :]
    source = lax.broadcasted_iota(jnp.int32, (LAYERS, SLOTS), 0)
    lane = lax.broadcasted_iota(jnp.int32, (LAYERS, SLOTS), 1)
    name_ref[...] = jnp.sum(
        jnp.where(source == jnp.bitwise_and(lane, LAYERS - 1), named, 0.0), 0, keepdims=True
    ).astype(jnp.int32)
    copy = pltpu.make_async_copy(name_ref, block_ref, sem)
    copy.start()
    grid_ref[...] = jnp.zeros_like(grid_ref)
    offsets = jnp.concatenate(
        [got_ref[pl.ds(4 * slot + 3, LAYERS, stride=SENT), :] for slot in range(CAP)], 0
    ).T * NARROW
    rows = (lax.broadcasted_iota(jnp.int32, (RB, VIS), 0).astype(f32) + 0.5) * NARROW
    cols = (lax.broadcasted_iota(jnp.int32, (VIS, CB), 1).astype(f32) + 0.5) * NARROW
    copy.wait()

    def one(source, slot, center):
        start = source * SENT + 4 * slot
        real = got_ref[pl.ds(start, 1), :]
        imag = got_ref[pl.ds(start + 1, 1), :]
        away = rows - got_ref[pl.ds(start + 2, 1), :] * NARROW
        near = jnp.exp2(-(away * away))
        upper, lower = split(jnp.concatenate([near * real, near * imag], 0))
        away = cols - center
        col_upper, col_lower = split(jnp.exp2(-(away * away)))
        left = jnp.concatenate([upper, lower], 0)
        both = dot(left, jnp.concatenate([col_upper, col_lower], 1), NN)
        patch = both[:, :CB] + both[:, CB:]
        grid_ref[block_ref[0, slot * LAYERS + source]] += patch[: 2 * RB] + patch[2 * RB :]

    together = 16

    def some(step, held):
        for part in range(together):
            for slot in range(CAP):
                lane = slot * LAYERS + part
                one(step * together + part, slot, held[:, lane : lane + 1])
        return pltpu.roll(held, SLOTS - together, 1)

    lax.fori_loop(0, LAYERS // together, some, offsets)

    wide, narrow = 8, SUB // 8
    for second in range(2):
        for low in range(wide):
            at = [second * SUB + low + wide * high for high in range(narrow)]
            turned = dft([(grid_ref[k, :RB, :], grid_ref[k, RB:, :]) for k in at])
            for index, k in enumerate(at):
                real, imag = turn_by(turned[index], index * low, SUB)
                grid_ref[k, :RB, :] = real
                grid_ref[k, RB:, :] = imag
        for low in range(narrow):
            at = [second * SUB + wide * low + high for high in range(wide)]
            turned = dft([(grid_ref[k, :RB, :], grid_ref[k, RB:, :]) for k in at])
            for index, (real, imag) in enumerate(turned):
                q = low + narrow * index
                cos_part = twist_ref[q : q + 1, :]
                sin_part = twist_ref[SUB + q : SUB + q + 1, :]
                upper, lower = split(
                    jnp.concatenate(
                        [real * cos_part - imag * sin_part, real * sin_part + imag * cos_part], 1
                    )
                )
                place = (second * SUB + q) * RB
                upper_ref[place : place + RB, :] = upper
                lower_ref[place : place + RB, :] = lower

    last_both = last_ref[...]
    last_upper = last_both[: 2 * SUB]
    for pair in range(PAIRS // 2):
        piece = slice(pair * 2 * LANES, (pair + 1) * 2 * LANES)
        both = dot(last_both, upper_ref[piece, :], NT)
        wave_sum = both[: 2 * SUB] + both[2 * SUB :] + dot(last_upper, lower_ref[piece, :], NT)
        for half in range(2):
            for part in range(2):
                row = 2 * (2 * pair + half) + part
                out_ref[pl.ds(row, PEERS, stride=2 * PAIRS), :] = wave_sum[
                    part * PEERS : (part + 1) * PEERS, half * LANES : (half + 1) * LANES
                ]


def swap_blocks(value):
    line = lax.broadcasted_iota(jnp.int32, value.shape, 0)
    block = lax.broadcasted_iota(jnp.int32, value.shape, 1) // RB
    for step in (4, 2, 1):
        line_bit = jnp.bitwise_and(line, step) != 0
        block_bit = jnp.bitwise_and(block, step) != 0
        up = pltpu.roll(pltpu.roll(value, 8 - step, 0), RB * step, 1)
        down = pltpu.roll(pltpu.roll(value, step, 0), LANES - RB * step, 1)
        moved = jnp.where(line_bit, down, up)
        value = jnp.where(line_bit == block_bit, value, moved)
    return value


def image_kernel(got_ref, upper_ref, lower_ref, cos_ref, sin_ref, out_ref, right_ref):
    blocks = SUB // N_SLAB
    for layer in range(X_CHIPS):
        for pair in range(blocks // 2):
            lines = []
            for high in (2 * pair, 2 * pair + 1):
                parts = []
                for y in range(2):
                    for h in range(2):
                        step = 2 * (h * blocks + high) + y
                        row = layer * N_SLAB * 2 * PAIRS + step
                        parts.append(
                            swap_blocks(got_ref[pl.ds(row, N_SLAB, stride=2 * PAIRS), :])
                        )
                lines.append(jnp.concatenate(parts, 1))
            upper, lower = split(jnp.concatenate(lines, 0))
            row = layer * SUB + pair * 2 * N_SLAB
            right_ref[row : row + 2 * N_SLAB, :] = upper
            right_ref[LANES + row : LANES + row + 2 * N_SLAB, :] = lower
    count = IMG_L // X_CHIPS
    group = lax.broadcasted_iota(jnp.int32, (count, LANES), 1) // SUB
    right = right_ref[...]
    total = None
    for part in range(X_CHIPS):
        rows = pl.ds(part * 2 * count, 2 * count)
        both = dot(upper_ref[rows, :], right, NT)
        wave_sum = both[:, :LANES] + both[:, LANES:] + dot(lower_ref[rows, :], right[:LANES], NT)
        lines = pl.ds(part * count, count)
        screened = wave_sum[:count] * cos_ref[lines, :] - wave_sum[count:] * sin_ref[lines, :]
        screened = screened + pltpu.roll(screened, 2 * SUB, 1)
        screened = screened + pltpu.roll(screened, SUB, 1)
        total = screened if total is None else jnp.where(group == part, screened, total)
    out_ref[...] = total


def sum_kernel(got_ref, out_ref):
    line = lax.broadcasted_iota(jnp.int32, (8, LANES), 0)
    group = lax.broadcasted_iota(jnp.int32, (8, LANES), 1) // SUB
    parts = [got_ref[8 * step : 8 * step + 8, :] for step in range(Z_CHIPS)]
    while len(parts) > 1:
        parts = [a + b for a, b in zip(parts[::2], parts[1::2])]
    result = jnp.zeros((8, LANES), f32)
    for place in range(X_CHIPS):
        chip = (place + FIRST_X) % X_CHIPS
        total = jnp.where(
            line < 4, parts[0][2 * place : 2 * place + 1], parts[0][2 * place + 1 : 2 * place + 2]
        )
        for part in range(X_CHIPS):
            shift = (chip - part) % X_CHIPS
            moved = pltpu.roll(total, SUB * shift, 1) if shift else total
            chosen = (group == chip) & (jnp.bitwise_and(line, 3) == part)
            result = jnp.where(chosen, moved, result)
    out_ref[...] = result


def call(kernel, shape, specs, scratch, flops, moved, limit=24):
    return pl.pallas_call(
        kernel,
        out_shape=jax.ShapeDtypeStruct(shape, f32),
        in_specs=specs,
        out_specs=VMEM,
        scratch_shapes=scratch,
        compiler_params=pltpu.CompilerParams(vmem_limit_bytes=limit * 1024 * 1024),
        cost_estimate=pl.CostEstimate(flops=flops, bytes_accessed=moved, transcendentals=0),
    )


def grid_tables():
    q = np.arange(SUB)
    c = np.arange(CB)
    sign = (1 - 2 * (q % 2))[:, None]
    twist = np.concatenate([part * sign for part in wave(q[:, None] * c[None, :], NG)], 0)
    x, slab = np.divmod(column_members(), N_SLAB)
    n = 4 * slab + x
    cos_part, sin_part = wave((n[:, None] - SUB // 2) * c[None, :], CB)
    last = np.concatenate(
        [
            np.concatenate([cos_part, -sin_part], 1),
            np.concatenate([sin_part, cos_part], 1),
        ],
        0,
    )
    return twist.astype(np.float32), np.concatenate(np_split(last), 0)


def rotated(slow, fast, first_slow, first_fast):
    i, j = np.meshgrid(np.arange(slow), np.arange(fast), indexing="ij")
    return ((i + first_slow) % slow * fast + (j + first_fast) % fast).reshape(-1)


def far_members(first_z):
    z, x = np.meshgrid(np.arange(Z_CHIPS), np.arange(X_CHIPS), indexing="ij")
    return ((x + FIRST_X) % X_CHIPS * Z_CHIPS + (z + first_z) % Z_CHIPS).reshape(-1)


def layer_members():
    return far_members(TILE_Z)


def column_members():
    return rotated(X_CHIPS, N_SLAB, FIRST_X, FIRST_SLAB)


def image_members():
    return far_members(IMAGE_Z)


def exchange(value, axes, members):
    groups = [[int(member) for member in members]]
    return lax.all_to_all(
        value, axes, split_axis=0, concat_axis=0, tiled=True, axis_index_groups=groups
    )


def image_lines():
    part, chip, half = np.meshgrid(
        np.arange(4), image_members(), np.arange(2), indexing="ij"
    )
    return (8 * chip + 4 * half + part).reshape(-1) - IMG_L // 2


def image_tables(spread):
    y, h, slab, r = np.meshgrid(
        np.arange(2), np.arange(2), np.arange(N_SLAB), np.arange(RB), indexing="ij"
    )
    slab = (slab + FIRST_SLAB) % N_SLAB
    row = (slab * ROWS_DEV + h * RB + r).reshape(-1) - ROWS_DEV * N_SLAB // 2
    y = y.reshape(-1)[None, :]
    cos_part, sin_part = wave(image_lines()[:, None] * row[None, :], NG)
    real = np.where(y == 0, cos_part, -sin_part).reshape(4, -1, row.size)
    imag = np.where(y == 0, sin_part, cos_part).reshape(4, -1, row.size)
    return np_split(np.concatenate([real, imag], 1).reshape(2 * IMG_L, row.size) * spread)


def screen_tables():
    columns = IMG_M // N_SLAB
    lines = jnp.asarray(image_lines().astype(np.float32))
    lane = jnp.arange(LANES, dtype=jnp.int32)
    m_index = (
        lax.axis_index("slab") * columns
        + lax.axis_index("x") * SUB
        + jnp.bitwise_and(lane, SUB - 1)
        - IMG_M // 2
    )
    place = (lax.axis_index("z") + Z_CHIPS - TILE_Z) % Z_CHIPS
    layer = (place * X_CHIPS + lane // SUB).astype(f32)
    w_value = w_reach * (2.0 * layer + 1.0 - LAYERS) / LAYERS
    l_direction = lines[:, None] * cell_size
    m_direction = m_index.astype(f32)[None, :] * cell_size
    radius = l_direction * l_direction + m_direction * m_direction
    n_lift = -radius / (1.0 + jnp.sqrt(1.0 - radius))
    phase_angle = -2.0 * math.pi * w_value[None, :] * n_lift
    return jnp.cos(phase_angle), jnp.sin(phase_angle)


def body(visibilities, row_offset, col_offset, w_layer, grid_block):
    tiles = w_layer.shape[0]
    spread = 1.0 / (
        2.0 * math.pi * kernel_width**2 * math.sqrt(tiles * LAYERS * N_SLAB * VIS)
    )
    sent = call(
        route_kernel,
        (LAYERS * SENT, VIS),
        [HBM] * 5,
        [
            pltpu.SMEM((tiles,), jnp.int32),
            pltpu.SMEM((tiles,), jnp.int32),
            pltpu.VMEM((2 * tiles, VIS), f32),
            pltpu.VMEM((tiles, VIS), f32),
            pltpu.VMEM((tiles, VIS), f32),
            pltpu.SMEM((LAYERS,), jnp.int32),
            pltpu.SemaphoreType.DMA((5,)),
        ],
        10**6,
        5 * 10**5,
        limit=60,
    )(w_layer, grid_block, visibilities.reshape(2 * tiles, VIS), row_offset, col_offset)
    got = exchange(sent.reshape(LAYERS, 1, SENT * VIS), ("x", "z"), layer_members())
    got = got.reshape(LAYERS * SENT, VIS)
    cos_screen, sin_screen = screen_tables()
    twist, last = grid_tables()
    pieces = call(
        grid_kernel,
        (PEERS * 2 * PAIRS, LANES),
        [VMEM] * 3,
        [
            pltpu.VMEM((2 * SUB, 2 * RB, CB), f32),
            pltpu.VMEM((2 * SUB * RB, 2 * CB), bf16),
            pltpu.VMEM((2 * SUB * RB, 2 * CB), bf16),
            pltpu.VMEM((1, SLOTS), jnp.int32),
            pltpu.SMEM((1, SLOTS), jnp.int32),
            pltpu.SemaphoreType.DMA,
        ],
        10**9,
        10**6,
    )(got, jnp.asarray(twist), jnp.asarray(last))
    turned = exchange(
        pieces.reshape(PEERS, 2 * PAIRS, LANES), ("x", "slab"), column_members()
    ).reshape(PEERS * 2 * PAIRS, LANES)
    upper, lower = image_tables(spread)
    shares = call(
        image_kernel,
        (2 * LAYERS, LANES),
        [VMEM] * 5,
        [pltpu.VMEM((2 * LANES, 2 * ROWS_DEV * N_SLAB), bf16)],
        10**9,
        3 * 10**6,
    )(turned, jnp.asarray(upper), jnp.asarray(lower), cos_screen, sin_screen)
    got = exchange(shares.reshape(LAYERS, 2, LANES), ("x", "z"), image_members())
    got = got.reshape(2 * LAYERS, LANES)
    return call(sum_kernel, (8, LANES), [VMEM], [], 10**5, 7 * 10**4)(got)


def solution(mesh):
    whole = ("x", "z", "slab")
    chips = Mesh(mesh.devices.reshape(X_CHIPS, Z_CHIPS, N_SLAB), whole)
    placed = (P(whole, None, None), P(whole, None), P(whole, None), P(whole), P(whole))
    return jax.shard_map(
        body, mesh=chips, in_specs=placed, out_specs=P(("x", "z"), "slab"), check_vma=False
    )
```

```python
import math

import ml_dtypes
import numpy as np

import jax
import jax.numpy as jnp
from jax import lax
from jax.experimental import pallas as pl
from jax.experimental.pallas import tpu as pltpu
from jax.sharding import Mesh
from jax.sharding import PartitionSpec as P

NG = 4096
VIS = 128
RB = 16
CB = 128
ROWS_DEV = 32
IMG_L = 512
IMG_M = 1024
CAP = 2
LAYERS = 64
N_SLAB = 8
X_CHIPS = 4
Z_CHIPS = 16
FIRST_X = 2
FIRST_SLAB = 4
TILE_Z = 9
IMAGE_Z = 8
SUB = 32
SLOTS = LAYERS * CAP
LANES = 128
SENT = 4 * CAP + 1
PEERS = X_CHIPS * N_SLAB
PAIRS = RB // 2
EARLY = 8
NARROW = math.sqrt(0.5 / math.log(2.0))


kernel_width = 1.0
cell_size = 2.4e-05
w_reach = 20000.0

f32 = jnp.float32
bf16 = jnp.bfloat16
VMEM = pl.BlockSpec(memory_space=pltpu.VMEM)
HBM = pl.BlockSpec(memory_space=pltpu.HBM)
NT = (((1,), (1,)), ((), ()))
NN = (((1,), (0,)), ((), ()))


def wave(turns, period):
    angle = 2.0 * np.pi * (np.asarray(turns) % period) / period
    return np.cos(angle), np.sin(angle)


def np_split(table):
    table = np.asarray(table, np.float32)
    upper = table.astype(ml_dtypes.bfloat16)
    return upper, (table - upper.astype(np.float32)).astype(ml_dtypes.bfloat16)


def split(value):
    upper = value.astype(bf16)
    return upper, (value - upper.astype(f32)).astype(bf16)


def dot(left, right, dims):
    return lax.dot_general(left, right, dims, preferred_element_type=f32)


def route_kernel(*refs):
    given, out_ref, held, (count_ref, sems) = refs[:5], refs[5], refs[6:11], refs[11:]
    layer_ref, block_ref, vis_ref, row_ref, col_ref = held
    copies = [
        pltpu.make_async_copy(source, target, sems.at[index])
        for index, (source, target) in enumerate(zip(given, held))
    ]
    for copy in copies:
        copy.start()
    out_ref[...] = jnp.zeros_like(out_ref)

    def clear(layer, carry):
        count_ref[layer] = 0
        return carry

    lax.fori_loop(0, LAYERS, clear, 0, unroll=16)
    for copy in copies:
        copy.wait()
    part = lax.broadcasted_iota(jnp.int32, (1, LANES), 1) // (LANES // CAP)

    def place(tile, carry):
        layer = layer_ref[tile]
        slot = count_ref[layer]
        count_ref[layer] = slot + 1
        start = layer * SENT + slot * 4
        out_ref[pl.ds(start, 2), :] = vis_ref[pl.ds(2 * tile, 2), :]
        out_ref[pl.ds(start + 2, 1), :] = row_ref[pl.ds(tile, 1), :]
        out_ref[pl.ds(start + 3, 1), :] = col_ref[pl.ds(tile, 1), :]
        named = out_ref.at[pl.ds(layer * SENT + 4 * CAP, 1), :]
        block = jnp.full((1, LANES), block_ref[tile], jnp.int32).astype(f32)
        pltpu.store(named, block, mask=part == slot)
        return carry

    lax.fori_loop(0, layer_ref.shape[0], place, 0, unroll=16)


def turn_by(value, step, period):
    real, imag = value
    step = step % period
    if 4 * step % period == 0:
        quarter = 4 * step // period
        return [(real, imag), (-imag, real), (-real, -imag), (imag, -real)][quarter]
    angle = 2.0 * math.pi * step / period
    cos_part, sin_part = math.cos(angle), math.sin(angle)
    return real * cos_part - imag * sin_part, real * sin_part + imag * cos_part


def dft(values):
    count = len(values)
    if count == 1:
        return values
    even, odd = dft(values[::2]), dft(values[1::2])
    odd = [turn_by(value, index, count) for index, value in enumerate(odd)]
    return [(a[0] + b[0], a[1] + b[1]) for a, b in zip(even, odd)] + [
        (a[0] - b[0], a[1] - b[1]) for a, b in zip(even, odd)
    ]


def grid_kernel(
    got_ref,
    twist_ref,
    last_ref,
    out_ref,
    grid_ref,
    upper_ref,
    lower_ref,
    early_ref,
    name_ref,
    block_ref,
    sem,
):
    named = got_ref[pl.ds(4 * CAP, LAYERS, stride=SENT), :]
    source = lax.broadcasted_iota(jnp.int32, (LAYERS, SLOTS), 0)
    lane = lax.broadcasted_iota(jnp.int32, (LAYERS, SLOTS), 1)
    name_ref[...] = jnp.sum(
        jnp.where(source == jnp.bitwise_and(lane, LAYERS - 1), named, 0.0), 0, keepdims=True
    ).astype(jnp.int32)
    copy = pltpu.make_async_copy(name_ref, block_ref, sem)
    copy.start()
    grid_ref[...] = jnp.zeros_like(grid_ref)
    offsets = jnp.concatenate(
        [got_ref[pl.ds(4 * slot + 3, LAYERS, stride=SENT), :] for slot in range(CAP)], 0
    ).T * NARROW
    rows = (lax.broadcasted_iota(jnp.int32, (RB, VIS), 0).astype(f32) + 0.5) * NARROW
    cols = (lax.broadcasted_iota(jnp.int32, (VIS, CB), 1).astype(f32) + 0.5) * NARROW

    def patch(source, slot, center):
        start = source * SENT + 4 * slot
        real = got_ref[pl.ds(start, 1), :]
        imag = got_ref[pl.ds(start + 1, 1), :]
        away = rows - got_ref[pl.ds(start + 2, 1), :] * NARROW
        near = jnp.exp2(-(away * away))
        upper, lower = split(jnp.concatenate([near * real, near * imag], 0))
        away = cols - center
        col_upper, col_lower = split(jnp.exp2(-(away * away)))
        left = jnp.concatenate([upper, lower], 0)
        both = dot(left, jnp.concatenate([col_upper, col_lower], 1), NN)
        half = both[:, :CB] + both[:, CB:]
        return half[: 2 * RB] + half[2 * RB :]

    early = [(source, slot) for source in range(EARLY) for slot in range(CAP)]
    for index, (source, slot) in enumerate(early):
        lane = slot * LAYERS + source
        early_ref[index] = patch(source, slot, offsets[:, lane : lane + 1])
    copy.wait()
    for index, (source, slot) in enumerate(early):
        grid_ref[block_ref[0, slot * LAYERS + source]] += early_ref[index]

    together = (LAYERS - EARLY) // 2

    def some(step, held):
        for part in range(together):
            for slot in range(CAP):
                source = EARLY + step * together + part
                lane = slot * LAYERS + part
                grid_ref[block_ref[0, slot * LAYERS + source]] += patch(
                    source, slot, held[:, lane : lane + 1]
                )
        return pltpu.roll(held, SLOTS - together, 1)

    lax.fori_loop(0, 2, some, pltpu.roll(offsets, SLOTS - EARLY, 1))

    wide, narrow = 8, SUB // 8
    for second in range(2):
        for low in range(wide):
            at = [second * SUB + low + wide * high for high in range(narrow)]
            turned = dft([(grid_ref[k, :RB, :], grid_ref[k, RB:, :]) for k in at])
            for index, k in enumerate(at):
                real, imag = turn_by(turned[index], index * low, SUB)
                grid_ref[k, :RB, :] = real
                grid_ref[k, RB:, :] = imag
        for low in range(narrow):
            at = [second * SUB + wide * low + high for high in range(wide)]
            turned = dft([(grid_ref[k, :RB, :], grid_ref[k, RB:, :]) for k in at])
            for index, (real, imag) in enumerate(turned):
                q = low + narrow * index
                cos_part = twist_ref[q : q + 1, :]
                sin_part = twist_ref[SUB + q : SUB + q + 1, :]
                upper, lower = split(
                    jnp.concatenate(
                        [real * cos_part - imag * sin_part, real * sin_part + imag * cos_part], 1
                    )
                )
                place = (second * SUB + q) * RB
                upper_ref[place : place + RB, :] = upper
                lower_ref[place : place + RB, :] = lower

    last_both = last_ref[...]
    last_upper = last_both[: 2 * SUB]
    for pair in range(PAIRS // 2):
        piece = slice(pair * 2 * LANES, (pair + 1) * 2 * LANES)
        both = dot(last_both, upper_ref[piece, :], NT)
        wave_sum = both[: 2 * SUB] + both[2 * SUB :] + dot(last_upper, lower_ref[piece, :], NT)
        for half in range(2):
            for part in range(2):
                row = 2 * (2 * pair + half) + part
                out_ref[pl.ds(row, PEERS, stride=2 * PAIRS), :] = wave_sum[
                    part * PEERS : (part + 1) * PEERS, half * LANES : (half + 1) * LANES
                ]


def swap_blocks(value):
    line = lax.broadcasted_iota(jnp.int32, value.shape, 0)
    block = lax.broadcasted_iota(jnp.int32, value.shape, 1) // RB
    for step in (4, 2, 1):
        line_bit = jnp.bitwise_and(line, step) != 0
        block_bit = jnp.bitwise_and(block, step) != 0
        up = pltpu.roll(pltpu.roll(value, 8 - step, 0), RB * step, 1)
        down = pltpu.roll(pltpu.roll(value, step, 0), LANES - RB * step, 1)
        moved = jnp.where(line_bit, down, up)
        value = jnp.where(line_bit == block_bit, value, moved)
    return value


def image_kernel(got_ref, upper_ref, lower_ref, cos_ref, sin_ref, out_ref, right_ref):
    blocks = SUB // N_SLAB
    for layer in range(X_CHIPS):
        for pair in range(blocks // 2):
            lines = []
            for high in (2 * pair, 2 * pair + 1):
                parts = []
                for y in range(2):
                    for h in range(2):
                        step = 2 * (h * blocks + high) + y
                        row = layer * N_SLAB * 2 * PAIRS + step
                        parts.append(
                            swap_blocks(got_ref[pl.ds(row, N_SLAB, stride=2 * PAIRS), :])
                        )
                lines.append(jnp.concatenate(parts, 1))
            upper, lower = split(jnp.concatenate(lines, 0))
            row = layer * SUB + pair * 2 * N_SLAB
            right_ref[row : row + 2 * N_SLAB, :] = upper
            right_ref[LANES + row : LANES + row + 2 * N_SLAB, :] = lower
    count = IMG_L // X_CHIPS
    group = lax.broadcasted_iota(jnp.int32, (count, LANES), 1) // SUB
    right = right_ref[...]
    total = None
    for part in range(X_CHIPS):
        rows = pl.ds(part * 2 * count, 2 * count)
        both = dot(upper_ref[rows, :], right, NT)
        wave_sum = both[:, :LANES] + both[:, LANES:] + dot(lower_ref[rows, :], right[:LANES], NT)
        lines = pl.ds(part * count, count)
        screened = wave_sum[:count] * cos_ref[lines, :] - wave_sum[count:] * sin_ref[lines, :]
        screened = screened + pltpu.roll(screened, 2 * SUB, 1)
        screened = screened + pltpu.roll(screened, SUB, 1)
        total = screened if total is None else jnp.where(group == part, screened, total)
    out_ref[...] = total


def sum_kernel(got_ref, out_ref):
    line = lax.broadcasted_iota(jnp.int32, (8, LANES), 0)
    group = lax.broadcasted_iota(jnp.int32, (8, LANES), 1) // SUB
    straight = (line // 4) == jnp.bitwise_and(line, 1)
    result = jnp.zeros((8, LANES), f32)
    for place in range(X_CHIPS):
        chip = (place + FIRST_X) % X_CHIPS
        total = got_ref[pl.ds(place * 2 * Z_CHIPS, 8), :]
        for step in range(1, 2 * Z_CHIPS // 8):
            total = total + got_ref[pl.ds(place * 2 * Z_CHIPS + 8 * step, 8), :]
        total = total + pltpu.roll(total, 4, 0)
        total = total + pltpu.roll(total, 2, 0)
        total = jnp.where(straight, total, pltpu.roll(total, 1, 0))
        for part in range(X_CHIPS):
            shift = (chip - part) % X_CHIPS
            moved = pltpu.roll(total, SUB * shift, 1) if shift else total
            chosen = (group == chip) & (jnp.bitwise_and(line, 3) == part)
            result = jnp.where(chosen, moved, result)
    out_ref[...] = result


def call(kernel, shape, specs, scratch, flops, moved, limit=24):
    return pl.pallas_call(
        kernel,
        out_shape=jax.ShapeDtypeStruct(shape, f32),
        in_specs=specs,
        out_specs=VMEM,
        scratch_shapes=scratch,
        compiler_params=pltpu.CompilerParams(vmem_limit_bytes=limit * 1024 * 1024),
        cost_estimate=pl.CostEstimate(flops=flops, bytes_accessed=moved, transcendentals=0),
    )


def grid_tables():
    q = np.arange(SUB)
    c = np.arange(CB)
    sign = (1 - 2 * (q % 2))[:, None]
    twist = np.concatenate([part * sign for part in wave(q[:, None] * c[None, :], NG)], 0)
    x, slab = np.divmod(column_members(), N_SLAB)
    n = 4 * slab + x
    cos_part, sin_part = wave((n[:, None] - SUB // 2) * c[None, :], CB)
    last = np.concatenate(
        [
            np.concatenate([cos_part, -sin_part], 1),
            np.concatenate([sin_part, cos_part], 1),
        ],
        0,
    )
    return twist.astype(np.float32), np.concatenate(np_split(last), 0)


def rotated(slow, fast, first_slow, first_fast):
    i, j = np.meshgrid(np.arange(slow), np.arange(fast), indexing="ij")
    return ((i + first_slow) % slow * fast + (j + first_fast) % fast).reshape(-1)


def layer_members():
    z, x = np.meshgrid(np.arange(Z_CHIPS), np.arange(X_CHIPS), indexing="ij")
    return ((x + FIRST_X) % X_CHIPS * Z_CHIPS + (z + TILE_Z) % Z_CHIPS).reshape(-1)


def column_members():
    return rotated(X_CHIPS, N_SLAB, FIRST_X, FIRST_SLAB)


def image_members():
    return rotated(X_CHIPS, Z_CHIPS, FIRST_X, IMAGE_Z)


def exchange(value, axes, members):
    groups = [[int(member) for member in members]]
    return lax.all_to_all(
        value, axes, split_axis=0, concat_axis=0, tiled=True, axis_index_groups=groups
    )


def image_lines():
    part, chip, half = np.meshgrid(
        np.arange(4), image_members(), np.arange(2), indexing="ij"
    )
    return (8 * chip + 4 * half + part).reshape(-1) - IMG_L // 2


def image_tables(spread):
    y, h, slab, r = np.meshgrid(
        np.arange(2), np.arange(2), np.arange(N_SLAB), np.arange(RB), indexing="ij"
    )
    slab = (slab + FIRST_SLAB) % N_SLAB
    row = (slab * ROWS_DEV + h * RB + r).reshape(-1) - ROWS_DEV * N_SLAB // 2
    y = y.reshape(-1)[None, :]
    cos_part, sin_part = wave(image_lines()[:, None] * row[None, :], NG)
    real = np.where(y == 0, cos_part, -sin_part).reshape(4, -1, row.size)
    imag = np.where(y == 0, sin_part, cos_part).reshape(4, -1, row.size)
    return np_split(np.concatenate([real, imag], 1).reshape(2 * IMG_L, row.size) * spread)


def screen_tables():
    columns = IMG_M // N_SLAB
    lines = jnp.asarray(image_lines().astype(np.float32))
    lane = jnp.arange(LANES, dtype=jnp.int32)
    m_index = (
        lax.axis_index("slab") * columns
        + lax.axis_index("x") * SUB
        + jnp.bitwise_and(lane, SUB - 1)
        - IMG_M // 2
    )
    place = (lax.axis_index("z") + Z_CHIPS - TILE_Z) % Z_CHIPS
    layer = (place * X_CHIPS + lane // SUB).astype(f32)
    w_value = w_reach * (2.0 * layer + 1.0 - LAYERS) / LAYERS
    l_direction = lines[:, None] * cell_size
    m_direction = m_index.astype(f32)[None, :] * cell_size
    radius = l_direction * l_direction + m_direction * m_direction
    n_lift = -radius / (1.0 + jnp.sqrt(1.0 - radius))
    phase_angle = -2.0 * math.pi * w_value[None, :] * n_lift
    return jnp.cos(phase_angle), jnp.sin(phase_angle)


def body(visibilities, row_offset, col_offset, w_layer, grid_block):
    tiles = w_layer.shape[0]
    spread = 1.0 / (
        2.0 * math.pi * kernel_width**2 * math.sqrt(tiles * LAYERS * N_SLAB * VIS)
    )
    sent = call(
        route_kernel,
        (LAYERS * SENT, VIS),
        [HBM] * 5,
        [
            pltpu.SMEM((tiles,), jnp.int32),
            pltpu.SMEM((tiles,), jnp.int32),
            pltpu.VMEM((2 * tiles, VIS), f32),
            pltpu.VMEM((tiles, VIS), f32),
            pltpu.VMEM((tiles, VIS), f32),
            pltpu.SMEM((LAYERS,), jnp.int32),
            pltpu.SemaphoreType.DMA((5,)),
        ],
        10**6,
        5 * 10**5,
        limit=60,
    )(w_layer, grid_block, visibilities.reshape(2 * tiles, VIS), row_offset, col_offset)
    got = exchange(sent.reshape(LAYERS, 1, SENT * VIS), ("x", "z"), layer_members())
    got = got.reshape(LAYERS * SENT, VIS)
    cos_screen, sin_screen = screen_tables()
    twist, last = grid_tables()
    pieces = call(
        grid_kernel,
        (PEERS * 2 * PAIRS, LANES),
        [VMEM] * 3,
        [
            pltpu.VMEM((2 * SUB, 2 * RB, CB), f32),
            pltpu.VMEM((2 * SUB * RB, 2 * CB), bf16),
            pltpu.VMEM((2 * SUB * RB, 2 * CB), bf16),
            pltpu.VMEM((EARLY * CAP, 2 * RB, CB), f32),
            pltpu.VMEM((1, SLOTS), jnp.int32),
            pltpu.SMEM((1, SLOTS), jnp.int32),
            pltpu.SemaphoreType.DMA,
        ],
        10**9,
        10**6,
    )(got, jnp.asarray(twist), jnp.asarray(last))
    turned = exchange(
        pieces.reshape(PEERS, 2 * PAIRS, LANES), ("x", "slab"), column_members()
    ).reshape(PEERS * 2 * PAIRS, LANES)
    upper, lower = image_tables(spread)
    shares = call(
        image_kernel,
        (2 * LAYERS, LANES),
        [VMEM] * 5,
        [pltpu.VMEM((2 * LANES, 2 * ROWS_DEV * N_SLAB), bf16)],
        10**9,
        3 * 10**6,
    )(turned, jnp.asarray(upper), jnp.asarray(lower), cos_screen, sin_screen)
    got = exchange(shares.reshape(LAYERS, 2, LANES), ("x", "z"), image_members())
    got = got.reshape(2 * LAYERS, LANES)
    return call(sum_kernel, (8, LANES), [VMEM], [], 10**5, 7 * 10**4)(got)


def solution(mesh):
    whole = ("x", "z", "slab")
    chips = Mesh(mesh.devices.reshape(X_CHIPS, Z_CHIPS, N_SLAB), whole)
    placed = (P(whole, None, None), P(whole, None), P(whole, None), P(whole), P(whole))
    return jax.shard_map(
        body, mesh=chips, in_specs=placed, out_specs=P(("x", "z"), "slab"), check_vma=False
    )
```

```python
import math

import ml_dtypes
import numpy as np

import jax
import jax.numpy as jnp
from jax import lax
from jax.experimental import pallas as pl
from jax.experimental.pallas import tpu as pltpu
from jax.sharding import Mesh
from jax.sharding import PartitionSpec as P

NG = 4096
VIS = 128
RB = 16
CB = 128
ROWS_DEV = 32
IMG_L = 512
IMG_M = 1024
CAP = 2
LAYERS = 64
N_SLAB = 8
X_CHIPS = 4
Z_CHIPS = 16
FIRST_X = 2
FIRST_SLAB = 4
TILE_Z = 11
IMAGE_Z = 8
SUB = 32
SLOTS = LAYERS * CAP
LANES = 128
SENT = 4 * CAP + 1
PEERS = X_CHIPS * N_SLAB
PAIRS = RB // 2
EARLY = 8
NARROW = math.sqrt(0.5 / math.log(2.0))


kernel_width = 1.0
cell_size = 2.4e-05
w_reach = 20000.0

f32 = jnp.float32
bf16 = jnp.bfloat16
VMEM = pl.BlockSpec(memory_space=pltpu.VMEM)
HBM = pl.BlockSpec(memory_space=pltpu.HBM)
NT = (((1,), (1,)), ((), ()))
NN = (((1,), (0,)), ((), ()))


def wave(turns, period):
    angle = 2.0 * np.pi * (np.asarray(turns) % period) / period
    return np.cos(angle), np.sin(angle)


def np_split(table):
    table = np.asarray(table, np.float32)
    upper = table.astype(ml_dtypes.bfloat16)
    return upper, (table - upper.astype(np.float32)).astype(ml_dtypes.bfloat16)


def split(value):
    upper = value.astype(bf16)
    return upper, (value - upper.astype(f32)).astype(bf16)


def dot(left, right, dims):
    return lax.dot_general(left, right, dims, preferred_element_type=f32)


def route_kernel(*refs):
    given, out_ref, held, (count_ref, sems) = refs[:5], refs[5], refs[6:11], refs[11:]
    layer_ref, block_ref, vis_ref, row_ref, col_ref = held
    copies = [
        pltpu.make_async_copy(source, target, sems.at[index])
        for index, (source, target) in enumerate(zip(given, held))
    ]
    for copy in copies:
        copy.start()
    out_ref[...] = jnp.zeros_like(out_ref)

    def clear(layer, carry):
        count_ref[layer] = 0
        return carry

    lax.fori_loop(0, LAYERS, clear, 0, unroll=16)
    for copy in copies:
        copy.wait()
    part = lax.broadcasted_iota(jnp.int32, (1, LANES), 1) // (LANES // CAP)

    def place(tile, carry):
        layer = layer_ref[tile]
        slot = count_ref[layer]
        count_ref[layer] = slot + 1
        start = layer * SENT + slot * 4
        out_ref[pl.ds(start, 2), :] = vis_ref[pl.ds(2 * tile, 2), :]
        out_ref[pl.ds(start + 2, 1), :] = row_ref[pl.ds(tile, 1), :]
        out_ref[pl.ds(start + 3, 1), :] = col_ref[pl.ds(tile, 1), :]
        named = out_ref.at[pl.ds(layer * SENT + 4 * CAP, 1), :]
        block = jnp.full((1, LANES), block_ref[tile], jnp.int32).astype(f32)
        pltpu.store(named, block, mask=part == slot)
        return carry

    lax.fori_loop(0, layer_ref.shape[0], place, 0, unroll=16)


def turn_by(value, step, period):
    real, imag = value
    step = step % period
    if 4 * step % period == 0:
        quarter = 4 * step // period
        return [(real, imag), (-imag, real), (-real, -imag), (imag, -real)][quarter]
    angle = 2.0 * math.pi * step / period
    cos_part, sin_part = math.cos(angle), math.sin(angle)
    return real * cos_part - imag * sin_part, real * sin_part + imag * cos_part


def dft(values):
    count = len(values)
    if count == 1:
        return values
    even, odd = dft(values[::2]), dft(values[1::2])
    odd = [turn_by(value, index, count) for index, value in enumerate(odd)]
    return [(a[0] + b[0], a[1] + b[1]) for a, b in zip(even, odd)] + [
        (a[0] - b[0], a[1] - b[1]) for a, b in zip(even, odd)
    ]


def grid_kernel(
    got_ref,
    twist_ref,
    last_ref,
    out_ref,
    grid_ref,
    upper_ref,
    lower_ref,
    early_ref,
    name_ref,
    block_ref,
    sem,
):
    named = got_ref[pl.ds(4 * CAP, LAYERS, stride=SENT), :]
    source = lax.broadcasted_iota(jnp.int32, (LAYERS, SLOTS), 0)
    lane = lax.broadcasted_iota(jnp.int32, (LAYERS, SLOTS), 1)
    name_ref[...] = jnp.sum(
        jnp.where(source == jnp.bitwise_and(lane, LAYERS - 1), named, 0.0), 0, keepdims=True
    ).astype(jnp.int32)
    copy = pltpu.make_async_copy(name_ref, block_ref, sem)
    copy.start()
    grid_ref[...] = jnp.zeros_like(grid_ref)
    offsets = jnp.concatenate(
        [got_ref[pl.ds(4 * slot + 3, LAYERS, stride=SENT), :] for slot in range(CAP)], 0
    ).T * NARROW
    rows = (lax.broadcasted_iota(jnp.int32, (RB, VIS), 0).astype(f32) + 0.5) * NARROW
    cols = (lax.broadcasted_iota(jnp.int32, (VIS, CB), 1).astype(f32) + 0.5) * NARROW

    def patch(source, slot, center):
        start = source * SENT + 4 * slot
        real = got_ref[pl.ds(start, 1), :]
        imag = got_ref[pl.ds(start + 1, 1), :]
        away = rows - got_ref[pl.ds(start + 2, 1), :] * NARROW
        near = jnp.exp2(-(away * away))
        upper, lower = split(jnp.concatenate([near * real, near * imag], 0))
        away = cols - center
        col_upper, col_lower = split(jnp.exp2(-(away * away)))
        left = jnp.concatenate([upper, lower], 0)
        both = dot(left, jnp.concatenate([col_upper, col_lower], 1), NN)
        half = both[:, :CB] + both[:, CB:]
        return half[: 2 * RB] + half[2 * RB :]

    early = [(source, slot) for source in range(EARLY) for slot in range(CAP)]
    for index, (source, slot) in enumerate(early):
        lane = slot * LAYERS + source
        early_ref[index] = patch(source, slot, offsets[:, lane : lane + 1])
    copy.wait()
    for index, (source, slot) in enumerate(early):
        grid_ref[block_ref[0, slot * LAYERS + source]] += early_ref[index]

    together = (LAYERS - EARLY) // 2

    def some(step, held):
        for part in range(together):
            for slot in range(CAP):
                source = EARLY + step * together + part
                lane = slot * LAYERS + part
                grid_ref[block_ref[0, slot * LAYERS + source]] += patch(
                    source, slot, held[:, lane : lane + 1]
                )
        return pltpu.roll(held, SLOTS - together, 1)

    lax.fori_loop(0, 2, some, pltpu.roll(offsets, SLOTS - EARLY, 1))

    wide, narrow = 8, SUB // 8
    for second in range(2):
        for low in range(wide):
            at = [second * SUB + low + wide * high for high in range(narrow)]
            turned = dft([(grid_ref[k, :RB, :], grid_ref[k, RB:, :]) for k in at])
            for index, k in enumerate(at):
                real, imag = turn_by(turned[index], index * low, SUB)
                grid_ref[k, :RB, :] = real
                grid_ref[k, RB:, :] = imag
        for low in range(narrow):
            at = [second * SUB + wide * low + high for high in range(wide)]
            turned = dft([(grid_ref[k, :RB, :], grid_ref[k, RB:, :]) for k in at])
            for index, (real, imag) in enumerate(turned):
                q = low + narrow * index
                cos_part = twist_ref[q : q + 1, :]
                sin_part = twist_ref[SUB + q : SUB + q + 1, :]
                upper, lower = split(
                    jnp.concatenate(
                        [real * cos_part - imag * sin_part, real * sin_part + imag * cos_part], 1
                    )
                )
                place = (second * SUB + q) * RB
                upper_ref[place : place + RB, :] = upper
                lower_ref[place : place + RB, :] = lower

    last_both = last_ref[...]
    last_upper = last_both[: 2 * SUB]
    for pair in range(PAIRS // 2):
        piece = slice(pair * 2 * LANES, (pair + 1) * 2 * LANES)
        both = dot(last_both, upper_ref[piece, :], NT)
        wave_sum = both[: 2 * SUB] + both[2 * SUB :] + dot(last_upper, lower_ref[piece, :], NT)
        for half in range(2):
            for part in range(2):
                row = 2 * (2 * pair + half) + part
                out_ref[pl.ds(row, PEERS, stride=2 * PAIRS), :] = wave_sum[
                    part * PEERS : (part + 1) * PEERS, half * LANES : (half + 1) * LANES
                ]


def swap_blocks(value):
    line = lax.broadcasted_iota(jnp.int32, value.shape, 0)
    block = lax.broadcasted_iota(jnp.int32, value.shape, 1) // RB
    for step in (4, 2, 1):
        line_bit = jnp.bitwise_and(line, step) != 0
        block_bit = jnp.bitwise_and(block, step) != 0
        up = pltpu.roll(pltpu.roll(value, 8 - step, 0), RB * step, 1)
        down = pltpu.roll(pltpu.roll(value, step, 0), LANES - RB * step, 1)
        moved = jnp.where(line_bit, down, up)
        value = jnp.where(line_bit == block_bit, value, moved)
    return value


def image_kernel(got_ref, upper_ref, lower_ref, cos_ref, sin_ref, out_ref, right_ref):
    blocks = SUB // N_SLAB
    for layer in range(X_CHIPS):
        for pair in range(blocks // 2):
            lines = []
            for high in (2 * pair, 2 * pair + 1):
                parts = []
                for y in range(2):
                    for h in range(2):
                        step = 2 * (h * blocks + high) + y
                        row = layer * N_SLAB * 2 * PAIRS + step
                        parts.append(
                            swap_blocks(got_ref[pl.ds(row, N_SLAB, stride=2 * PAIRS), :])
                        )
                lines.append(jnp.concatenate(parts, 1))
            upper, lower = split(jnp.concatenate(lines, 0))
            row = layer * SUB + pair * 2 * N_SLAB
            right_ref[row : row + 2 * N_SLAB, :] = upper
            right_ref[LANES + row : LANES + row + 2 * N_SLAB, :] = lower
    count = IMG_L // X_CHIPS
    group = lax.broadcasted_iota(jnp.int32, (count, LANES), 1) // SUB
    right = right_ref[...]
    total = None
    for part in range(X_CHIPS):
        rows = pl.ds(part * 2 * count, 2 * count)
        both = dot(upper_ref[rows, :], right, NT)
        wave_sum = both[:, :LANES] + both[:, LANES:] + dot(lower_ref[rows, :], right[:LANES], NT)
        lines = pl.ds(part * count, count)
        screened = wave_sum[:count] * cos_ref[lines, :] - wave_sum[count:] * sin_ref[lines, :]
        screened = screened + pltpu.roll(screened, 2 * SUB, 1)
        screened = screened + pltpu.roll(screened, SUB, 1)
        total = screened if total is None else jnp.where(group == part, screened, total)
    out_ref[...] = total


def sum_kernel(got_ref, out_ref):
    line = lax.broadcasted_iota(jnp.int32, (8, LANES), 0)
    group = lax.broadcasted_iota(jnp.int32, (8, LANES), 1) // SUB
    straight = (line // 4) == jnp.bitwise_and(line, 1)
    result = jnp.zeros((8, LANES), f32)
    for place in range(X_CHIPS):
        chip = (place + FIRST_X) % X_CHIPS
        total = got_ref[pl.ds(place * 2 * Z_CHIPS, 8), :]
        for step in range(1, 2 * Z_CHIPS // 8):
            total = total + got_ref[pl.ds(place * 2 * Z_CHIPS + 8 * step, 8), :]
        total = total + pltpu.roll(total, 4, 0)
        total = total + pltpu.roll(total, 2, 0)
        total = jnp.where(straight, total, pltpu.roll(total, 1, 0))
        for part in range(X_CHIPS):
            shift = (chip - part) % X_CHIPS
            moved = pltpu.roll(total, SUB * shift, 1) if shift else total
            chosen = (group == chip) & (jnp.bitwise_and(line, 3) == part)
            result = jnp.where(chosen, moved, result)
    out_ref[...] = result


def call(kernel, shape, specs, scratch, flops, moved, limit=24):
    return pl.pallas_call(
        kernel,
        out_shape=jax.ShapeDtypeStruct(shape, f32),
        in_specs=specs,
        out_specs=VMEM,
        scratch_shapes=scratch,
        compiler_params=pltpu.CompilerParams(vmem_limit_bytes=limit * 1024 * 1024),
        cost_estimate=pl.CostEstimate(flops=flops, bytes_accessed=moved, transcendentals=0),
    )


def grid_tables():
    q = np.arange(SUB)
    c = np.arange(CB)
    sign = (1 - 2 * (q % 2))[:, None]
    twist = np.concatenate([part * sign for part in wave(q[:, None] * c[None, :], NG)], 0)
    x, slab = np.divmod(column_members(), N_SLAB)
    n = 4 * slab + x
    cos_part, sin_part = wave((n[:, None] - SUB // 2) * c[None, :], CB)
    last = np.concatenate(
        [
            np.concatenate([cos_part, -sin_part], 1),
            np.concatenate([sin_part, cos_part], 1),
        ],
        0,
    )
    return twist.astype(np.float32), np.concatenate(np_split(last), 0)


def rotated(slow, fast, first_slow, first_fast):
    i, j = np.meshgrid(np.arange(slow), np.arange(fast), indexing="ij")
    return ((i + first_slow) % slow * fast + (j + first_fast) % fast).reshape(-1)


def layer_members():
    z, x = np.meshgrid(np.arange(Z_CHIPS), np.arange(X_CHIPS), indexing="ij")
    return ((x + FIRST_X) % X_CHIPS * Z_CHIPS + (z + TILE_Z) % Z_CHIPS).reshape(-1)


def column_members():
    return rotated(X_CHIPS, N_SLAB, FIRST_X, FIRST_SLAB)


def image_members():
    return rotated(X_CHIPS, Z_CHIPS, FIRST_X, IMAGE_Z)


def exchange(value, axes, members):
    groups = [[int(member) for member in members]]
    return lax.all_to_all(
        value, axes, split_axis=0, concat_axis=0, tiled=True, axis_index_groups=groups
    )


def image_lines():
    part, chip, half = np.meshgrid(
        np.arange(4), image_members(), np.arange(2), indexing="ij"
    )
    return (8 * chip + 4 * half + part).reshape(-1) - IMG_L // 2


def image_tables(spread):
    y, h, slab, r = np.meshgrid(
        np.arange(2), np.arange(2), np.arange(N_SLAB), np.arange(RB), indexing="ij"
    )
    slab = (slab + FIRST_SLAB) % N_SLAB
    row = (slab * ROWS_DEV + h * RB + r).reshape(-1) - ROWS_DEV * N_SLAB // 2
    y = y.reshape(-1)[None, :]
    cos_part, sin_part = wave(image_lines()[:, None] * row[None, :], NG)
    real = np.where(y == 0, cos_part, -sin_part).reshape(4, -1, row.size)
    imag = np.where(y == 0, sin_part, cos_part).reshape(4, -1, row.size)
    return np_split(np.concatenate([real, imag], 1).reshape(2 * IMG_L, row.size) * spread)


def screen_tables():
    columns = IMG_M // N_SLAB
    lines = jnp.asarray(image_lines().astype(np.float32))
    lane = jnp.arange(LANES, dtype=jnp.int32)
    m_index = (
        lax.axis_index("slab") * columns
        + lax.axis_index("x") * SUB
        + jnp.bitwise_and(lane, SUB - 1)
        - IMG_M // 2
    )
    place = (lax.axis_index("z") + Z_CHIPS - TILE_Z) % Z_CHIPS
    layer = (place * X_CHIPS + lane // SUB).astype(f32)
    w_value = w_reach * (2.0 * layer + 1.0 - LAYERS) / LAYERS
    l_direction = lines[:, None] * cell_size
    m_direction = m_index.astype(f32)[None, :] * cell_size
    radius = l_direction * l_direction + m_direction * m_direction
    n_lift = -radius / (1.0 + jnp.sqrt(1.0 - radius))
    phase_angle = -2.0 * math.pi * w_value[None, :] * n_lift
    return jnp.cos(phase_angle), jnp.sin(phase_angle)


def body(visibilities, row_offset, col_offset, w_layer, grid_block):
    tiles = w_layer.shape[0]
    spread = 1.0 / (
        2.0 * math.pi * kernel_width**2 * math.sqrt(tiles * LAYERS * N_SLAB * VIS)
    )
    sent = call(
        route_kernel,
        (LAYERS * SENT, VIS),
        [HBM] * 5,
        [
            pltpu.SMEM((tiles,), jnp.int32),
            pltpu.SMEM((tiles,), jnp.int32),
            pltpu.VMEM((2 * tiles, VIS), f32),
            pltpu.VMEM((tiles, VIS), f32),
            pltpu.VMEM((tiles, VIS), f32),
            pltpu.SMEM((LAYERS,), jnp.int32),
            pltpu.SemaphoreType.DMA((5,)),
        ],
        10**6,
        5 * 10**5,
        limit=60,
    )(w_layer, grid_block, visibilities.reshape(2 * tiles, VIS), row_offset, col_offset)
    got = exchange(sent.reshape(LAYERS, 1, SENT * VIS), ("x", "z"), layer_members())
    got = got.reshape(LAYERS * SENT, VIS)
    cos_screen, sin_screen = screen_tables()
    twist, last = grid_tables()
    pieces = call(
        grid_kernel,
        (PEERS * 2 * PAIRS, LANES),
        [VMEM] * 3,
        [
            pltpu.VMEM((2 * SUB, 2 * RB, CB), f32),
            pltpu.VMEM((2 * SUB * RB, 2 * CB), bf16),
            pltpu.VMEM((2 * SUB * RB, 2 * CB), bf16),
            pltpu.VMEM((EARLY * CAP, 2 * RB, CB), f32),
            pltpu.VMEM((1, SLOTS), jnp.int32),
            pltpu.SMEM((1, SLOTS), jnp.int32),
            pltpu.SemaphoreType.DMA,
        ],
        10**9,
        10**6,
    )(got, jnp.asarray(twist), jnp.asarray(last))
    turned = exchange(
        pieces.reshape(PEERS, 2 * PAIRS, LANES), ("x", "slab"), column_members()
    ).reshape(PEERS * 2 * PAIRS, LANES)
    upper, lower = image_tables(spread)
    shares = call(
        image_kernel,
        (2 * LAYERS, LANES),
        [VMEM] * 5,
        [pltpu.VMEM((2 * LANES, 2 * ROWS_DEV * N_SLAB), bf16)],
        10**9,
        3 * 10**6,
    )(turned, jnp.asarray(upper), jnp.asarray(lower), cos_screen, sin_screen)
    got = exchange(shares.reshape(LAYERS, 2, LANES), ("x", "z"), image_members())
    got = got.reshape(2 * LAYERS, LANES)
    return call(sum_kernel, (8, LANES), [VMEM], [], 10**5, 7 * 10**4)(got)


def solution(mesh):
    whole = ("x", "z", "slab")
    chips = Mesh(mesh.devices.reshape(X_CHIPS, Z_CHIPS, N_SLAB), whole)
    placed = (P(whole, None, None), P(whole, None), P(whole, None), P(whole), P(whole))
    return jax.shard_map(
        body, mesh=chips, in_specs=placed, out_specs=P(("x", "z"), "slab"), check_vma=False
    )
```

```python
import math

import ml_dtypes
import numpy as np

import jax
import jax.numpy as jnp
from jax import lax
from jax.experimental import pallas as pl
from jax.experimental.pallas import tpu as pltpu
from jax.sharding import Mesh
from jax.sharding import PartitionSpec as P

NG = 4096
VIS = 128
RB = 16
CB = 128
ROWS_DEV = 32
IMG_L = 512
IMG_M = 1024
CAP = 2
LAYERS = 64
N_SLAB = 8
X_CHIPS = 4
Z_CHIPS = 16
FIRST_X = 2
FIRST_SLAB = 4
TILE_Z = 9
IMAGE_Z = 8
SUB = 32
SLOTS = LAYERS * CAP
LANES = 128
SENT = 4 * CAP + 1
PEERS = X_CHIPS * N_SLAB
PAIRS = RB // 2
EARLY = 8
NARROW = math.sqrt(0.5 / math.log(2.0))


kernel_width = 1.0
cell_size = 2.4e-05
w_reach = 20000.0

f32 = jnp.float32
bf16 = jnp.bfloat16
VMEM = pl.BlockSpec(memory_space=pltpu.VMEM)
HBM = pl.BlockSpec(memory_space=pltpu.HBM)
NT = (((1,), (1,)), ((), ()))
NN = (((1,), (0,)), ((), ()))


def wave(turns, period):
    angle = 2.0 * np.pi * (np.asarray(turns) % period) / period
    return np.cos(angle), np.sin(angle)


def np_split(table):
    table = np.asarray(table, np.float32)
    upper = table.astype(ml_dtypes.bfloat16)
    return upper, (table - upper.astype(np.float32)).astype(ml_dtypes.bfloat16)


def split(value):
    upper = value.astype(bf16)
    return upper, (value - upper.astype(f32)).astype(bf16)


def dot(left, right, dims):
    return lax.dot_general(left, right, dims, preferred_element_type=f32)


def route_kernel(*refs):
    given, out_ref, held, (count_ref, sems) = refs[:5], refs[5], refs[6:11], refs[11:]
    layer_ref, block_ref, vis_ref, row_ref, col_ref = held
    copies = [
        pltpu.make_async_copy(source, target, sems.at[index])
        for index, (source, target) in enumerate(zip(given, held))
    ]
    for copy in copies:
        copy.start()
    out_ref[...] = jnp.zeros_like(out_ref)

    def clear(layer, carry):
        count_ref[layer] = 0
        return carry

    lax.fori_loop(0, LAYERS, clear, 0, unroll=16)
    for copy in copies:
        copy.wait()
    part = lax.broadcasted_iota(jnp.int32, (1, LANES), 1) // (LANES // CAP)

    def place(tile, carry):
        layer = layer_ref[tile]
        slot = count_ref[layer]
        count_ref[layer] = slot + 1
        start = layer * SENT + slot * 4
        out_ref[pl.ds(start, 2), :] = vis_ref[pl.ds(2 * tile, 2), :]
        out_ref[pl.ds(start + 2, 1), :] = row_ref[pl.ds(tile, 1), :]
        out_ref[pl.ds(start + 3, 1), :] = col_ref[pl.ds(tile, 1), :]
        named = out_ref.at[pl.ds(layer * SENT + 4 * CAP, 1), :]
        block = jnp.full((1, LANES), block_ref[tile], jnp.int32).astype(f32)
        pltpu.store(named, block, mask=part == slot)
        return carry

    lax.fori_loop(0, layer_ref.shape[0], place, 0, unroll=16)


def turn_by(value, step, period):
    real, imag = value
    step = step % period
    if 4 * step % period == 0:
        quarter = 4 * step // period
        return [(real, imag), (-imag, real), (-real, -imag), (imag, -real)][quarter]
    angle = 2.0 * math.pi * step / period
    cos_part, sin_part = math.cos(angle), math.sin(angle)
    return real * cos_part - imag * sin_part, real * sin_part + imag * cos_part


def dft(values):
    count = len(values)
    if count == 1:
        return values
    even, odd = dft(values[::2]), dft(values[1::2])
    odd = [turn_by(value, index, count) for index, value in enumerate(odd)]
    return [(a[0] + b[0], a[1] + b[1]) for a, b in zip(even, odd)] + [
        (a[0] - b[0], a[1] - b[1]) for a, b in zip(even, odd)
    ]


def grid_kernel(
    got_ref,
    twist_ref,
    last_ref,
    out_ref,
    grid_ref,
    upper_ref,
    lower_ref,
    early_ref,
    name_ref,
    block_ref,
    sem,
):
    named = got_ref[pl.ds(4 * CAP, LAYERS, stride=SENT), :]
    source = lax.broadcasted_iota(jnp.int32, (LAYERS, SLOTS), 0)
    lane = lax.broadcasted_iota(jnp.int32, (LAYERS, SLOTS), 1)
    name_ref[...] = jnp.sum(
        jnp.where(source == jnp.bitwise_and(lane, LAYERS - 1), named, 0.0), 0, keepdims=True
    ).astype(jnp.int32)
    copy = pltpu.make_async_copy(name_ref, block_ref, sem)
    copy.start()
    grid_ref[...] = jnp.zeros_like(grid_ref)
    offsets = jnp.concatenate(
        [got_ref[pl.ds(4 * slot + 3, LAYERS, stride=SENT), :] for slot in range(CAP)], 0
    ).T * NARROW
    rows = (lax.broadcasted_iota(jnp.int32, (RB, VIS), 0).astype(f32) + 0.5) * NARROW
    cols = (lax.broadcasted_iota(jnp.int32, (VIS, CB), 1).astype(f32) + 0.5) * NARROW

    def patch(source, slot, center):
        start = source * SENT + 4 * slot
        real = got_ref[pl.ds(start, 1), :]
        imag = got_ref[pl.ds(start + 1, 1), :]
        away = rows - got_ref[pl.ds(start + 2, 1), :] * NARROW
        near = jnp.exp2(-(away * away))
        upper, lower = split(jnp.concatenate([near * real, near * imag], 0))
        away = cols - center
        col_upper, col_lower = split(jnp.exp2(-(away * away)))
        left = jnp.concatenate([upper, lower], 0)
        both = dot(left, jnp.concatenate([col_upper, col_lower], 1), NN)
        half = both[:, :CB] + both[:, CB:]
        return half[: 2 * RB] + half[2 * RB :]

    early = [(source, slot) for source in range(EARLY) for slot in range(CAP)]
    for index, (source, slot) in enumerate(early):
        lane = slot * LAYERS + source
        early_ref[index] = patch(source, slot, offsets[:, lane : lane + 1])
    copy.wait()
    for index, (source, slot) in enumerate(early):
        grid_ref[block_ref[0, slot * LAYERS + source]] += early_ref[index]

    together = (LAYERS - EARLY) // 2

    def some(step, held):
        for part in range(together):
            for slot in range(CAP):
                source = EARLY + step * together + part
                lane = slot * LAYERS + part
                grid_ref[block_ref[0, slot * LAYERS + source]] += patch(
                    source, slot, held[:, lane : lane + 1]
                )
        return pltpu.roll(held, SLOTS - together, 1)

    lax.fori_loop(0, 2, some, pltpu.roll(offsets, SLOTS - EARLY, 1))

    wide, narrow = 8, SUB // 8
    for second in range(2):
        for low in range(wide):
            at = [second * SUB + low + wide * high for high in range(narrow)]
            turned = dft([(grid_ref[k, :RB, :], grid_ref[k, RB:, :]) for k in at])
            for index, k in enumerate(at):
                real, imag = turn_by(turned[index], index * low, SUB)
                grid_ref[k, :RB, :] = real
                grid_ref[k, RB:, :] = imag
        for low in range(narrow):
            at = [second * SUB + wide * low + high for high in range(wide)]
            turned = dft([(grid_ref[k, :RB, :], grid_ref[k, RB:, :]) for k in at])
            for index, (real, imag) in enumerate(turned):
                q = low + narrow * index
                cos_part = twist_ref[q : q + 1, :]
                sin_part = twist_ref[SUB + q : SUB + q + 1, :]
                upper, lower = split(
                    jnp.concatenate(
                        [real * cos_part - imag * sin_part, real * sin_part + imag * cos_part], 1
                    )
                )
                place = (second * SUB + q) * RB
                upper_ref[place : place + RB, :] = upper
                lower_ref[place : place + RB, :] = lower

    last_both = last_ref[...]
    last_upper = last_both[: 2 * SUB]
    for pair in range(PAIRS // 2):
        piece = slice(pair * 2 * LANES, (pair + 1) * 2 * LANES)
        both = dot(last_both, upper_ref[piece, :], NT)
        wave_sum = both[: 2 * SUB] + both[2 * SUB :] + dot(last_upper, lower_ref[piece, :], NT)
        for half in range(2):
            for part in range(2):
                row = 2 * (2 * pair + half) + part
                out_ref[pl.ds(row, PEERS, stride=2 * PAIRS), :] = wave_sum[
                    part * PEERS : (part + 1) * PEERS, half * LANES : (half + 1) * LANES
                ]


def swap_blocks(value):
    line = lax.broadcasted_iota(jnp.int32, value.shape, 0)
    block = lax.broadcasted_iota(jnp.int32, value.shape, 1) // RB
    for step in (4, 2, 1):
        line_bit = jnp.bitwise_and(line, step) != 0
        block_bit = jnp.bitwise_and(block, step) != 0
        up = pltpu.roll(pltpu.roll(value, 8 - step, 0), RB * step, 1)
        down = pltpu.roll(pltpu.roll(value, step, 0), LANES - RB * step, 1)
        moved = jnp.where(line_bit, down, up)
        value = jnp.where(line_bit == block_bit, value, moved)
    return value


def image_kernel(got_ref, upper_ref, lower_ref, cos_ref, sin_ref, out_ref, right_ref):
    blocks = SUB // N_SLAB
    for layer in range(X_CHIPS):
        for pair in range(blocks // 2):
            lines = []
            for high in (2 * pair, 2 * pair + 1):
                parts = []
                for y in range(2):
                    for h in range(2):
                        step = 2 * (h * blocks + high) + y
                        row = layer * 2 * PAIRS + step
                        parts.append(
                            swap_blocks(
                                got_ref[pl.ds(row, N_SLAB, stride=X_CHIPS * 2 * PAIRS), :]
                            )
                        )
                lines.append(jnp.concatenate(parts, 1))
            upper, lower = split(jnp.concatenate(lines, 0))
            row = layer * SUB + pair * 2 * N_SLAB
            right_ref[row : row + 2 * N_SLAB, :] = upper
            right_ref[LANES + row : LANES + row + 2 * N_SLAB, :] = lower
    count = IMG_L // X_CHIPS
    group = lax.broadcasted_iota(jnp.int32, (count, LANES), 1) // SUB
    right = right_ref[...]
    total = None
    for part in range(X_CHIPS):
        rows = pl.ds(part * 2 * count, 2 * count)
        both = dot(upper_ref[rows, :], right, NT)
        wave_sum = both[:, :LANES] + both[:, LANES:] + dot(lower_ref[rows, :], right[:LANES], NT)
        lines = pl.ds(part * count, count)
        screened = wave_sum[:count] * cos_ref[lines, :] - wave_sum[count:] * sin_ref[lines, :]
        screened = screened + pltpu.roll(screened, 2 * SUB, 1)
        screened = screened + pltpu.roll(screened, SUB, 1)
        total = screened if total is None else jnp.where(group == part, screened, total)
    out_ref[...] = total


def sum_kernel(got_ref, out_ref):
    line = lax.broadcasted_iota(jnp.int32, (8, LANES), 0)
    group = lax.broadcasted_iota(jnp.int32, (8, LANES), 1) // SUB
    straight = (line // 4) == jnp.bitwise_and(line, 1)
    result = jnp.zeros((8, LANES), f32)
    for place in range(X_CHIPS):
        chip = (place + FIRST_X) % X_CHIPS
        total = got_ref[pl.ds(place * 2 * Z_CHIPS, 8), :]
        for step in range(1, 2 * Z_CHIPS // 8):
            total = total + got_ref[pl.ds(place * 2 * Z_CHIPS + 8 * step, 8), :]
        total = total + pltpu.roll(total, 4, 0)
        total = total + pltpu.roll(total, 2, 0)
        total = jnp.where(straight, total, pltpu.roll(total, 1, 0))
        for part in range(X_CHIPS):
            shift = (chip - part) % X_CHIPS
            moved = pltpu.roll(total, SUB * shift, 1) if shift else total
            chosen = (group == chip) & (jnp.bitwise_and(line, 3) == part)
            result = jnp.where(chosen, moved, result)
    out_ref[...] = result


def call(kernel, shape, specs, scratch, flops, moved, limit=24):
    return pl.pallas_call(
        kernel,
        out_shape=jax.ShapeDtypeStruct(shape, f32),
        in_specs=specs,
        out_specs=VMEM,
        scratch_shapes=scratch,
        compiler_params=pltpu.CompilerParams(vmem_limit_bytes=limit * 1024 * 1024),
        cost_estimate=pl.CostEstimate(flops=flops, bytes_accessed=moved, transcendentals=0),
    )


def grid_tables():
    q = np.arange(SUB)
    c = np.arange(CB)
    sign = (1 - 2 * (q % 2))[:, None]
    twist = np.concatenate([part * sign for part in wave(q[:, None] * c[None, :], NG)], 0)
    x, slab = np.divmod(column_members(), N_SLAB)
    n = 4 * slab + x
    cos_part, sin_part = wave((n[:, None] - SUB // 2) * c[None, :], CB)
    last = np.concatenate(
        [
            np.concatenate([cos_part, -sin_part], 1),
            np.concatenate([sin_part, cos_part], 1),
        ],
        0,
    )
    return twist.astype(np.float32), np.concatenate(np_split(last), 0)


def rotated(slow, fast, first_slow, first_fast):
    i, j = np.meshgrid(np.arange(slow), np.arange(fast), indexing="ij")
    return ((i + first_slow) % slow * fast + (j + first_fast) % fast).reshape(-1)


def layer_members():
    z, x = np.meshgrid(np.arange(Z_CHIPS), np.arange(X_CHIPS), indexing="ij")
    return ((x + FIRST_X) % X_CHIPS * Z_CHIPS + (z + TILE_Z) % Z_CHIPS).reshape(-1)


def column_members():
    slab, x = np.meshgrid(np.arange(N_SLAB), np.arange(X_CHIPS), indexing="ij")
    return ((x + FIRST_X) % X_CHIPS * N_SLAB + (slab + FIRST_SLAB) % N_SLAB).reshape(-1)


def image_members():
    return rotated(X_CHIPS, Z_CHIPS, FIRST_X, IMAGE_Z)


def exchange(value, axes, members):
    groups = [[int(member) for member in members]]
    return lax.all_to_all(
        value, axes, split_axis=0, concat_axis=0, tiled=True, axis_index_groups=groups
    )


def image_lines():
    part, chip, half = np.meshgrid(
        np.arange(4), image_members(), np.arange(2), indexing="ij"
    )
    return (8 * chip + 4 * half + part).reshape(-1) - IMG_L // 2


def image_tables(spread):
    y, h, slab, r = np.meshgrid(
        np.arange(2), np.arange(2), np.arange(N_SLAB), np.arange(RB), indexing="ij"
    )
    slab = (slab + FIRST_SLAB) % N_SLAB
    row = (slab * ROWS_DEV + h * RB + r).reshape(-1) - ROWS_DEV * N_SLAB // 2
    y = y.reshape(-1)[None, :]
    cos_part, sin_part = wave(image_lines()[:, None] * row[None, :], NG)
    real = np.where(y == 0, cos_part, -sin_part).reshape(4, -1, row.size)
    imag = np.where(y == 0, sin_part, cos_part).reshape(4, -1, row.size)
    return np_split(np.concatenate([real, imag], 1).reshape(2 * IMG_L, row.size) * spread)


def screen_tables():
    columns = IMG_M // N_SLAB
    lines = jnp.asarray(image_lines().astype(np.float32))
    lane = jnp.arange(LANES, dtype=jnp.int32)
    m_index = (
        lax.axis_index("slab") * columns
        + lax.axis_index("x") * SUB
        + jnp.bitwise_and(lane, SUB - 1)
        - IMG_M // 2
    )
    place = (lax.axis_index("z") + Z_CHIPS - TILE_Z) % Z_CHIPS
    layer = (place * X_CHIPS + lane // SUB).astype(f32)
    w_value = w_reach * (2.0 * layer + 1.0 - LAYERS) / LAYERS
    l_direction = lines[:, None] * cell_size
    m_direction = m_index.astype(f32)[None, :] * cell_size
    radius = l_direction * l_direction + m_direction * m_direction
    n_lift = -radius / (1.0 + jnp.sqrt(1.0 - radius))
    phase_angle = -2.0 * math.pi * w_value[None, :] * n_lift
    return jnp.cos(phase_angle), jnp.sin(phase_angle)


def body(visibilities, row_offset, col_offset, w_layer, grid_block):
    tiles = w_layer.shape[0]
    spread = 1.0 / (
        2.0 * math.pi * kernel_width**2 * math.sqrt(tiles * LAYERS * N_SLAB * VIS)
    )
    sent = call(
        route_kernel,
        (LAYERS * SENT, VIS),
        [HBM] * 5,
        [
            pltpu.SMEM((tiles,), jnp.int32),
            pltpu.SMEM((tiles,), jnp.int32),
            pltpu.VMEM((2 * tiles, VIS), f32),
            pltpu.VMEM((tiles, VIS), f32),
            pltpu.VMEM((tiles, VIS), f32),
            pltpu.SMEM((LAYERS,), jnp.int32),
            pltpu.SemaphoreType.DMA((5,)),
        ],
        10**6,
        5 * 10**5,
        limit=60,
    )(w_layer, grid_block, visibilities.reshape(2 * tiles, VIS), row_offset, col_offset)
    got = exchange(sent.reshape(LAYERS, 1, SENT * VIS), ("x", "z"), layer_members())
    got = got.reshape(LAYERS * SENT, VIS)
    cos_screen, sin_screen = screen_tables()
    twist, last = grid_tables()
    pieces = call(
        grid_kernel,
        (PEERS * 2 * PAIRS, LANES),
        [VMEM] * 3,
        [
            pltpu.VMEM((2 * SUB, 2 * RB, CB), f32),
            pltpu.VMEM((2 * SUB * RB, 2 * CB), bf16),
            pltpu.VMEM((2 * SUB * RB, 2 * CB), bf16),
            pltpu.VMEM((EARLY * CAP, 2 * RB, CB), f32),
            pltpu.VMEM((1, SLOTS), jnp.int32),
            pltpu.SMEM((1, SLOTS), jnp.int32),
            pltpu.SemaphoreType.DMA,
        ],
        10**9,
        10**6,
    )(got, jnp.asarray(twist), jnp.asarray(last))
    turned = exchange(
        pieces.reshape(PEERS, 2 * PAIRS, LANES), ("x", "slab"), column_members()
    ).reshape(PEERS * 2 * PAIRS, LANES)
    upper, lower = image_tables(spread)
    shares = call(
        image_kernel,
        (2 * LAYERS, LANES),
        [VMEM] * 5,
        [pltpu.VMEM((2 * LANES, 2 * ROWS_DEV * N_SLAB), bf16)],
        10**9,
        3 * 10**6,
    )(turned, jnp.asarray(upper), jnp.asarray(lower), cos_screen, sin_screen)
    got = exchange(shares.reshape(LAYERS, 2, LANES), ("x", "z"), image_members())
    got = got.reshape(2 * LAYERS, LANES)
    return call(sum_kernel, (8, LANES), [VMEM], [], 10**5, 7 * 10**4)(got)


def solution(mesh):
    whole = ("x", "z", "slab")
    chips = Mesh(mesh.devices.reshape(X_CHIPS, Z_CHIPS, N_SLAB), whole)
    placed = (P(whole, None, None), P(whole, None), P(whole, None), P(whole), P(whole))
    return jax.shard_map(
        body, mesh=chips, in_specs=placed, out_specs=P(("x", "z"), "slab"), check_vma=False
    )
```

```python
import math

import ml_dtypes
import numpy as np

import jax
import jax.numpy as jnp
from jax import lax
from jax.experimental import pallas as pl
from jax.experimental.pallas import tpu as pltpu
from jax.sharding import Mesh
from jax.sharding import PartitionSpec as P

NG = 4096
VIS = 128
RB = 16
CB = 128
ROWS_DEV = 32
IMG_L = 512
IMG_M = 1024
CAP = 2
LAYERS = 64
N_SLAB = 8
X_CHIPS = 4
Z_CHIPS = 16
FIRST_X = 2
FIRST_SLAB = 4
TILE_Z = 9
IMAGE_Z = 8
SUB = 32
SLOTS = LAYERS * CAP
LANES = 128
SENT = 4 * CAP + 1
PEERS = X_CHIPS * N_SLAB
PAIRS = RB // 2
EARLY = 8
NARROW = math.sqrt(0.5 / math.log(2.0))


kernel_width = 1.0
cell_size = 2.4e-05
w_reach = 20000.0

f32 = jnp.float32
bf16 = jnp.bfloat16
VMEM = pl.BlockSpec(memory_space=pltpu.VMEM)
HBM = pl.BlockSpec(memory_space=pltpu.HBM)
NT = (((1,), (1,)), ((), ()))
NN = (((1,), (0,)), ((), ()))


def wave(turns, period):
    angle = 2.0 * np.pi * (np.asarray(turns) % period) / period
    return np.cos(angle), np.sin(angle)


def np_split(table):
    table = np.asarray(table, np.float32)
    upper = table.astype(ml_dtypes.bfloat16)
    return upper, (table - upper.astype(np.float32)).astype(ml_dtypes.bfloat16)


def split(value):
    upper = value.astype(bf16)
    return upper, (value - upper.astype(f32)).astype(bf16)


def dot(left, right, dims):
    return lax.dot_general(left, right, dims, preferred_element_type=f32)


def route_kernel(*refs):
    given, out_ref, held, (count_ref, sems) = refs[:5], refs[5], refs[6:11], refs[11:]
    layer_ref, block_ref, vis_ref, row_ref, col_ref = held
    copies = [
        pltpu.make_async_copy(source, target, sems.at[index])
        for index, (source, target) in enumerate(zip(given, held))
    ]
    for copy in copies:
        copy.start()
    out_ref[...] = jnp.zeros_like(out_ref)

    def clear(layer, carry):
        count_ref[layer] = 0
        return carry

    lax.fori_loop(0, LAYERS, clear, 0, unroll=16)
    for copy in copies:
        copy.wait()
    part = lax.broadcasted_iota(jnp.int32, (1, LANES), 1) // (LANES // CAP)

    def place(tile, carry):
        layer = layer_ref[tile]
        slot = count_ref[layer]
        count_ref[layer] = slot + 1
        start = layer * SENT + slot * 4
        out_ref[pl.ds(start, 2), :] = vis_ref[pl.ds(2 * tile, 2), :]
        out_ref[pl.ds(start + 2, 1), :] = row_ref[pl.ds(tile, 1), :] * NARROW
        out_ref[pl.ds(start + 3, 1), :] = col_ref[pl.ds(tile, 1), :] * NARROW
        named = out_ref.at[pl.ds(layer * SENT + 4 * CAP, 1), :]
        block = jnp.full((1, LANES), block_ref[tile], jnp.int32).astype(f32)
        pltpu.store(named, block, mask=part == slot)
        return carry

    lax.fori_loop(0, layer_ref.shape[0], place, 0, unroll=16)


def turn_by(value, step, period):
    real, imag = value
    step = step % period
    if 4 * step % period == 0:
        quarter = 4 * step // period
        return [(real, imag), (-imag, real), (-real, -imag), (imag, -real)][quarter]
    angle = 2.0 * math.pi * step / period
    cos_part, sin_part = math.cos(angle), math.sin(angle)
    return real * cos_part - imag * sin_part, real * sin_part + imag * cos_part


def dft(values):
    count = len(values)
    if count == 1:
        return values
    even, odd = dft(values[::2]), dft(values[1::2])
    odd = [turn_by(value, index, count) for index, value in enumerate(odd)]
    return [(a[0] + b[0], a[1] + b[1]) for a, b in zip(even, odd)] + [
        (a[0] - b[0], a[1] - b[1]) for a, b in zip(even, odd)
    ]


def grid_kernel(
    got_ref,
    twist_ref,
    last_ref,
    out_ref,
    grid_ref,
    upper_ref,
    lower_ref,
    early_ref,
    name_ref,
    block_ref,
    sem,
):
    named = got_ref[pl.ds(4 * CAP, LAYERS, stride=SENT), :]
    source = lax.broadcasted_iota(jnp.int32, (LAYERS, SLOTS), 0)
    lane = lax.broadcasted_iota(jnp.int32, (LAYERS, SLOTS), 1)
    name_ref[...] = jnp.sum(
        jnp.where(source == jnp.bitwise_and(lane, LAYERS - 1), named, 0.0), 0, keepdims=True
    ).astype(jnp.int32)
    copy = pltpu.make_async_copy(name_ref, block_ref, sem)
    copy.start()
    grid_ref[...] = jnp.zeros_like(grid_ref)
    offsets = jnp.concatenate(
        [got_ref[pl.ds(4 * slot + 3, LAYERS, stride=SENT), :] for slot in range(CAP)], 0
    ).T
    rows = (lax.broadcasted_iota(jnp.int32, (RB, VIS), 0).astype(f32) + 0.5) * NARROW
    cols = (lax.broadcasted_iota(jnp.int32, (VIS, CB), 1).astype(f32) + 0.5) * NARROW

    def patch(source, slot, center):
        start = source * SENT + 4 * slot
        real = got_ref[pl.ds(start, 1), :]
        imag = got_ref[pl.ds(start + 1, 1), :]
        away = rows - got_ref[pl.ds(start + 2, 1), :]
        near = jnp.exp2(-(away * away))
        upper, lower = split(jnp.concatenate([near * real, near * imag], 0))
        away = cols - center
        col_upper, col_lower = split(jnp.exp2(-(away * away)))
        left = jnp.concatenate([upper, lower], 0)
        both = dot(left, jnp.concatenate([col_upper, col_lower], 1), NN)
        half = both[:, :CB] + both[:, CB:]
        return half[: 2 * RB] + half[2 * RB :]

    early = [(source, slot) for source in range(EARLY) for slot in range(CAP)]
    for index, (source, slot) in enumerate(early):
        lane = slot * LAYERS + source
        early_ref[index] = patch(source, slot, offsets[:, lane : lane + 1])
    copy.wait()
    for index, (source, slot) in enumerate(early):
        grid_ref[block_ref[0, slot * LAYERS + source]] += early_ref[index]

    together = (LAYERS - EARLY) // 2

    def some(step, held):
        for part in range(together):
            for slot in range(CAP):
                source = EARLY + step * together + part
                lane = slot * LAYERS + part
                grid_ref[block_ref[0, slot * LAYERS + source]] += patch(
                    source, slot, held[:, lane : lane + 1]
                )
        return pltpu.roll(held, SLOTS - together, 1)

    lax.fori_loop(0, 2, some, pltpu.roll(offsets, SLOTS - EARLY, 1))

    wide, narrow = 8, SUB // 8
    for second in range(2):
        for low in range(wide):
            at = [second * SUB + low + wide * high for high in range(narrow)]
            turned = dft([(grid_ref[k, :RB, :], grid_ref[k, RB:, :]) for k in at])
            for index, k in enumerate(at):
                real, imag = turn_by(turned[index], index * low, SUB)
                grid_ref[k, :RB, :] = real
                grid_ref[k, RB:, :] = imag
        for low in range(narrow):
            at = [second * SUB + wide * low + high for high in range(wide)]
            turned = dft([(grid_ref[k, :RB, :], grid_ref[k, RB:, :]) for k in at])
            for index, (real, imag) in enumerate(turned):
                q = low + narrow * index
                cos_part = twist_ref[q : q + 1, :]
                sin_part = twist_ref[SUB + q : SUB + q + 1, :]
                upper, lower = split(
                    jnp.concatenate(
                        [real * cos_part - imag * sin_part, real * sin_part + imag * cos_part], 1
                    )
                )
                place = (second * SUB + q) * RB
                upper_ref[place : place + RB, :] = upper
                lower_ref[place : place + RB, :] = lower

    last_both = last_ref[...]
    last_upper = last_both[: 2 * SUB]
    for pair in range(PAIRS // 2):
        piece = slice(pair * 2 * LANES, (pair + 1) * 2 * LANES)
        both = dot(last_both, upper_ref[piece, :], NT)
        wave_sum = both[: 2 * SUB] + both[2 * SUB :] + dot(last_upper, lower_ref[piece, :], NT)
        for half in range(2):
            for part in range(2):
                row = 2 * (2 * pair + half) + part
                out_ref[pl.ds(row, PEERS, stride=2 * PAIRS), :] = wave_sum[
                    part * PEERS : (part + 1) * PEERS, half * LANES : (half + 1) * LANES
                ]


def swap_blocks(value):
    line = lax.broadcasted_iota(jnp.int32, value.shape, 0)
    block = lax.broadcasted_iota(jnp.int32, value.shape, 1) // RB
    for step in (4, 2, 1):
        line_bit = jnp.bitwise_and(line, step) != 0
        block_bit = jnp.bitwise_and(block, step) != 0
        up = pltpu.roll(pltpu.roll(value, 8 - step, 0), RB * step, 1)
        down = pltpu.roll(pltpu.roll(value, step, 0), LANES - RB * step, 1)
        moved = jnp.where(line_bit, down, up)
        value = jnp.where(line_bit == block_bit, value, moved)
    return value


def image_kernel(got_ref, upper_ref, lower_ref, cos_ref, sin_ref, out_ref, right_ref):
    blocks = SUB // N_SLAB
    for layer in range(X_CHIPS):
        for pair in range(blocks // 2):
            lines = []
            for high in (2 * pair, 2 * pair + 1):
                parts = []
                for y in range(2):
                    for h in range(2):
                        step = 2 * (h * blocks + high) + y
                        row = layer * N_SLAB * 2 * PAIRS + step
                        parts.append(
                            swap_blocks(got_ref[pl.ds(row, N_SLAB, stride=2 * PAIRS), :])
                        )
                lines.append(jnp.concatenate(parts, 1))
            upper, lower = split(jnp.concatenate(lines, 0))
            row = layer * SUB + pair * 2 * N_SLAB
            right_ref[row : row + 2 * N_SLAB, :] = upper
            right_ref[LANES + row : LANES + row + 2 * N_SLAB, :] = lower
    count = IMG_L // X_CHIPS
    group = lax.broadcasted_iota(jnp.int32, (count, LANES), 1) // SUB
    right = right_ref[...]
    total = None
    for part in range(X_CHIPS):
        rows = pl.ds(part * 2 * count, 2 * count)
        both = dot(upper_ref[rows, :], right, NT)
        wave_sum = both[:, :LANES] + both[:, LANES:] + dot(lower_ref[rows, :], right[:LANES], NT)
        lines = pl.ds(part * count, count)
        screened = wave_sum[:count] * cos_ref[lines, :] - wave_sum[count:] * sin_ref[lines, :]
        screened = screened + pltpu.roll(screened, 2 * SUB, 1)
        screened = screened + pltpu.roll(screened, SUB, 1)
        total = screened if total is None else jnp.where(group == part, screened, total)
    out_ref[...] = total


def sum_kernel(got_ref, out_ref):
    line = lax.broadcasted_iota(jnp.int32, (8, LANES), 0)
    group = lax.broadcasted_iota(jnp.int32, (8, LANES), 1) // SUB
    straight = (line // 4) == jnp.bitwise_and(line, 1)
    result = jnp.zeros((8, LANES), f32)
    for place in range(X_CHIPS):
        chip = (place + FIRST_X) % X_CHIPS
        total = got_ref[pl.ds(place * 2 * Z_CHIPS, 8), :]
        for step in range(1, 2 * Z_CHIPS // 8):
            total = total + got_ref[pl.ds(place * 2 * Z_CHIPS + 8 * step, 8), :]
        total = total + pltpu.roll(total, 4, 0)
        total = total + pltpu.roll(total, 2, 0)
        total = jnp.where(straight, total, pltpu.roll(total, 1, 0))
        for part in range(X_CHIPS):
            shift = (chip - part) % X_CHIPS
            moved = pltpu.roll(total, SUB * shift, 1) if shift else total
            chosen = (group == chip) & (jnp.bitwise_and(line, 3) == part)
            result = jnp.where(chosen, moved, result)
    out_ref[...] = result


def call(kernel, shape, specs, scratch, flops, moved, limit=24):
    return pl.pallas_call(
        kernel,
        out_shape=jax.ShapeDtypeStruct(shape, f32),
        in_specs=specs,
        out_specs=VMEM,
        scratch_shapes=scratch,
        compiler_params=pltpu.CompilerParams(vmem_limit_bytes=limit * 1024 * 1024),
        cost_estimate=pl.CostEstimate(flops=flops, bytes_accessed=moved, transcendentals=0),
    )


def grid_tables():
    q = np.arange(SUB)
    c = np.arange(CB)
    sign = (1 - 2 * (q % 2))[:, None]
    twist = np.concatenate([part * sign for part in wave(q[:, None] * c[None, :], NG)], 0)
    x, slab = np.divmod(column_members(), N_SLAB)
    n = 4 * slab + x
    cos_part, sin_part = wave((n[:, None] - SUB // 2) * c[None, :], CB)
    last = np.concatenate(
        [
            np.concatenate([cos_part, -sin_part], 1),
            np.concatenate([sin_part, cos_part], 1),
        ],
        0,
    )
    return twist.astype(np.float32), np.concatenate(np_split(last), 0)


def rotated(slow, fast, first_slow, first_fast):
    i, j = np.meshgrid(np.arange(slow), np.arange(fast), indexing="ij")
    return ((i + first_slow) % slow * fast + (j + first_fast) % fast).reshape(-1)


def layer_members():
    z, x = np.meshgrid(np.arange(Z_CHIPS), np.arange(X_CHIPS), indexing="ij")
    return ((x + FIRST_X) % X_CHIPS * Z_CHIPS + (z + TILE_Z) % Z_CHIPS).reshape(-1)


def column_members():
    return rotated(X_CHIPS, N_SLAB, FIRST_X, FIRST_SLAB)


def image_members():
    return rotated(X_CHIPS, Z_CHIPS, FIRST_X, IMAGE_Z)


def exchange(value, axes, members):
    groups = [[int(member) for member in members]]
    return lax.all_to_all(
        value, axes, split_axis=0, concat_axis=0, tiled=True, axis_index_groups=groups
    )


def image_lines():
    part, chip, half = np.meshgrid(
        np.arange(4), image_members(), np.arange(2), indexing="ij"
    )
    return (8 * chip + 4 * half + part).reshape(-1) - IMG_L // 2


def image_tables(spread):
    y, h, slab, r = np.meshgrid(
        np.arange(2), np.arange(2), np.arange(N_SLAB), np.arange(RB), indexing="ij"
    )
    slab = (slab + FIRST_SLAB) % N_SLAB
    row = (slab * ROWS_DEV + h * RB + r).reshape(-1) - ROWS_DEV * N_SLAB // 2
    y = y.reshape(-1)[None, :]
    cos_part, sin_part = wave(image_lines()[:, None] * row[None, :], NG)
    real = np.where(y == 0, cos_part, -sin_part).reshape(4, -1, row.size)
    imag = np.where(y == 0, sin_part, cos_part).reshape(4, -1, row.size)
    return np_split(np.concatenate([real, imag], 1).reshape(2 * IMG_L, row.size) * spread)


def screen_tables():
    columns = IMG_M // N_SLAB
    lines = jnp.asarray(image_lines().astype(np.float32))
    lane = jnp.arange(LANES, dtype=jnp.int32)
    m_index = (
        lax.axis_index("slab") * columns
        + lax.axis_index("x") * SUB
        + jnp.bitwise_and(lane, SUB - 1)
        - IMG_M // 2
    )
    place = (lax.axis_index("z") + Z_CHIPS - TILE_Z) % Z_CHIPS
    layer = (place * X_CHIPS + lane // SUB).astype(f32)
    w_value = w_reach * (2.0 * layer + 1.0 - LAYERS) / LAYERS
    l_direction = lines[:, None] * cell_size
    m_direction = m_index.astype(f32)[None, :] * cell_size
    radius = l_direction * l_direction + m_direction * m_direction
    n_lift = -radius / (1.0 + jnp.sqrt(1.0 - radius))
    phase_angle = -2.0 * math.pi * w_value[None, :] * n_lift
    return jnp.cos(phase_angle), jnp.sin(phase_angle)


def body(visibilities, row_offset, col_offset, w_layer, grid_block):
    tiles = w_layer.shape[0]
    spread = 1.0 / (
        2.0 * math.pi * kernel_width**2 * math.sqrt(tiles * LAYERS * N_SLAB * VIS)
    )
    sent = call(
        route_kernel,
        (LAYERS * SENT, VIS),
        [HBM] * 5,
        [
            pltpu.SMEM((tiles,), jnp.int32),
            pltpu.SMEM((tiles,), jnp.int32),
            pltpu.VMEM((2 * tiles, VIS), f32),
            pltpu.VMEM((tiles, VIS), f32),
            pltpu.VMEM((tiles, VIS), f32),
            pltpu.SMEM((LAYERS,), jnp.int32),
            pltpu.SemaphoreType.DMA((5,)),
        ],
        10**6,
        5 * 10**5,
        limit=60,
    )(w_layer, grid_block, visibilities.reshape(2 * tiles, VIS), row_offset, col_offset)
    got = exchange(sent.reshape(LAYERS, 1, SENT * VIS), ("x", "z"), layer_members())
    got = got.reshape(LAYERS * SENT, VIS)
    cos_screen, sin_screen = screen_tables()
    twist, last = grid_tables()
    pieces = call(
        grid_kernel,
        (PEERS * 2 * PAIRS, LANES),
        [VMEM] * 3,
        [
            pltpu.VMEM((2 * SUB, 2 * RB, CB), f32),
            pltpu.VMEM((2 * SUB * RB, 2 * CB), bf16),
            pltpu.VMEM((2 * SUB * RB, 2 * CB), bf16),
            pltpu.VMEM((EARLY * CAP, 2 * RB, CB), f32),
            pltpu.VMEM((1, SLOTS), jnp.int32),
            pltpu.SMEM((1, SLOTS), jnp.int32),
            pltpu.SemaphoreType.DMA,
        ],
        10**9,
        10**6,
    )(got, jnp.asarray(twist), jnp.asarray(last))
    turned = exchange(
        pieces.reshape(PEERS, 2 * PAIRS, LANES), ("x", "slab"), column_members()
    ).reshape(PEERS * 2 * PAIRS, LANES)
    upper, lower = image_tables(spread)
    shares = call(
        image_kernel,
        (2 * LAYERS, LANES),
        [VMEM] * 5,
        [pltpu.VMEM((2 * LANES, 2 * ROWS_DEV * N_SLAB), bf16)],
        10**9,
        3 * 10**6,
    )(turned, jnp.asarray(upper), jnp.asarray(lower), cos_screen, sin_screen)
    got = exchange(shares.reshape(LAYERS, 2, LANES), ("x", "z"), image_members())
    got = got.reshape(2 * LAYERS, LANES)
    return call(sum_kernel, (8, LANES), [VMEM], [], 10**5, 7 * 10**4)(got)


def solution(mesh):
    whole = ("x", "z", "slab")
    chips = Mesh(mesh.devices.reshape(X_CHIPS, Z_CHIPS, N_SLAB), whole)
    placed = (P(whole, None, None), P(whole, None), P(whole, None), P(whole), P(whole))
    return jax.shard_map(
        body, mesh=chips, in_specs=placed, out_specs=P(("x", "z"), "slab"), check_vma=False
    )
```
